256 devices in a mesh: row: 32 (over x, z_hi, core), col: 8 (over z_lo, y).
Axes of the slice: x: 4, y: 4, z: 8 (z_hi: 4, z_lo: 2; z = z_hi * 2 + z_lo), core: 2. Of those that a mesh axis runs over, the one named last changes fastest.
Arguments:
- pair_acts: bfloat16 [384, 384, 128], P('row', 'col'), may hold values from -6 to 6
- token_valid: int32 [384], replicated, may hold values from 0 to 1, as said below
- norm_gain: float32 [128], replicated, may hold values from 0.5 to 1.5
- proj_weight: bfloat16 [128, 640], replicated, may hold values from -0.5 to 0.5
- out_gain: float32 [128], replicated, may hold values from 0.5 to 1.5
- out_weight: bfloat16 [128, 128], replicated, may hold values from -0.5 to 0.5
- out_cotangent: bfloat16 [384, 384, 128], P('row', 'col'), may hold values from -6 to 6
Outputs:
- update: bfloat16 [384, 384, 128], P('row', 'col')
- grad_pair: bfloat16 [384, 384, 128], P('row', 'col')
- grad_weight: float32 [128, 640], replicated
The draws below stay inside these ranges and needn't reach their ends.
Inputs may be any that keep to these rules, and one draw needn't show every extreme that they name: `token_valid`: in every aligned block of 12 tokens the valid tokens come before the padding, and at least half of the block is valid.
All inputs are finite; a program needn't handle non-finite values.
Results may differ from the reference program's by a relative error of at most 0.018.
Values may be sent and summed in bfloat16 or wider, within the bound.
No kernel may reach another device: no remote copies, remote signals or barrier semaphores. Data moves between devices by JAX's collectives and lax.ppermute only.
A program may use at most 128 MiB of HBM per device.

```python
import jax
import jax.numpy as jnp
from jax import lax

C = 128
H = 128
TOK_ROW = 12
N = 384


def draw_token_valid(key, part):
    key = jax.random.fold_in(key, 11)
    num_blocks = N // TOK_ROW
    first_key, second_key = jax.random.split(key)
    dropped = jax.random.randint(first_key, (num_blocks,), 0, TOK_ROW // 2 + 1)
    chosen = jax.random.permutation(second_key, num_blocks)
    dropped = dropped.at[chosen[0]].set(TOK_ROW // 2).at[chosen[1]].set(0)
    counts = TOK_ROW - dropped
    places = jnp.arange(N, dtype=jnp.int32)
    block_of = places // TOK_ROW
    inside = places % TOK_ROW
    return (inside < counts[block_of]).astype(jnp.int32)


def raised(entries, own_key, source, target, blocks, factor):
    owner, partner = [(jnp.arange(entries.shape[axis_at]) // (entries.shape[axis_at] // blocks)).reshape([-1 if axis == axis_at else 1 for axis in range(entries.ndim)]) for axis_at in (source, target)]
    chosen = jax.random.permutation(own_key, blocks)[partner]
    strong = (owner == chosen) | (owner == (partner + blocks // 2) % blocks)
    return jnp.where(strong, factor * entries, entries)


def block_levels(stream_key, dims, cuts, least, largest):
    factor_of = 1.0
    for dim, parts in cuts:
        draws = jax.random.uniform(jax.random.fold_in(jax.random.fold_in(stream_key, 6), dim), (parts,), jnp.float32, least / len(cuts), largest / len(cuts))
        factor_of = factor_of * jnp.repeat(jnp.exp(draws), dims[dim] // parts).reshape((-1,) + (1,) * (len(dims) - 1 - dim))
    return factor_of


def scatter_about(stream_key, extent, spread, limit, cuts=(), kind=jnp.bfloat16):
    result = spread * jax.random.normal(stream_key, extent, jnp.float32)
    if cuts:
        result = result * block_levels(stream_key, extent, cuts, -0.22, 0.18)
    return jnp.clip(result, -limit, limit).astype(kind)


def gaussian_with(key, extent, deviation, bound, shards, heavy, kind=jnp.bfloat16):
    array = deviation * jax.random.normal(key, extent, jnp.float32)
    if shards:
        array = array * block_levels(key, extent, shards, -0.22, 0.18)
    return jnp.clip(raised(array, jax.random.fold_in(key, 3), *heavy), -bound, bound).astype(kind)


def setup_inputs(seed: int = 0) -> dict:
    seeds = jax.random.split(jax.random.key(seed), 8)
    return {
        "pair_acts": scatter_about(seeds[0], (N, N, C), 1.0, 6.0, ((0, 32), (1, 8))),
        "token_valid": draw_token_valid(jax.random.fold_in(seeds[7], 71), 0),
        "norm_gain": jnp.clip(1.0 + 0.1 * jax.random.normal(seeds[2], (C,), jnp.float32), 0.5, 1.5),
        "proj_weight": scatter_about(seeds[3], (C, 4 * H + C), C ** -0.5, 0.5),
        "out_gain": jnp.clip(1.0 + 0.1 * jax.random.normal(seeds[4], (H,), jnp.float32), 0.5, 1.5),
        "out_weight": scatter_about(seeds[5], (H, C), H ** -0.5, 0.5),
        "out_cotangent": gaussian_with(seeds[6], (N, N, C), 1.0, 6.0, ((0, 32), (1, 8)), (0, 1, 32, 2.75)),
    }


EPSILON = 1e-05

def normalize(values):
    center = lax.optimization_barrier(jnp.mean(values, axis=-1, keepdims=True))
    shifted = values - center
    inv_std = lax.rsqrt(lax.optimization_barrier(jnp.mean(shifted * shifted, axis=-1, keepdims=True)) + EPSILON)
    return (shifted * inv_std, inv_std)

def norm_grad(upstream, scaled, inv_std):
    first = lax.optimization_barrier(jnp.mean(upstream, axis=-1, keepdims=True))
    second = lax.optimization_barrier(jnp.mean(upstream * scaled, axis=-1, keepdims=True))
    return inv_std * (upstream - first - scaled * second)

def reference(pair_acts, token_valid, norm_gain, proj_weight, out_gain, out_weight, out_cotangent):
    full_len = pair_acts.shape[0]
    channels = pair_acts.shape[2]
    hidden_dim = out_weight.shape[0]
    width_all = proj_weight.shape[1]
    scaled_in, inv_in = normalize(pair_acts.astype(jnp.float32))
    normed = (scaled_in * norm_gain).astype(jnp.bfloat16)
    normed_flat = normed.reshape(-1, channels)
    projected = jnp.dot(normed_flat, proj_weight, preferred_element_type=jnp.float32).reshape(full_len, full_len, width_all)
    validity = token_valid.astype(jnp.float32)
    pair_mask = (validity[:, None] * validity[None, :])[:, :, None]
    left_sig = jax.nn.sigmoid(projected[:, :, 0:hidden_dim])
    left_val = projected[:, :, hidden_dim:2 * hidden_dim]
    right_sig = jax.nn.sigmoid(projected[:, :, 2 * hidden_dim:3 * hidden_dim])
    right_val = projected[:, :, 3 * hidden_dim:4 * hidden_dim]
    gate_sig = jax.nn.sigmoid(projected[:, :, 4 * hidden_dim:])
    left_side = (left_sig * left_val * pair_mask).astype(jnp.bfloat16)
    right_side = (right_sig * right_val * pair_mask).astype(jnp.bfloat16)
    left_wide = left_side.astype(jnp.float32)
    right_wide = right_side.astype(jnp.float32)
    tri_sum = jnp.einsum('ikh,jkh->ijh', left_wide, right_wide)
    scaled_out, inv_out = normalize(tri_sum)
    normed_out = (scaled_out * out_gain).astype(jnp.bfloat16)
    out_proj = jnp.dot(normed_out.reshape(-1, hidden_dim), out_weight, preferred_element_type=jnp.float32).reshape(full_len, full_len, channels)
    gate_mask = gate_sig * pair_mask
    update = (gate_mask * out_proj).astype(jnp.bfloat16)
    cotangent = out_cotangent.astype(jnp.float32)
    back_out = (cotangent * gate_mask).astype(jnp.bfloat16)
    back_norm = jnp.dot(back_out.reshape(-1, channels), out_weight.T, preferred_element_type=jnp.float32).reshape(full_len, full_len, hidden_dim) * out_gain
    back_tri = norm_grad(back_norm, scaled_out, inv_out).astype(jnp.bfloat16)
    back_wide = back_tri.astype(jnp.float32)
    back_left = jnp.einsum('ijh,jkh->ikh', back_wide, right_wide) * pair_mask
    back_right = jnp.einsum('ijh,ikh->jkh', back_wide, left_wide) * pair_mask
    back_gate = cotangent * pair_mask * out_proj * gate_sig * (1.0 - gate_sig)
    back_proj = jnp.concatenate([back_left * left_val * left_sig * (1.0 - left_sig), back_left * left_sig, back_right * right_val * right_sig * (1.0 - right_sig), back_right * right_sig, back_gate], axis=-1).astype(jnp.bfloat16)
    back_flat = back_proj.reshape(-1, width_all)
    back_normed = jnp.dot(back_flat, proj_weight.T, preferred_element_type=jnp.float32).reshape(full_len, full_len, channels) * norm_gain
    grad_pair = norm_grad(back_normed, scaled_in, inv_in).astype(jnp.bfloat16)
    grad_weight = lax.dot_general(normed_flat, back_flat, (((0,), (0,)), ((), ())), preferred_element_type=jnp.float32) / full_len
    return (update, grad_pair, grad_weight)
```

```python
import jax
import jax.numpy as jnp
from jax import lax
from jax.sharding import PartitionSpec as P

EPSILON = 1e-05
BF16 = jnp.bfloat16
F32 = jnp.float32
AXES = ("row", "col")


def normalize(values):
    center = jnp.mean(values, axis=-1, keepdims=True)
    shifted = values - center
    inv_std = lax.rsqrt(jnp.mean(shifted * shifted, axis=-1, keepdims=True) + EPSILON)
    return (shifted * inv_std, inv_std)


def norm_grad(upstream, scaled, inv_std):
    first = jnp.mean(upstream, axis=-1, keepdims=True)
    second = jnp.mean(upstream * scaled, axis=-1, keepdims=True)
    return inv_std * (upstream - first - scaled * second)


def exchange(chunks):
    return lax.all_to_all(chunks, AXES, 0, 0, tiled=True)


def other_core(values, num_rows):
    return lax.ppermute(values, "row", [(i, i ^ 1) for i in range(num_rows)])


def gather_plane(chunks, rows, cols, part, wide):
    return (
        chunks.reshape(rows, cols, part, wide).transpose(2, 0, 1, 3).reshape(part * rows, cols * wide)
    )


def scatter_plane(plane, rows, cols, part, wide):
    return (
        plane.reshape(part, rows, cols, wide).transpose(1, 2, 0, 3).reshape(rows * cols, part * wide)
    )


def make_per_device(num_r, num_c):
    def per_device(pair_acts, token_valid, norm_gain, proj_weight, out_gain, out_weight, out_cotangent):
        na, nb, channels = pair_acts.shape
        hidden = out_weight.shape[0]
        width_all = proj_weight.shape[1]
        full_len = token_valid.shape[0]
        pairs = na * nb
        half_a = na // 2
        chips = num_r // 2
        core = lax.axis_index("row") % 2
        validity = token_valid.astype(F32)
        valid_rows = lax.dynamic_slice_in_dim(validity, lax.axis_index("row") * na, na)
        valid_cols = lax.dynamic_slice_in_dim(validity, lax.axis_index("col") * nb, nb)
        pair_mask = (valid_rows[:, None] * valid_cols[None, :]).reshape(pairs, 1)

        scaled_in, inv_in = normalize(pair_acts.reshape(pairs, channels).astype(F32))
        normed = (scaled_in * norm_gain).astype(BF16)
        projected = jnp.dot(normed, proj_weight, preferred_element_type=F32)
        left_sig = jax.nn.sigmoid(projected[:, 0:hidden])
        left_val = projected[:, hidden : 2 * hidden]
        right_sig = jax.nn.sigmoid(projected[:, 2 * hidden : 3 * hidden])
        right_val = projected[:, 3 * hidden : 4 * hidden]
        gate_sig = jax.nn.sigmoid(projected[:, 4 * hidden :])
        left_side = (left_sig * left_val * pair_mask).astype(BF16)
        right_side = (right_sig * right_val * pair_mask).astype(BF16)

        sides = jnp.stack(
            [left_side.T.reshape(chips, num_c, pairs), right_side.T.reshape(chips, num_c, pairs)], axis=1
        )
        mine = gather_plane(exchange(sides.reshape(num_r * num_c, pairs)), num_r, num_c, na, nb)
        theirs = other_core(mine, num_r)
        left = jnp.where(core == 0, mine, theirs)
        right = jnp.where(core == 0, theirs, mine)
        right_nat = right.reshape(na, num_r, full_len).transpose(1, 0, 2).reshape(full_len, full_len)
        left_half = lax.dynamic_slice_in_dim(left, core * (full_len // 2), full_len // 2)
        tri = lax.dot_general(
            left_half, right_nat, (((1,), (1,)), ((), ())), preferred_element_type=F32
        ).astype(BF16)
        tri = exchange(scatter_plane(tri, num_r, num_c, half_a, nb))
        tri_sum = (
            tri.reshape(chips, 2, num_c, pairs // 2)
            .transpose(1, 3, 0, 2)
            .reshape(pairs, hidden)
            .astype(F32)
        )

        scaled_out, inv_out = normalize(tri_sum)
        normed_out = (scaled_out * out_gain).astype(BF16)
        out_proj = jnp.dot(normed_out, out_weight, preferred_element_type=F32)
        gate_mask = gate_sig * pair_mask
        update = (gate_mask * out_proj).astype(BF16)
        cotangent = out_cotangent.reshape(pairs, channels).astype(F32)
        back_out = (cotangent * gate_mask).astype(BF16)
        back_norm = jnp.dot(back_out, out_weight.T, preferred_element_type=F32) * out_gain
        back_tri = norm_grad(back_norm, scaled_out, inv_out).astype(BF16)

        back = back_tri.reshape(2, pairs // 2, chips, num_c).transpose(2, 0, 3, 1)
        back = exchange(back.reshape(num_r * num_c, pairs // 2))
        back_half = gather_plane(back, num_r, num_c, half_a, nb)
        back_other = other_core(back_half, num_r)
        back_plane = jnp.concatenate(
            [
                jnp.where(core == 0, back_half, back_other),
                jnp.where(core == 0, back_other, back_half),
            ]
        )
        back_perm = (
            back_plane.reshape(full_len, num_r, na).transpose(0, 2, 1).reshape(full_len, full_len)
        )
        back_side = jnp.dot(
            jnp.where(core == 0, back_perm, back_perm.T),
            jnp.where(core == 0, right, left),
            preferred_element_type=F32,
        ).astype(BF16)
        back_sides = exchange(scatter_plane(back_side, num_r, num_c, na, nb))
        back_sides = back_sides.reshape(chips, 2, num_c, pairs)
        back_left = back_sides[:, 0].reshape(hidden, pairs).T.astype(F32) * pair_mask
        back_right = back_sides[:, 1].reshape(hidden, pairs).T.astype(F32) * pair_mask

        back_gate = cotangent * pair_mask * out_proj * gate_sig * (1.0 - gate_sig)
        back_proj = jnp.concatenate(
            [
                back_left * left_val * left_sig * (1.0 - left_sig),
                back_left * left_sig,
                back_right * right_val * right_sig * (1.0 - right_sig),
                back_right * right_sig,
                back_gate,
            ],
            axis=-1,
        ).astype(BF16)
        weight_term = lax.dot_general(
            normed, back_proj, (((0,), (0,)), ((), ())), preferred_element_type=F32
        ).astype(BF16)
        parts = exchange(weight_term.reshape(num_r * num_c, -1))
        total = jnp.sum(parts.astype(F32), axis=0) / full_len
        spread = jnp.broadcast_to(total.astype(BF16), (num_r * num_c,) + total.shape)
        grad_weight = exchange(spread).reshape(channels, width_all).astype(F32)

        back_normed = jnp.dot(back_proj, proj_weight.T, preferred_element_type=F32) * norm_gain
        grad_pair = norm_grad(back_normed, scaled_in, inv_in).astype(BF16)
        return (
            update.reshape(na, nb, channels),
            grad_pair.reshape(na, nb, channels),
            grad_weight,
        )

    return per_device


def solution(mesh):
    placed = (P("row", "col", None), P(), P(), P(), P(), P(), P("row", "col", None))
    return jax.shard_map(
        make_per_device(mesh.shape["row"], mesh.shape["col"]),
        mesh=mesh,
        in_specs=placed,
        out_specs=(P("row", "col", None), P("row", "col", None), P()),
        check_vma=False,
    )
```

```python
import functools

import jax
import jax.numpy as jnp
from jax import lax
from jax.experimental import pallas as pl
from jax.experimental.pallas import tpu as pltpu
from jax.sharding import PartitionSpec as P

EPSILON = 1e-05
BF16 = jnp.bfloat16
F32 = jnp.float32
AXES = ("row", "col")
LANES = 128
SLOT = 64
VMEM_LIMIT = 48 * 1024 * 1024

NT = (((1,), (1,)), ((), ()))
NN = (((1,), (0,)), ((), ()))
TN = (((0,), (0,)), ((), ()))


def matmul(lhs, rhs, dims=NN):
    return lax.dot_general(lhs, rhs, dims, preferred_element_type=F32)


def column(row_ref):
    return jnp.broadcast_to(row_ref[...], (LANES, LANES)).T


def swap_halves(values):
    return pltpu.roll(values, SLOT, 1)


def low_half(shape):
    return lax.broadcasted_iota(jnp.int32, shape, 1) < SLOT


def spread(pairs_ref, spread_ref):
    na, nb, channels = pairs_ref.shape
    for a in range(na):
        spread_ref[a * SLOT : a * SLOT + nb, :] = pairs_ref[a].astype(F32)
        spread_ref[a * SLOT + nb : (a + 1) * SLOT, :] = jnp.zeros((SLOT - nb, channels), F32)


def store_pairs(out_ref, t, values):
    nb = out_ref.shape[1]
    turned = values.T
    out_ref[2 * t] = turned[0:nb].astype(out_ref.dtype)
    out_ref[2 * t + 1] = turned[SLOT : SLOT + nb].astype(out_ref.dtype)


def masks(valid_ref, na, nb):
    lane = lax.broadcasted_iota(jnp.int32, (1, LANES), 1)
    place = lane % SLOT
    first_row = lax.axis_index("row") * na
    first_col = lax.axis_index("col") * nb
    cols = jnp.zeros((1, LANES), jnp.int32)
    for b in range(nb):
        cols = jnp.where(place == b, valid_ref[first_col + b], cols)
    found = []
    for t in range(na // 2):
        rows = jnp.where(lane < SLOT, valid_ref[first_row + 2 * t], valid_ref[first_row + 2 * t + 1])
        found.append((rows * cols).astype(F32))
    return found


def tile_norm(values):
    center = jnp.mean(values, axis=0, keepdims=True)
    shifted = values - center
    inv_std = lax.rsqrt(jnp.mean(shifted * shifted, axis=0, keepdims=True) + EPSILON)
    return shifted * inv_std, inv_std


def tile_norm_grad(upstream, scaled, inv_std):
    first = jnp.mean(upstream, axis=0, keepdims=True)
    second = jnp.mean(upstream * scaled, axis=0, keepdims=True)
    return inv_std * (upstream - first - scaled * second)


def norm_tiles(spread_ref, gain_ref, normed_ref):
    gain = column(gain_ref)
    tiles = spread_ref.shape[0] // LANES
    for t in range(tiles):
        at = slice(t * LANES, (t + 1) * LANES)
        scaled, _ = tile_norm(spread_ref[at, :].T)
        normed_ref[:, at] = (scaled * gain).astype(BF16)


def put_channels(chunk_ref, t, depth, side, values):
    for m in range(values.shape[0] // 8):
        start = depth * (16 * m + 8 * side) + t
        chunk_ref[pl.ds(start, 8, stride=depth), :] = values[8 * m : 8 * m + 8, :]


def get_channels(chunk_ref, t, depth, side, hidden):
    return jnp.concatenate(
        [
            chunk_ref[pl.ds(depth * (16 * m + 8 * side) + t, 8, stride=depth), :]
            for m in range(hidden // 8)
        ],
        axis=0,
    )


def chunks_to_plane(chunk_ref, plane_ref, depth, tiles, first_a, na):
    low = low_half((8, LANES))
    for pair in range(4):
        for t in range(tiles):
            for lo in range(4):
                start = depth * (8 * lo + 2 * pair) + t
                even = chunk_ref[pl.ds(start, 8, stride=32 * depth), :]
                odd = chunk_ref[pl.ds(start + depth, 8, stride=32 * depth), :]
                row = na * lo + first_a + 2 * t
                plane_ref[pair, pl.ds(row, 8, stride=SLOT), :] = jnp.where(low, even, swap_halves(odd))
                plane_ref[pair, pl.ds(row + 1, 8, stride=SLOT), :] = jnp.where(
                    low, swap_halves(even), odd
                )


def plane_to_chunks(plane_ref, chunk_ref, depth, tiles, first_a, na):
    low = low_half((8, LANES))
    for pair in range(4):
        for t in range(tiles):
            for lo in range(4):
                row = na * lo + first_a + 2 * t
                upper = plane_ref[pair, pl.ds(row, 8, stride=SLOT), :]
                lower = plane_ref[pair, pl.ds(row + 1, 8, stride=SLOT), :]
                start = depth * (8 * lo + 2 * pair) + t
                chunk_ref[pl.ds(start, 8, stride=32 * depth), :] = jnp.where(
                    low, upper, swap_halves(lower)
                )
                chunk_ref[pl.ds(start + depth, 8, stride=32 * depth), :] = jnp.where(
                    low, swap_halves(upper), lower
                )


def clear_gaps(plane_ref, used):
    rows = plane_ref.shape[1]
    for pair in range(plane_ref.shape[0]):
        for group in range(rows // SLOT):
            plane_ref[pair, group * SLOT + used : (group + 1) * SLOT, :] = jnp.zeros(
                (SLOT - used, LANES), F32
            )


def whole_plane(plane_ref):
    return jnp.concatenate([plane_ref[pair].astype(BF16) for pair in range(4)], axis=1)


def my_core():
    return lax.axis_index("row") % 2


def sides_kernel(valid_ref, acts_ref, gain_ref, weight_ref, out_ref, spread_ref, normed_ref, chunk_ref):
    na, nb, _ = acts_ref.shape
    tiles = na // 2
    hidden = weight_ref.shape[0]
    spread(acts_ref, spread_ref)
    norm_tiles(spread_ref, gain_ref, normed_ref)
    mask = masks(valid_ref, na, nb)
    projected = matmul(weight_ref[:, 0 : 4 * hidden], normed_ref[...], TN)
    for t in range(tiles):
        at = slice(t * LANES, (t + 1) * LANES)
        for side in range(2):
            base = 2 * side * hidden
            gate = jax.nn.sigmoid(projected[base : base + hidden, at])
            value = projected[base + hidden : base + 2 * hidden, at]
            put_channels(chunk_ref, t, tiles, side, gate * value * mask[t])
    out_ref[...] = chunk_ref[...].astype(BF16)


def tri_kernel(na, nb, mine_ref, theirs_ref, tri_ref, keep_ref, chunk_ref, plane_ref, tri_chunk_ref):
    tiles = na // 2
    half = tiles // 2
    core = my_core()
    chunk_ref[0] = mine_ref[...].astype(F32)
    chunk_ref[1] = theirs_ref[...].astype(F32)
    for side in range(2):
        clear_gaps(plane_ref.at[side], nb)
        chunks_to_plane(chunk_ref.at[side], plane_ref.at[side], tiles, tiles, 0, na)
    keep_ref[...] = whole_plane(plane_ref.at[1])
    left = whole_plane(plane_ref.at[core])
    right = whole_plane(plane_ref.at[1 - core])
    tri = matmul(left, right, NT)
    for pair in range(4):
        plane_ref[0, pair] = tri[:, pair * LANES : (pair + 1) * LANES]
    plane_to_chunks(plane_ref.at[0], tri_chunk_ref, 4, half, core * 2 * half, na)
    tri_ref[...] = tri_chunk_ref[...].astype(BF16)


def middle_kernel(
    valid_ref,
    tri_ref,
    acts_ref,
    cotangent_ref,
    gain_ref,
    weight_ref,
    out_gain_ref,
    out_weight_ref,
    update_ref,
    back_ref,
    gate_ref,
    spread_ref,
    normed_ref,
    tri_chunk_ref,
    tri_plane_ref,
    normed_out_ref,
    back_out_ref,
):
    na, nb, _ = acts_ref.shape
    tiles = na // 2
    half = tiles // 2
    hidden = out_weight_ref.shape[0]
    spread(acts_ref, spread_ref)
    norm_tiles(spread_ref, gain_ref, normed_ref)
    mask = masks(valid_ref, na, nb)
    gate_sig = jax.nn.sigmoid(matmul(weight_ref[:, 4 * hidden :], normed_ref[...], TN))
    spread(cotangent_ref, spread_ref)
    tri_chunk_ref[...] = tri_ref[...].astype(F32)
    out_gain = column(out_gain_ref)
    inv_out = []
    for t in range(tiles):
        at = slice(t * LANES, (t + 1) * LANES)
        scaled, inv = tile_norm(get_channels(tri_chunk_ref, t % half, 4, t // half, hidden))
        inv_out.append(inv)
        tri_plane_ref[:, at] = scaled
        normed_out_ref[:, at] = (scaled * out_gain).astype(BF16)
        gate_mask = gate_sig[:, at] * mask[t]
        back_out_ref[:, at] = (spread_ref[at, :].T * gate_mask).astype(BF16)
    out_proj = matmul(out_weight_ref[...], normed_out_ref[...], TN)
    back_norm = matmul(out_weight_ref[...], back_out_ref[...])
    for t in range(tiles):
        at = slice(t * LANES, (t + 1) * LANES)
        back_tri = tile_norm_grad(back_norm[:, at] * out_gain, tri_plane_ref[:, at], inv_out[t])
        put_channels(tri_chunk_ref, t % half, 4, t // half, back_tri)
    back_ref[...] = tri_chunk_ref[...].astype(BF16)
    for t in range(tiles):
        at = slice(t * LANES, (t + 1) * LANES)
        gate = gate_sig[:, at]
        gate_mask = gate * mask[t]
        store_pairs(update_ref, t, gate_mask * out_proj[:, at])
        cotangent = spread_ref[at, :].T
        gate_ref[:, at] = (cotangent * mask[t] * out_proj[:, at] * gate * (1.0 - gate)).astype(BF16)


def back_kernel(
    na, nb, mine_ref, theirs_ref, keep_ref, out_ref, back_chunk_ref, plane_ref, chunk_ref, whole_ref
):
    tiles = na // 2
    half = tiles // 2
    core = my_core()
    back_chunk_ref[core] = mine_ref[...].astype(F32)
    back_chunk_ref[1 - core] = theirs_ref[...].astype(F32)
    clear_gaps(plane_ref, nb)
    for side in range(2):
        chunks_to_plane(back_chunk_ref.at[side], plane_ref, 4, half, side * 2 * half, na)
    whole_ref[...] = whole_plane(plane_ref)

    def keep_tiles(product):
        for pair in range(4):
            plane_ref[pair] = product[:, pair * LANES : (pair + 1) * LANES]

    @pl.when(core == 0)
    def _():
        keep_tiles(matmul(whole_ref[...], keep_ref[...]))

    @pl.when(core == 1)
    def _():
        keep_tiles(matmul(whole_ref[...], keep_ref[...], TN))

    plane_to_chunks(plane_ref, chunk_ref, tiles, tiles, 0, na)
    out_ref[...] = chunk_ref[...].astype(BF16)


def weight_kernel(
    valid_ref,
    back_ref,
    acts_ref,
    gain_ref,
    weight_ref,
    gate_ref,
    grad_weight_ref,
    back_proj_ref,
    spread_ref,
    normed_ref,
    chunk_ref,
):
    na, nb, _ = acts_ref.shape
    tiles = na // 2
    hidden = weight_ref.shape[0]
    spread(acts_ref, spread_ref)
    norm_tiles(spread_ref, gain_ref, normed_ref)
    mask = masks(valid_ref, na, nb)
    projected = matmul(weight_ref[:, 0 : 4 * hidden], normed_ref[...], TN)
    chunk_ref[...] = back_ref[...].astype(F32)
    back_proj_ref[4 * hidden :, :] = gate_ref[...]
    for t in range(tiles):
        at = slice(t * LANES, (t + 1) * LANES)
        for side in range(2):
            base = 2 * side * hidden
            upstream = get_channels(chunk_ref, t, tiles, side, hidden) * mask[t]
            gate = jax.nn.sigmoid(projected[base : base + hidden, at])
            value = projected[base + hidden : base + 2 * hidden, at]
            back_proj_ref[base : base + hidden, at] = (upstream * value * gate * (1.0 - gate)).astype(
                BF16
            )
            back_proj_ref[base + hidden : base + 2 * hidden, at] = (upstream * gate).astype(BF16)
    grad_weight_ref[...] = matmul(normed_ref[...], back_proj_ref[...], NT).astype(BF16)


def pair_kernel(acts_ref, gain_ref, weight_ref, back_proj_ref, grad_pair_ref, spread_ref):
    na, nb, _ = acts_ref.shape
    spread(acts_ref, spread_ref)
    gain = column(gain_ref)
    back_normed = matmul(weight_ref[...], back_proj_ref[...])
    for t in range(na // 2):
        at = slice(t * LANES, (t + 1) * LANES)
        scaled, inv = tile_norm(spread_ref[at, :].T)
        store_pairs(grad_pair_ref, t, tile_norm_grad(back_normed[:, at] * gain, scaled, inv))


def local_call(body, outs, scratch, flops, smem_first=False, inputs=1):
    specs = [pl.BlockSpec(memory_space=pltpu.VMEM)] * inputs
    if smem_first:
        specs[0] = pl.BlockSpec(memory_space=pltpu.SMEM)
    return pl.pallas_call(
        body,
        out_shape=outs,
        in_specs=specs,
        out_specs=jax.tree.map(lambda _: pl.BlockSpec(memory_space=pltpu.VMEM), outs),
        scratch_shapes=scratch,
        compiler_params=pltpu.CompilerParams(vmem_limit_bytes=VMEM_LIMIT),
        cost_estimate=pl.CostEstimate(flops=flops, bytes_accessed=2_000_000, transcendentals=0),
    )


def exchange(chunks, depth):
    devices = chunks.shape[0] // depth
    split = chunks.reshape(devices, depth // 2, 2, chunks.shape[1])
    return lax.all_to_all(split, AXES, 0, 0, tiled=True).reshape(chunks.shape)


def make_per_device(num_r, num_c):
    devices = num_r * num_c

    def other_core(values):
        return lax.ppermute(values, "row", [(i, i ^ 1) for i in range(num_r)])

    def per_device(pair_acts, token_valid, norm_gain, proj_weight, out_gain, out_weight, out_cotangent):
        na, nb, channels = pair_acts.shape
        hidden = out_weight.shape[0]
        width_all = proj_weight.shape[1]
        full_len = token_valid.shape[0]
        tiles = na // 2
        lanes = tiles * LANES
        plane = (num_r // 4) * SLOT
        full = jax.ShapeDtypeStruct((devices * tiles, LANES), BF16)
        part = jax.ShapeDtypeStruct((devices * 4, LANES), BF16)
        pairs = jax.ShapeDtypeStruct(pair_acts.shape, BF16)
        gain = norm_gain.reshape(1, channels)
        spread_scratch = pltpu.VMEM((lanes, channels), F32)
        normed_scratch = pltpu.VMEM((channels, lanes), BF16)
        full_scratch = pltpu.VMEM(full.shape, F32)

        sides = local_call(
            sides_kernel,
            full,
            [spread_scratch, normed_scratch, full_scratch],
            100_000_000,
            smem_first=True,
            inputs=4,
        )(token_valid, pair_acts, gain, proj_weight)
        mine = exchange(sides, tiles)
        theirs = other_core(mine)
        tri, keep = local_call(
            functools.partial(tri_kernel, na, nb),
            (part, jax.ShapeDtypeStruct((plane, plane), BF16)),
            [
                pltpu.VMEM((2,) + full.shape, F32),
                pltpu.VMEM((2, 4, plane, LANES), F32),
                pltpu.VMEM(part.shape, F32),
            ],
            300_000_000,
            inputs=2,
        )(mine, theirs)
        tri = exchange(tri, 4)
        update, back, gate = local_call(
            middle_kernel,
            (pairs, part, jax.ShapeDtypeStruct((channels, lanes), BF16)),
            [
                spread_scratch,
                normed_scratch,
                pltpu.VMEM(part.shape, F32),
                pltpu.VMEM((hidden, lanes), F32),
                pltpu.VMEM((hidden, lanes), BF16),
                pltpu.VMEM((channels, lanes), BF16),
            ],
            100_000_000,
            smem_first=True,
            inputs=8,
        )(
            token_valid,
            tri,
            pair_acts,
            out_cotangent,
            gain,
            proj_weight,
            out_gain.reshape(1, hidden),
            out_weight,
        )
        back = exchange(back, 4)
        back_sides = local_call(
            functools.partial(back_kernel, na, nb),
            full,
            [
                pltpu.VMEM((2,) + part.shape, F32),
                pltpu.VMEM((4, plane, LANES), F32),
                full_scratch,
                pltpu.VMEM((plane, plane), BF16),
            ],
            300_000_000,
            inputs=3,
        )(back, other_core(back), keep)
        back_sides = exchange(back_sides, tiles)
        weight_term, back_proj = local_call(
            weight_kernel,
            (
                jax.ShapeDtypeStruct((channels, width_all), BF16),
                jax.ShapeDtypeStruct((width_all, lanes), BF16),
            ),
            [spread_scratch, normed_scratch, full_scratch],
            200_000_000,
            smem_first=True,
            inputs=6,
        )(token_valid, back_sides, pair_acts, gain, proj_weight, gate)
        grad_pair = local_call(pair_kernel, pairs, [spread_scratch], 100_000_000, inputs=4)(
            pair_acts, gain, proj_weight, back_proj
        )
        parts = lax.all_to_all(weight_term.reshape(devices, -1), AXES, 0, 0, tiled=True)
        total = jnp.sum(parts.astype(F32), axis=0) / full_len
        copies = jnp.broadcast_to(total.astype(BF16), (devices,) + total.shape)
        grad_weight = lax.all_to_all(copies, AXES, 0, 0, tiled=True)
        return update, grad_pair, grad_weight.reshape(channels, width_all).astype(F32)

    return per_device


def solution(mesh):
    placed = (P("row", "col", None), P(), P(), P(), P(), P(), P("row", "col", None))
    return jax.shard_map(
        make_per_device(mesh.shape["row"], mesh.shape["col"]),
        mesh=mesh,
        in_specs=placed,
        out_specs=(P("row", "col", None), P("row", "col", None), P()),
        check_vma=False,
    )
```

```python
import functools

import jax
import jax.numpy as jnp
from jax import lax
from jax.experimental import pallas as pl
from jax.experimental.pallas import tpu as pltpu
from jax.sharding import Mesh
from jax.sharding import PartitionSpec as P

EPSILON = 1e-05
BF16 = jnp.bfloat16
F32 = jnp.float32
ALL_AXES = ("chip", "core", "col")
CHANNEL_AXES = ("chip", "col")
LANES = 128
SLOT = 64
PIECE = 16
SIDE_ROWS = 10
TRI_ROWS = 6
VMEM_LIMIT = 48 * 1024 * 1024

NT = (((1,), (1,)), ((), ()))
NN = (((1,), (0,)), ((), ()))
TN = (((0,), (0,)), ((), ()))


def matmul(lhs, rhs, dims=NN):
    return lax.dot_general(lhs, rhs, dims, preferred_element_type=F32)


def column(row_ref):
    return jnp.broadcast_to(row_ref[...], (LANES, LANES)).T


def swap_halves(values):
    return pltpu.roll(values, SLOT, 1)


def low_half(shape):
    return lax.broadcasted_iota(jnp.int32, shape, 1) < SLOT


def spread(pairs_ref, spread_ref):
    na, nb, channels = pairs_ref.shape
    for a in range(na):
        spread_ref[a * SLOT : a * SLOT + nb, :] = pairs_ref[a].astype(F32)
        spread_ref[a * SLOT + nb : (a + 1) * SLOT, :] = jnp.zeros((SLOT - nb, channels), F32)


def store_pairs(out_ref, t, values):
    nb = out_ref.shape[1]
    turned = values.T
    out_ref[2 * t] = turned[0:nb].astype(out_ref.dtype)
    out_ref[2 * t + 1] = turned[SLOT : SLOT + nb].astype(out_ref.dtype)


def masks(valid_ref, na, nb):
    lane = lax.broadcasted_iota(jnp.int32, (1, LANES), 1)
    place = lane % SLOT
    first_row = (2 * lax.axis_index("chip") + lax.axis_index("core")) * na
    first_col = lax.axis_index("col") * nb
    cols = jnp.zeros((1, LANES), jnp.int32)
    for b in range(nb):
        cols = jnp.where(place == b, valid_ref[first_col + b], cols)
    found = []
    for t in range(na // 2):
        rows = jnp.where(lane < SLOT, valid_ref[first_row + 2 * t], valid_ref[first_row + 2 * t + 1])
        found.append((rows * cols).astype(F32))
    return found


def tile_norm(values):
    center = jnp.mean(values, axis=0, keepdims=True)
    shifted = values - center
    inv_std = lax.rsqrt(jnp.mean(shifted * shifted, axis=0, keepdims=True) + EPSILON)
    return shifted * inv_std, inv_std


def tile_norm_grad(upstream, scaled, inv_std):
    first = jnp.mean(upstream, axis=0, keepdims=True)
    second = jnp.mean(upstream * scaled, axis=0, keepdims=True)
    return inv_std * (upstream - first - scaled * second)


def norm_tiles(spread_ref, gain_ref, normed_ref):
    gain = column(gain_ref)
    tiles = spread_ref.shape[0] // LANES
    for t in range(tiles):
        at = slice(t * LANES, (t + 1) * LANES)
        scaled, _ = tile_norm(spread_ref[at, :].T)
        normed_ref[:, at] = (scaled * gain).astype(BF16)


def gap(shape):
    return lax.broadcasted_iota(jnp.int32, shape, 1) % SLOT >= SLOT - PIECE


def pack_tiles(tiles):
    free = gap(tiles[0].shape)
    rows = []
    for t in range(9):
        moved = pltpu.roll(tiles[9 + t // 3], SLOT - PIECE - PIECE * (t % 3), 1)
        rows.append(jnp.where(free, moved, tiles[t]))
    return rows


def unpack_tiles(rows):
    free = gap(rows[0].shape)
    place = lax.broadcasted_iota(jnp.int32, rows[0].shape, 1) % SLOT // PIECE
    tiles = [jnp.where(free, 0.0, row) for row in rows]
    for m in range(3):
        tile = jnp.zeros_like(rows[0])
        for p in range(3):
            moved = pltpu.roll(rows[3 * m + p], LANES - (SLOT - PIECE) + PIECE * p, 1)
            tile = jnp.where(place == p, moved, tile)
        tiles.append(tile)
    return tiles


def device_rows(chunk_ref, depth, row):
    return chunk_ref[pl.ds(row, chunk_ref.shape[0] // depth, stride=depth), :]


def put_device_rows(chunk_ref, depth, row, values):
    chunk_ref[pl.ds(row, chunk_ref.shape[0] // depth, stride=depth), :] = values


def group_rows(depth, lo, col, row):
    return pl.ds(depth * (8 * lo + col) + row, 8, stride=16 * depth)


def put_plane(plane_ref, pair, start, step, even, odd):
    low = low_half(even.shape)
    plane_ref[pair, pl.ds(start, 8, stride=step), :] = jnp.where(low, even, swap_halves(odd))
    plane_ref[pair, pl.ds(start + 1, 8, stride=step), :] = jnp.where(low, swap_halves(even), odd)


def get_plane(plane_ref, pair, start, step):
    upper = plane_ref[pair, pl.ds(start, 8, stride=step), :]
    lower = plane_ref[pair, pl.ds(start + 1, 8, stride=step), :]
    low = low_half(upper.shape)
    return jnp.where(low, upper, swap_halves(lower)), jnp.where(low, swap_halves(upper), lower)


def clear_rows(plane_ref, group, used):
    for pair in range(plane_ref.shape[0]):
        for start in range(0, plane_ref.shape[1], group):
            plane_ref[pair, start + used : start + group, :] = jnp.zeros((group - used, LANES), F32)


def whole_plane(plane_ref, rows=slice(None)):
    return jnp.concatenate([plane_ref[pair, rows, :].astype(BF16) for pair in range(4)], axis=1)


def keep_tiles(plane_ref, product):
    for pair in range(4):
        plane_ref[pair] = product[:, pair * LANES : (pair + 1) * LANES]


def sides_kernel(valid_ref, acts_ref, gain_ref, weight_ref, out_ref, spread_ref, normed_ref, chunk_ref):
    na, nb, _ = acts_ref.shape
    tiles = na // 2
    hidden = weight_ref.shape[0]
    spread(acts_ref, spread_ref)
    norm_tiles(spread_ref, gain_ref, normed_ref)
    mask = masks(valid_ref, na, nb)
    projected = matmul(weight_ref[:, 0 : 4 * hidden], normed_ref[...], TN)
    found = []
    for side in range(2):
        base = 2 * side * hidden
        for t in range(tiles):
            at = slice(t * LANES, (t + 1) * LANES)
            gate = jax.nn.sigmoid(projected[base : base + hidden, at])
            value = projected[base + hidden : base + 2 * hidden, at]
            found.append(gate * value * mask[t])
    for t, row in enumerate(pack_tiles(found)):
        put_device_rows(chunk_ref, SIDE_ROWS, t, row)
    put_device_rows(chunk_ref, SIDE_ROWS, 9, jnp.zeros((hidden, LANES), F32))
    out_ref[...] = chunk_ref[...].astype(BF16)


def tri_kernel(
    na, nb, mine_ref, theirs_ref, tri_ref, left_ref, right_ref, chunk_ref, left_plane_ref, right_plane_ref, tri_chunk_ref
):
    tiles = na // 2
    core = lax.axis_index("core")
    chunk_ref[core] = mine_ref[...].astype(F32)
    chunk_ref[1 - core] = theirs_ref[...].astype(F32)
    clear_rows(left_plane_ref, 32, 2 * na)
    clear_rows(right_plane_ref, SLOT, 4 * na)
    for side in range(2):
        for pair in range(4):
            for lo in range(2):
                both = []
                for col in (2 * pair, 2 * pair + 1):
                    both.append(
                        unpack_tiles(
                            [chunk_ref[side, group_rows(SIDE_ROWS, lo, col, t), :] for t in range(9)]
                        )
                    )
                even, odd = both
                for t in range(tiles):
                    put_plane(left_plane_ref, pair, 256 * side + na * lo + 2 * t, 32, even[t], odd[t])
                    start = na * (2 * lo + side) + 2 * t
                    put_plane(right_plane_ref, pair, start, SLOT, even[tiles + t], odd[tiles + t])
    left_ref[...] = whole_plane(left_plane_ref)
    right_ref[...] = whole_plane(right_plane_ref)
    half = pl.ds(pl.multiple_of(core * 256, 256), 256)
    tri = matmul(whole_plane(left_plane_ref, half), right_ref[...], NT)
    keep_tiles(left_plane_ref.at[:, 0:256], tri)
    for pair in range(4):
        for lo in range(2):
            for t in range(tiles):
                even, odd = get_plane(left_plane_ref, pair, na * lo + 2 * t, 32)
                tri_chunk_ref[group_rows(TRI_ROWS, lo, 2 * pair, t), :] = even
                tri_chunk_ref[group_rows(TRI_ROWS, lo, 2 * pair + 1, t), :] = odd
    tri_ref[...] = tri_chunk_ref[...].astype(BF16)


def middle_kernel(
    valid_ref,
    tri_ref,
    acts_ref,
    cotangent_ref,
    gain_ref,
    weight_ref,
    out_gain_ref,
    out_weight_ref,
    update_ref,
    back_ref,
    gate_ref,
    spread_ref,
    normed_ref,
    tri_chunk_ref,
    tri_plane_ref,
    normed_out_ref,
    back_out_ref,
):
    na, nb, _ = acts_ref.shape
    tiles = na // 2
    hidden = out_weight_ref.shape[0]
    spread(acts_ref, spread_ref)
    norm_tiles(spread_ref, gain_ref, normed_ref)
    mask = masks(valid_ref, na, nb)
    gate_sig = jax.nn.sigmoid(matmul(weight_ref[:, 4 * hidden :], normed_ref[...], TN))
    spread(cotangent_ref, spread_ref)
    tri_chunk_ref[...] = tri_ref[...].astype(F32)
    out_gain = column(out_gain_ref)
    inv_out = []
    for t in range(tiles):
        at = slice(t * LANES, (t + 1) * LANES)
        scaled, inv = tile_norm(device_rows(tri_chunk_ref, TRI_ROWS, t))
        inv_out.append(inv)
        tri_plane_ref[:, at] = scaled
        normed_out_ref[:, at] = (scaled * out_gain).astype(BF16)
        gate_mask = gate_sig[:, at] * mask[t]
        back_out_ref[:, at] = (spread_ref[at, :].T * gate_mask).astype(BF16)
    out_proj = matmul(out_weight_ref[...], normed_out_ref[...], TN)
    back_norm = matmul(out_weight_ref[...], back_out_ref[...])
    for t in range(tiles):
        at = slice(t * LANES, (t + 1) * LANES)
        gate = gate_sig[:, at]
        store_pairs(update_ref, t, gate * mask[t] * out_proj[:, at])
        cotangent = spread_ref[at, :].T
        gate_ref[:, at] = (cotangent * mask[t] * out_proj[:, at] * gate * (1.0 - gate)).astype(BF16)
    term = matmul(normed_ref[...], gate_ref[...], NT)
    free = gap(term.shape)
    for t in range(tiles):
        at = slice(t * LANES, (t + 1) * LANES)
        row = tile_norm_grad(back_norm[:, at] * out_gain, tri_plane_ref[:, at], inv_out[t])
        if t < 4:
            moved = pltpu.roll(term, SLOT - PIECE - PIECE * t, 1) if t < 3 else term
            row = jnp.where(free, moved, row)
        put_device_rows(tri_chunk_ref, TRI_ROWS, t, row)
    back_ref[...] = tri_chunk_ref[...].astype(BF16)


def back_kernel(
    na,
    nb,
    mine_ref,
    theirs_ref,
    left_ref,
    right_ref,
    out_ref,
    back_chunk_ref,
    left_plane_ref,
    right_plane_ref,
    chunk_ref,
    whole_ref,
):
    tiles = na // 2
    core = lax.axis_index("core")
    back_chunk_ref[core] = mine_ref[...].astype(F32)
    back_chunk_ref[1 - core] = theirs_ref[...].astype(F32)
    clear_rows(right_plane_ref, 32, 2 * na)
    free = gap((8, LANES))
    for side in range(2):
        for pair in range(4):
            for lo in range(2):
                for t in range(tiles):
                    even, odd = [
                        jnp.where(free, 0.0, back_chunk_ref[side, group_rows(TRI_ROWS, lo, col, t), :])
                        for col in (2 * pair, 2 * pair + 1)
                    ]
                    start = 256 * side + na * lo + 2 * t
                    put_plane(right_plane_ref, pair, start, 32, even, odd)
    whole_ref[...] = whole_plane(right_plane_ref)
    half = pl.ds(pl.multiple_of(core * 256, 256), 256)
    keep_tiles(left_plane_ref, matmul(whole_ref[half, :], right_ref[...]))
    keep_tiles(right_plane_ref, matmul(whole_ref[...], left_ref[...], TN))

    place = lax.broadcasted_iota(jnp.int32, (8, LANES), 1) % SLOT // PIECE
    total = jnp.zeros((8, LANES), F32)
    for t in range(4):
        rows = jnp.zeros((8, LANES), F32)
        for side in range(2):
            for m in range(back_chunk_ref.shape[1] // (8 * TRI_ROWS)):
                rows += back_chunk_ref[side, pl.ds(8 * TRI_ROWS * m + t, 8, stride=TRI_ROWS), :]
        rows = jnp.sum(rows, axis=0, keepdims=True)
        rows = jnp.broadcast_to(rows, (8, LANES))
        if t < 3:
            rows = pltpu.roll(rows, LANES - (SLOT - PIECE) + PIECE * t, 1)
        total = jnp.where(place == t, rows, total)
    total = total * (1.0 / (4 * 8 * na))
    for m in range(chunk_ref.shape[0] // (8 * SIDE_ROWS)):
        chunk_ref[pl.ds(8 * SIDE_ROWS * m + 9, 8, stride=SIDE_ROWS), :] = total

    for pair in range(4):
        for lo in range(2):
            found = [get_plane(left_plane_ref, pair, na * lo + 2 * t, 32) for t in range(tiles)]
            for t in range(tiles):
                start = na * (2 * lo + core) + 2 * t
                found.append(get_plane(right_plane_ref, pair, start, SLOT))
            for side in range(2):
                for t, row in enumerate(pack_tiles([both[side] for both in found])):
                    chunk_ref[group_rows(SIDE_ROWS, lo, 2 * pair + side, t), :] = row
    out_ref[...] = chunk_ref[...].astype(BF16)


def weight_kernel(
    valid_ref,
    back_ref,
    acts_ref,
    gain_ref,
    weight_ref,
    gate_ref,
    term_ref,
    back_proj_ref,
    gate_total_ref,
    spread_ref,
    normed_ref,
    chunk_ref,
    term_chunk_ref,
):
    na, nb, _ = acts_ref.shape
    tiles = na // 2
    hidden = weight_ref.shape[0]
    spread(acts_ref, spread_ref)
    norm_tiles(spread_ref, gain_ref, normed_ref)
    mask = masks(valid_ref, na, nb)
    projected = matmul(weight_ref[:, 0 : 4 * hidden], normed_ref[...], TN)
    chunk_ref[...] = back_ref[...].astype(F32)
    gate_total_ref[...] = device_rows(chunk_ref, SIDE_ROWS, 9)
    back_proj_ref[4 * hidden :, :] = gate_ref[...]
    upstreams = unpack_tiles([device_rows(chunk_ref, SIDE_ROWS, t) for t in range(9)])
    for t in range(tiles):
        at = slice(t * LANES, (t + 1) * LANES)
        for side in range(2):
            base = 2 * side * hidden
            upstream = upstreams[tiles * side + t] * mask[t]
            gate = jax.nn.sigmoid(projected[base : base + hidden, at])
            value = projected[base + hidden : base + 2 * hidden, at]
            back_proj_ref[base : base + hidden, at] = (upstream * value * gate * (1.0 - gate)).astype(
                BF16
            )
            back_proj_ref[base + hidden : base + 2 * hidden, at] = (upstream * gate).astype(BF16)
    term = matmul(normed_ref[...], back_proj_ref[0 : 4 * hidden, :], NT)
    for t in range(4):
        for m in range(hidden // 8):
            term_chunk_ref[weight_rows(m, t), :] = term[8 * m : 8 * m + 8, t * LANES : (t + 1) * LANES]
    term_ref[...] = term_chunk_ref[...].astype(BF16)


def weight_rows(chip, t):
    return pl.ds(2 * (16 * chip + 8 * (t // 2)) + t % 2, 8, stride=2)


def sum_kernel(full_len, parts_ref, out_ref):
    total = jnp.zeros((16, LANES), F32)
    for m in range(parts_ref.shape[0] // 16):
        total += parts_ref[16 * m : 16 * m + 16, :].astype(F32)
    total = total[0:8] + total[8:16]
    total = total + pltpu.roll(total, 4, 0)
    total = total + pltpu.roll(total, 2, 0)
    total = total / full_len
    total = jnp.concatenate([total, total], axis=0).astype(BF16)
    for m in range(parts_ref.shape[0] // 16):
        out_ref[16 * m : 16 * m + 16, :] = total


def grad_weight_kernel(sums_ref, gate_total_ref, out_ref, chunk_ref):
    chunk_ref[...] = sums_ref[...].astype(F32)
    for t in range(4):
        for m in range(out_ref.shape[0] // 8):
            out_ref[8 * m : 8 * m + 8, t * LANES : (t + 1) * LANES] = chunk_ref[weight_rows(m, t), :]
    out_ref[:, 4 * LANES :] = gate_total_ref[...]


def pair_kernel(acts_ref, gain_ref, weight_ref, back_proj_ref, grad_pair_ref, spread_ref):
    na, nb, _ = acts_ref.shape
    spread(acts_ref, spread_ref)
    gain = column(gain_ref)
    back_normed = matmul(weight_ref[...], back_proj_ref[...])
    for t in range(na // 2):
        at = slice(t * LANES, (t + 1) * LANES)
        scaled, inv = tile_norm(spread_ref[at, :].T)
        store_pairs(grad_pair_ref, t, tile_norm_grad(back_normed[:, at] * gain, scaled, inv))


def local_call(body, outs, scratch, flops, smem_first=False, inputs=1):
    specs = [pl.BlockSpec(memory_space=pltpu.VMEM)] * inputs
    if smem_first:
        specs[0] = pl.BlockSpec(memory_space=pltpu.SMEM)
    return pl.pallas_call(
        body,
        out_shape=outs,
        in_specs=specs,
        out_specs=jax.tree.map(lambda _: pl.BlockSpec(memory_space=pltpu.VMEM), outs),
        scratch_shapes=scratch,
        compiler_params=pltpu.CompilerParams(vmem_limit_bytes=VMEM_LIMIT),
        cost_estimate=pl.CostEstimate(flops=flops, bytes_accessed=2_000_000, transcendentals=0),
    )


def exchange(chunks, depth, axes):
    devices = chunks.shape[0] // depth
    split = chunks.reshape(devices, depth // 2, 2, chunks.shape[1])
    return lax.all_to_all(split, axes, 0, 0, tiled=True).reshape(chunks.shape)


def other_core(values):
    return lax.ppermute(values, "core", [(0, 1), (1, 0)])


def per_device(pair_acts, token_valid, norm_gain, proj_weight, out_gain, out_weight, out_cotangent):
    na, nb, channels = pair_acts.shape
    hidden = out_weight.shape[0]
    width_all = proj_weight.shape[1]
    full_len = token_valid.shape[0]
    lanes = na // 2 * LANES
    plane = 512
    sides_chunk = (hidden * SIDE_ROWS, LANES)
    tri_chunk = (hidden * TRI_ROWS, LANES)
    term_chunk = (4 * hidden, LANES)
    pairs = jax.ShapeDtypeStruct(pair_acts.shape, BF16)
    whole = jax.ShapeDtypeStruct((plane, plane), BF16)
    gain = norm_gain.reshape(1, channels)
    spread_scratch = pltpu.VMEM((lanes, channels), F32)
    normed_scratch = pltpu.VMEM((channels, lanes), BF16)
    half_plane = pltpu.VMEM((4, plane // 2, LANES), F32)
    full_plane = pltpu.VMEM((4, plane, LANES), F32)

    sides = local_call(
        sides_kernel,
        jax.ShapeDtypeStruct(sides_chunk, BF16),
        [spread_scratch, normed_scratch, pltpu.VMEM(sides_chunk, F32)],
        100_000_000,
        smem_first=True,
        inputs=4,
    )(token_valid, pair_acts, gain, proj_weight)
    mine = exchange(sides, SIDE_ROWS, CHANNEL_AXES)
    tri, left, right = local_call(
        functools.partial(tri_kernel, na, nb),
        (jax.ShapeDtypeStruct(tri_chunk, BF16), whole, whole),
        [pltpu.VMEM((2,) + sides_chunk, F32), full_plane, full_plane, pltpu.VMEM(tri_chunk, F32)],
        300_000_000,
        inputs=2,
    )(mine, other_core(mine))
    tri = exchange(tri, TRI_ROWS, CHANNEL_AXES)
    update, back, gate = local_call(
        middle_kernel,
        (pairs, jax.ShapeDtypeStruct(tri_chunk, BF16), jax.ShapeDtypeStruct((channels, lanes), BF16)),
        [
            spread_scratch,
            normed_scratch,
            pltpu.VMEM(tri_chunk, F32),
            pltpu.VMEM((hidden, lanes), F32),
            pltpu.VMEM((hidden, lanes), BF16),
            pltpu.VMEM((channels, lanes), BF16),
        ],
        100_000_000,
        smem_first=True,
        inputs=8,
    )(
        token_valid,
        tri,
        pair_acts,
        out_cotangent,
        gain,
        proj_weight,
        out_gain.reshape(1, hidden),
        out_weight,
    )
    back = exchange(back, TRI_ROWS, CHANNEL_AXES)
    back_sides = local_call(
        functools.partial(back_kernel, na, nb),
        jax.ShapeDtypeStruct(sides_chunk, BF16),
        [
            pltpu.VMEM((2,) + tri_chunk, F32),
            half_plane,
            full_plane,
            pltpu.VMEM(sides_chunk, F32),
            pltpu.VMEM((plane, plane), BF16),
        ],
        300_000_000,
        inputs=4,
    )(back, other_core(back), left, right)
    back_sides = exchange(back_sides, SIDE_ROWS, CHANNEL_AXES)
    term, back_proj, gate_total = local_call(
        weight_kernel,
        (
            jax.ShapeDtypeStruct(term_chunk, BF16),
            jax.ShapeDtypeStruct((width_all, lanes), BF16),
            jax.ShapeDtypeStruct((channels, channels), F32),
        ),
        [
            spread_scratch,
            normed_scratch,
            pltpu.VMEM(sides_chunk, F32),
            pltpu.VMEM(term_chunk, F32),
        ],
        200_000_000,
        smem_first=True,
        inputs=6,
    )(token_valid, back_sides, pair_acts, gain, proj_weight, gate)
    grad_pair = local_call(pair_kernel, pairs, [spread_scratch], 100_000_000, inputs=4)(
        pair_acts, gain, proj_weight, back_proj
    )
    parts = exchange(term, 2, ALL_AXES)
    sums = local_call(
        functools.partial(sum_kernel, full_len), jax.ShapeDtypeStruct(term_chunk, BF16), [], 100_000
    )(parts)
    sums = exchange(sums, 2, ALL_AXES)
    grad_weight = local_call(
        grad_weight_kernel,
        jax.ShapeDtypeStruct((channels, width_all), F32),
        [pltpu.VMEM(term_chunk, F32)],
        100_000,
        inputs=2,
    )(sums, gate_total)
    return update, grad_pair, grad_weight


def solution(mesh):
    rows, cols = mesh.devices.shape
    split = Mesh(mesh.devices.reshape(rows // 2, 2, cols), ("chip", "core", "col"))
    pairs = P(("chip", "core"), "col", None)
    return jax.shard_map(
        per_device,
        mesh=split,
        in_specs=(pairs, P(), P(), P(), P(), P(), pairs),
        out_specs=(pairs, pairs, P()),
        check_vma=False,
    )
```

```python
import functools

import jax
import jax.numpy as jnp
from jax import lax
from jax.experimental import pallas as pl
from jax.experimental.pallas import tpu as pltpu
from jax.sharding import Mesh
from jax.sharding import PartitionSpec as P

EPSILON = 1e-05
BF16 = jnp.bfloat16
F32 = jnp.float32
ALL_AXES = ("chip", "core", "col")
CHANNEL_AXES = ("col", "chip")
LANES = 128
SLOT = 64
PIECE = 16
SIDE_ROWS = 10
TRI_ROWS = 6
VMEM_LIMIT = 48 * 1024 * 1024

NT = (((1,), (1,)), ((), ()))
NN = (((1,), (0,)), ((), ()))
TN = (((0,), (0,)), ((), ()))


def matmul(lhs, rhs, dims=NN):
    return lax.dot_general(lhs, rhs, dims, preferred_element_type=F32)


def column(row_ref):
    return jnp.broadcast_to(row_ref[...], (LANES, LANES)).T


def swap_halves(values):
    return pltpu.roll(values, SLOT, 1)


def low_half(shape):
    return lax.broadcasted_iota(jnp.int32, shape, 1) < SLOT


def spread(pairs_ref, spread_ref):
    na, nb, channels = pairs_ref.shape
    for a in range(na):
        spread_ref[a * SLOT : a * SLOT + nb, :] = pairs_ref[a].astype(F32)
        spread_ref[a * SLOT + nb : (a + 1) * SLOT, :] = jnp.zeros((SLOT - nb, channels), F32)


def store_pairs(out_ref, t, values):
    nb = out_ref.shape[1]
    turned = values.T
    out_ref[2 * t] = turned[0:nb].astype(out_ref.dtype)
    out_ref[2 * t + 1] = turned[SLOT : SLOT + nb].astype(out_ref.dtype)


def masks(valid_ref, na, nb):
    lane = lax.broadcasted_iota(jnp.int32, (1, LANES), 1)
    place = lane % SLOT
    first_row = (2 * lax.axis_index("chip") + lax.axis_index("core")) * na
    first_col = lax.axis_index("col") * nb
    cols = jnp.zeros((1, LANES), jnp.int32)
    for b in range(nb):
        cols = jnp.where(place == b, valid_ref[first_col + b], cols)
    found = []
    for t in range(na // 2):
        rows = jnp.where(lane < SLOT, valid_ref[first_row + 2 * t], valid_ref[first_row + 2 * t + 1])
        found.append((rows * cols).astype(F32))
    return found


def tile_norm(values):
    center = jnp.mean(values, axis=0, keepdims=True)
    shifted = values - center
    inv_std = lax.rsqrt(jnp.mean(shifted * shifted, axis=0, keepdims=True) + EPSILON)
    return shifted * inv_std, inv_std


def tile_norm_grad(upstream, scaled, inv_std):
    first = jnp.mean(upstream, axis=0, keepdims=True)
    second = jnp.mean(upstream * scaled, axis=0, keepdims=True)
    return inv_std * (upstream - first - scaled * second)


def norm_tiles(spread_ref, gain_ref, normed_ref):
    gain = column(gain_ref)
    tiles = spread_ref.shape[0] // LANES
    for t in range(tiles):
        at = slice(t * LANES, (t + 1) * LANES)
        scaled, _ = tile_norm(spread_ref[at, :].T)
        normed_ref[:, at] = (scaled * gain).astype(BF16)


def gap(shape):
    return lax.broadcasted_iota(jnp.int32, shape, 1) % SLOT >= SLOT - PIECE


def pack_tiles(tiles):
    free = gap(tiles[0].shape)
    rows = []
    for t in range(9):
        moved = pltpu.roll(tiles[9 + t // 3], SLOT - PIECE - PIECE * (t % 3), 1)
        rows.append(jnp.where(free, moved, tiles[t]))
    return rows


def unpack_tiles(rows):
    free = gap(rows[0].shape)
    place = lax.broadcasted_iota(jnp.int32, rows[0].shape, 1) % SLOT // PIECE
    tiles = [jnp.where(free, 0.0, row) for row in rows]
    for m in range(3):
        tile = jnp.zeros_like(rows[0])
        for p in range(3):
            moved = pltpu.roll(rows[3 * m + p], LANES - (SLOT - PIECE) + PIECE * p, 1)
            tile = jnp.where(place == p, moved, tile)
        tiles.append(tile)
    return tiles


def device_rows(chunk_ref, depth, row):
    return chunk_ref[pl.ds(row, chunk_ref.shape[0] // depth, stride=depth), :]


def put_device_rows(chunk_ref, depth, row, values):
    chunk_ref[pl.ds(row, chunk_ref.shape[0] // depth, stride=depth), :] = values


def group_rows(depth, lo, col, row):
    return pl.ds(depth * (16 * col + lo) + row, 8, stride=2 * depth)


def plane_rows(na, lo, t):
    return slice(8 * (na * lo + 2 * t), 8 * (na * lo + 2 * t) + 16)


def plane_tile(even, odd):
    low = low_half(even.shape)
    upper = jnp.where(low, even, swap_halves(odd))
    lower = jnp.where(low, swap_halves(even), odd)
    return jnp.concatenate([upper, lower], axis=0)


def chunk_tiles(rows):
    upper, lower = rows[0:8], rows[8:16]
    low = low_half(upper.shape)
    return jnp.where(low, upper, swap_halves(lower)), jnp.where(low, swap_halves(upper), lower)


def token_order(na, plane):
    row = lax.broadcasted_iota(jnp.int32, (16 * 2 * na, plane), 0)
    token = lax.broadcasted_iota(jnp.int32, (16 * 2 * na, plane), 1)
    place = row // 8
    core = (place >= 2 * na).astype(jnp.int32)
    place = place - 2 * na * core
    lo = (place >= na).astype(jnp.int32)
    a = place - na * lo
    return (token == SLOT * (row % 8) + na * (2 * lo + core) + a).astype(F32).astype(BF16)


def sides_kernel(
    valid_hbm, acts_hbm, gain_hbm, weight_hbm, out_ref, mask_ref,
    valid_ref, acts_ref, gain_ref, weight_ref, spread_ref, normed_ref, chunk_ref, sems,
):
    na, nb, _ = acts_hbm.shape
    tiles = na // 2
    hidden = weight_hbm.shape[0]
    copies = [
        pltpu.make_async_copy(valid_hbm, valid_ref, sems.at[0]),
        pltpu.make_async_copy(acts_hbm, acts_ref, sems.at[1]),
        pltpu.make_async_copy(gain_hbm, gain_ref, sems.at[2]),
        pltpu.make_async_copy(weight_hbm, weight_ref, sems.at[3]),
    ]
    for copy in copies:
        copy.start()
    copies[0].wait()
    mask = masks(valid_ref, na, nb)
    for t in range(tiles):
        mask_ref[:, t * LANES : (t + 1) * LANES] = mask[t]
    copies[1].wait()
    spread(acts_ref, spread_ref)
    copies[2].wait()
    norm_tiles(spread_ref, gain_ref, normed_ref)
    copies[3].wait()
    projected = matmul(weight_ref[:, 0 : 4 * hidden], normed_ref[...], TN)
    found = []
    for side in range(2):
        base = 2 * side * hidden
        for t in range(tiles):
            at = slice(t * LANES, (t + 1) * LANES)
            gate = jax.nn.sigmoid(projected[base : base + hidden, at])
            value = projected[base + hidden : base + 2 * hidden, at]
            found.append(gate * value * mask[t])
    for t, row in enumerate(pack_tiles(found)):
        put_device_rows(chunk_ref, SIDE_ROWS, t, row)
    put_device_rows(chunk_ref, SIDE_ROWS, 9, jnp.zeros((hidden, LANES), F32))
    out_ref[...] = chunk_ref[...].astype(BF16)


def ready_kernel(
    mask_ref, acts_ref, cotangent_ref, gain_ref, weight_ref, out_gain_ref, out_weight_ref,
    normed_ref, back_norm_ref, gate_mask_ref, gate_coef_ref, coef_ref, order_ref,
    spread_ref, back_out_ref,
):
    na = acts_ref.shape[0]
    tiles = na // 2
    hidden = out_weight_ref.shape[0]
    spread(acts_ref, spread_ref)
    norm_tiles(spread_ref, gain_ref, normed_ref)
    spread(cotangent_ref, spread_ref)
    projected = matmul(weight_ref[...], normed_ref[...], TN)
    for t in range(tiles):
        at = slice(t * LANES, (t + 1) * LANES)
        mask = mask_ref[:, at]
        gate = jax.nn.sigmoid(projected[4 * hidden :, at])
        gate_mask = gate * mask
        cotangent = spread_ref[at, :].T
        gate_mask_ref[:, at] = gate_mask
        gate_coef_ref[:, at] = cotangent * gate_mask * (1.0 - gate)
        back_out_ref[:, at] = (cotangent * gate_mask).astype(BF16)
        for base in (0, 2 * hidden):
            gate = jax.nn.sigmoid(projected[base : base + hidden, at])
            value = projected[base + hidden : base + 2 * hidden, at]
            coef_ref[base : base + hidden, at] = value * gate * (1.0 - gate) * mask
            coef_ref[base + hidden : base + 2 * hidden, at] = gate * mask
    out_gain = column(out_gain_ref)
    back_norm = matmul(out_weight_ref[...], back_out_ref[...])
    for t in range(tiles):
        at = slice(t * LANES, (t + 1) * LANES)
        back_norm_ref[:, at] = back_norm[:, at] * out_gain
    order_ref[...] = token_order(na, order_ref.shape[1])


def my_rows(ref):
    half = ref.shape[-2] // 2
    return pl.ds(pl.multiple_of(lax.axis_index("core") * half, half), half)


def tri_kernel(
    na, mine_ref, theirs_ref, order_ref, tri_ref, left_ref, right_ref, chunk_ref, tri_chunk_ref
):
    tiles = na // 2
    core = lax.axis_index("core")
    chunk_ref[core] = mine_ref[...].astype(F32)
    chunk_ref[1 - core] = theirs_ref[...].astype(F32)
    half = left_ref.shape[0] // 2
    for side in range(2):
        for pair in range(4):
            at = slice(pair * LANES, (pair + 1) * LANES)
            for lo in range(2):
                even, odd = [
                    unpack_tiles(
                        [chunk_ref[side, group_rows(SIDE_ROWS, lo, col, t), :] for t in range(9)]
                    )
                    for col in (2 * pair, 2 * pair + 1)
                ]
                for t in range(tiles):
                    rows = plane_rows(na, lo, t)
                    rows = slice(side * half + rows.start, side * half + rows.stop)
                    left_ref[rows, at] = plane_tile(even[t], odd[t]).astype(BF16)
                    right_ref[rows, at] = plane_tile(even[tiles + t], odd[tiles + t]).astype(BF16)
    tri = matmul(left_ref[my_rows(left_ref), :], right_ref[...], NT).astype(BF16)
    tri = matmul(tri, order_ref[...])
    for pair in range(4):
        for lo in range(2):
            for t in range(tiles):
                both = chunk_tiles(tri[plane_rows(na, lo, t), pair * LANES : (pair + 1) * LANES])
                for side in range(2):
                    tri_chunk_ref[group_rows(TRI_ROWS, lo, 2 * pair + side, t), :] = both[side]
    tri_ref[...] = tri_chunk_ref[...].astype(BF16)


def middle_kernel(
    tri_ref, normed_ref, back_norm_ref, gate_coef_ref, out_gain_ref, out_weight_ref,
    back_ref, gate_ref, out_proj_ref,
    tri_chunk_ref, scaled_ref, normed_out_ref,
):
    tiles = normed_ref.shape[1] // LANES
    tri_chunk_ref[...] = tri_ref[...].astype(F32)
    out_gain = column(out_gain_ref)
    inv_out = []
    for t in range(tiles):
        at = slice(t * LANES, (t + 1) * LANES)
        scaled, inv = tile_norm(device_rows(tri_chunk_ref, TRI_ROWS, t))
        inv_out.append(inv)
        scaled_ref[:, at] = scaled
        normed_out_ref[:, at] = (scaled * out_gain).astype(BF16)
    out_proj = matmul(out_weight_ref[...], normed_out_ref[...], TN)
    out_proj_ref[...] = out_proj
    gate_ref[...] = (out_proj * gate_coef_ref[...]).astype(BF16)
    term = matmul(normed_ref[...], gate_ref[...], NT)
    free = gap(term.shape)
    for t in range(tiles):
        at = slice(t * LANES, (t + 1) * LANES)
        row = tile_norm_grad(back_norm_ref[:, at], scaled_ref[:, at], inv_out[t])
        if t < 4:
            moved = pltpu.roll(term, SLOT - PIECE - PIECE * t, 1) if t < 3 else term
            row = jnp.where(free, moved, row)
        put_device_rows(tri_chunk_ref, TRI_ROWS, t, row)
    back_ref[...] = tri_chunk_ref[...].astype(BF16)


def update_kernel(gate_mask_ref, out_proj_ref, update_ref):
    for t in range(update_ref.shape[0] // 2):
        at = slice(t * LANES, (t + 1) * LANES)
        store_pairs(update_ref, t, gate_mask_ref[:, at] * out_proj_ref[:, at])


def back_kernel(
    na, mine_ref, theirs_ref, left_ref, right_ref, order_ref, out_ref,
    back_chunk_ref, chunk_ref, back_ref, turned_ref, side_ref,
):
    tiles = na // 2
    core = lax.axis_index("core")
    back_chunk_ref[core] = mine_ref[...].astype(F32)
    back_chunk_ref[1 - core] = theirs_ref[...].astype(F32)
    half = back_ref.shape[0] // 2
    free = gap((8, LANES))
    for side in range(2):
        for pair in range(4):
            for lo in range(2):
                for t in range(tiles):
                    even, odd = [
                        jnp.where(free, 0.0, back_chunk_ref[side, group_rows(TRI_ROWS, lo, col, t), :])
                        for col in (2 * pair, 2 * pair + 1)
                    ]
                    rows = plane_rows(na, lo, t)
                    rows = slice(side * half + rows.start, side * half + rows.stop)
                    back_ref[rows, pair * LANES : (pair + 1) * LANES] = plane_tile(even, odd).astype(BF16)
    turned_ref[...] = matmul(back_ref[...], order_ref[...], NT).astype(BF16)
    back_left = matmul(turned_ref[my_rows(turned_ref), :], right_ref[...])
    side_ref[...] = matmul(turned_ref[...], left_ref[...], TN)
    back_right = side_ref[my_rows(side_ref), :]

    place = lax.broadcasted_iota(jnp.int32, (8, LANES), 1) % SLOT // PIECE
    total = jnp.zeros((8, LANES), F32)
    for t in range(4):
        rows = jnp.zeros((8, LANES), F32)
        for side in range(2):
            for m in range(back_chunk_ref.shape[1] // (8 * TRI_ROWS)):
                rows += back_chunk_ref[side, pl.ds(8 * TRI_ROWS * m + t, 8, stride=TRI_ROWS), :]
        rows = jnp.sum(rows, axis=0, keepdims=True)
        rows = jnp.broadcast_to(rows, (8, LANES))
        if t < 3:
            rows = pltpu.roll(rows, LANES - (SLOT - PIECE) + PIECE * t, 1)
        total = jnp.where(place == t, rows, total)
    total = total / (4 * 8 * na)
    for m in range(chunk_ref.shape[0] // (8 * SIDE_ROWS)):
        chunk_ref[pl.ds(8 * SIDE_ROWS * m + 9, 8, stride=SIDE_ROWS), :] = total

    for pair in range(4):
        at = slice(pair * LANES, (pair + 1) * LANES)
        for lo in range(2):
            found = [
                chunk_tiles(product[plane_rows(na, lo, t), at])
                for product in (back_left, back_right)
                for t in range(tiles)
            ]
            for side in range(2):
                for t, row in enumerate(pack_tiles([both[side] for both in found])):
                    chunk_ref[group_rows(SIDE_ROWS, lo, 2 * pair + side, t), :] = row
    out_ref[...] = chunk_ref[...].astype(BF16)


def weight_kernel(
    back_ref, normed_ref, coef_ref, gate_ref, term_ref, back_proj_ref, gate_total_ref,
    chunk_ref, term_chunk_ref,
):
    tiles = normed_ref.shape[1] // LANES
    hidden = normed_ref.shape[0]
    chunk_ref[...] = back_ref[...].astype(F32)
    gate_total_ref[...] = device_rows(chunk_ref, SIDE_ROWS, 9)
    back_proj_ref[4 * hidden :, :] = gate_ref[...]
    upstreams = unpack_tiles([device_rows(chunk_ref, SIDE_ROWS, t) for t in range(9)])
    for side in range(2):
        for t in range(tiles):
            at = slice(t * LANES, (t + 1) * LANES)
            for base in (2 * side * hidden, (2 * side + 1) * hidden):
                rows = slice(base, base + hidden)
                back_proj_ref[rows, at] = (upstreams[tiles * side + t] * coef_ref[rows, at]).astype(BF16)
    term = matmul(normed_ref[...], back_proj_ref[0 : 4 * hidden, :], NT)
    for t in range(4):
        for m in range(hidden // 8):
            term_chunk_ref[weight_rows(m, t), :] = term[8 * m : 8 * m + 8, t * LANES : (t + 1) * LANES]
    term_ref[...] = term_chunk_ref[...].astype(BF16)


def weight_rows(chip, t):
    return pl.ds(2 * (16 * chip + 8 * (t // 2)) + t % 2, 8, stride=2)


def sum_kernel(full_len, parts_ref, out_ref):
    total = jnp.zeros((16, LANES), F32)
    for m in range(parts_ref.shape[0] // 16):
        total += parts_ref[16 * m : 16 * m + 16, :].astype(F32)
    total = total[0:8] + total[8:16]
    total = total + pltpu.roll(total, 4, 0)
    total = total + pltpu.roll(total, 2, 0)
    total = total / full_len
    total = jnp.concatenate([total, total], axis=0).astype(BF16)
    for m in range(parts_ref.shape[0] // 16):
        out_ref[16 * m : 16 * m + 16, :] = total


def grad_weight_kernel(sums_ref, gate_total_ref, out_ref, chunk_ref):
    chunk_ref[...] = sums_ref[...].astype(F32)
    for t in range(4):
        for m in range(out_ref.shape[0] // 8):
            out_ref[8 * m : 8 * m + 8, t * LANES : (t + 1) * LANES] = chunk_ref[weight_rows(m, t), :]
    out_ref[:, 4 * LANES :] = gate_total_ref[...]


def pair_kernel(acts_ref, gain_ref, weight_ref, back_proj_ref, grad_pair_ref, spread_ref):
    na, nb, _ = acts_ref.shape
    spread(acts_ref, spread_ref)
    gain = column(gain_ref)
    back_normed = matmul(weight_ref[...], back_proj_ref[...])
    for t in range(na // 2):
        at = slice(t * LANES, (t + 1) * LANES)
        scaled, inv = tile_norm(spread_ref[at, :].T)
        store_pairs(grad_pair_ref, t, tile_norm_grad(back_normed[:, at] * gain, scaled, inv))


def local_call(body, outs, scratch, flops, inputs, space=pltpu.VMEM, limit=VMEM_LIMIT):
    return pl.pallas_call(
        body,
        out_shape=outs,
        in_specs=[pl.BlockSpec(memory_space=space)] * inputs,
        out_specs=jax.tree.map(lambda _: pl.BlockSpec(memory_space=pltpu.VMEM), outs),
        scratch_shapes=scratch,
        compiler_params=pltpu.CompilerParams(vmem_limit_bytes=limit),
        cost_estimate=pl.CostEstimate(flops=flops, bytes_accessed=2_000_000, transcendentals=0),
    )


def exchange(chunks, depth, axes):
    devices = chunks.shape[0] // depth
    split = chunks.reshape(devices, depth // 2, 2, chunks.shape[1])
    return lax.all_to_all(split, axes, 0, 0, tiled=True).reshape(chunks.shape)


def other_core(values):
    return lax.ppermute(values, "core", [(0, 1), (1, 0)])


def array(shape, dtype=BF16):
    return jax.ShapeDtypeStruct(shape, dtype)


def per_device(pair_acts, token_valid, norm_gain, proj_weight, out_gain, out_weight, out_cotangent):
    na, _, channels = pair_acts.shape
    hidden = out_weight.shape[0]
    width_all = proj_weight.shape[1]
    full_len = token_valid.shape[0]
    lanes = na // 2 * LANES
    plane = (full_len, 8 * SLOT)
    sides_chunk = (hidden * SIDE_ROWS, LANES)
    tri_chunk = (hidden * TRI_ROWS, LANES)
    term_chunk = (4 * hidden, LANES)
    gain = norm_gain.reshape(1, channels)
    out_gain = out_gain.reshape(1, hidden)
    spread_scratch = pltpu.VMEM((lanes, channels), F32)

    sides, mask = local_call(
        sides_kernel,
        (array(sides_chunk), array((1, lanes), F32)),
        [
            pltpu.SMEM(token_valid.shape, jnp.int32),
            pltpu.VMEM(pair_acts.shape, BF16),
            pltpu.VMEM(gain.shape, F32),
            pltpu.VMEM(proj_weight.shape, BF16),
            spread_scratch,
            pltpu.VMEM((channels, lanes), BF16),
            pltpu.VMEM(sides_chunk, F32),
            pltpu.SemaphoreType.DMA((4,)),
        ],
        100_000_000,
        4,
        pltpu.HBM,
        64 * 1024 * 1024 - 65536,
    )(token_valid, pair_acts, gain, proj_weight)
    mine = exchange(sides, SIDE_ROWS, CHANNEL_AXES)
    normed, back_norm, gate_mask, gate_coef, coef, order = local_call(
        ready_kernel,
        (
            array((channels, lanes)),
            array((hidden, lanes), F32),
            array((channels, lanes), F32),
            array((channels, lanes), F32),
            array((4 * hidden, lanes), F32),
            array(plane),
        ),
        [spread_scratch, pltpu.VMEM((channels, lanes), BF16)],
        1_000_000_000,
        7,
    )(mask, pair_acts, out_cotangent, gain, proj_weight, out_gain, out_weight)
    mine, normed, order = lax.optimization_barrier((mine, normed, order))
    tri, left, right = local_call(
        functools.partial(tri_kernel, na),
        (array(tri_chunk), array(plane), array(plane)),
        [pltpu.VMEM((2,) + sides_chunk, F32), pltpu.VMEM(tri_chunk, F32)],
        300_000_000,
        3,
    )(mine, other_core(mine), order)
    tri = exchange(tri, TRI_ROWS, CHANNEL_AXES)
    back, gate, out_proj = local_call(
        middle_kernel,
        (array(tri_chunk), array((channels, lanes)), array((channels, lanes), F32)),
        [
            pltpu.VMEM(tri_chunk, F32),
            pltpu.VMEM((hidden, lanes), F32),
            pltpu.VMEM((hidden, lanes), BF16),
        ],
        100_000_000,
        6,
    )(tri, normed, back_norm, gate_coef, out_gain, out_weight)
    back = exchange(back, TRI_ROWS, CHANNEL_AXES)
    update = local_call(update_kernel, array(pair_acts.shape), [], 1_000_000_000, 2)(
        gate_mask, out_proj
    )
    back_sides = local_call(
        functools.partial(back_kernel, na),
        array(sides_chunk),
        [
            pltpu.VMEM((2,) + tri_chunk, F32),
            pltpu.VMEM(sides_chunk, F32),
            pltpu.VMEM(plane, BF16),
            pltpu.VMEM((full_len, full_len), BF16),
            pltpu.VMEM(plane, F32),
        ],
        300_000_000,
        5,
    )(back, other_core(back), left, right, order)
    back_sides = exchange(back_sides, SIDE_ROWS, CHANNEL_AXES)
    term, back_proj, gate_total = local_call(
        weight_kernel,
        (array(term_chunk), array((width_all, lanes)), array((channels, channels), F32)),
        [pltpu.VMEM(sides_chunk, F32), pltpu.VMEM(term_chunk, F32)],
        200_000_000,
        4,
    )(back_sides, normed, coef, gate)
    grad_pair = local_call(
        pair_kernel, array(pair_acts.shape), [spread_scratch], 1_000_000_000, 4
    )(pair_acts, gain, proj_weight, back_proj)
    parts = exchange(term, 2, ALL_AXES)
    sums = local_call(functools.partial(sum_kernel, full_len), array(term_chunk), [], 100_000, 1)(parts)
    sums = exchange(sums, 2, ALL_AXES)
    grad_weight = local_call(
        grad_weight_kernel,
        array((channels, width_all), F32),
        [pltpu.VMEM(term_chunk, F32)],
        100_000,
        2,
    )(sums, gate_total)
    return update, grad_pair, grad_weight


def solution(mesh):
    rows, cols = mesh.devices.shape
    split = Mesh(mesh.devices.reshape(rows // 2, 2, cols), ("chip", "core", "col"))
    pairs = P(("chip", "core"), "col", None)
    return jax.shard_map(
        per_device,
        mesh=split,
        in_specs=(pairs, P(), P(), P(), P(), P(), pairs),
        out_specs=(pairs, pairs, P()),
        check_vma=False,
    )
```

```python
import functools

import jax
import jax.numpy as jnp
from jax import lax
from jax.experimental import pallas as pl
from jax.experimental.pallas import tpu as pltpu
from jax.sharding import Mesh
from jax.sharding import PartitionSpec as P

EPSILON = 1e-05
BF16 = jnp.bfloat16
F32 = jnp.float32
ALL_AXES = ("chip", "core", "col")
CHANNEL_AXES = ("col", "chip")
LANES = 128
SLOT = 64
PIECE = 16
SIDE_ROWS = 10
TRI_ROWS = 6
VMEM_LIMIT = 48 * 1024 * 1024
WHOLE_VMEM = 64 * 1024 * 1024 - 65536
READY_VMEM = 62 * 1024 * 1024

NT = (((1,), (1,)), ((), ()))
NN = (((1,), (0,)), ((), ()))
TN = (((0,), (0,)), ((), ()))


def matmul(lhs, rhs, dims=NN):
    return lax.dot_general(lhs, rhs, dims, preferred_element_type=F32)


def column(row_ref):
    return jnp.broadcast_to(row_ref[...], (LANES, LANES)).T


def swap_halves(values):
    return pltpu.roll(values, SLOT, 1)


def low_half(shape):
    return lax.broadcasted_iota(jnp.int32, shape, 1) < SLOT


def spread(pairs_ref, spread_ref):
    na, nb, channels = pairs_ref.shape
    for a in range(na):
        spread_ref[a * SLOT : a * SLOT + nb, :] = pairs_ref[a].astype(F32)
        spread_ref[a * SLOT + nb : (a + 1) * SLOT, :] = jnp.zeros((SLOT - nb, channels), F32)


def store_pairs(out_ref, t, values):
    nb = out_ref.shape[1]
    turned = values.T
    out_ref[2 * t] = turned[0:nb].astype(out_ref.dtype)
    out_ref[2 * t + 1] = turned[SLOT : SLOT + nb].astype(out_ref.dtype)


def masks(valid_ref, na, nb):
    lane = lax.broadcasted_iota(jnp.int32, (1, LANES), 1)
    place = lane % SLOT
    first_row = (2 * lax.axis_index("chip") + lax.axis_index("core")) * na
    first_col = lax.axis_index("col") * nb
    cols = jnp.zeros((1, LANES), jnp.int32)
    for b in range(nb):
        cols = jnp.where(place == b, valid_ref[first_col + b], cols)
    found = []
    for t in range(na // 2):
        rows = jnp.where(lane < SLOT, valid_ref[first_row + 2 * t], valid_ref[first_row + 2 * t + 1])
        found.append((rows * cols).astype(F32))
    return found


def tile_norm(values):
    center = jnp.mean(values, axis=0, keepdims=True)
    shifted = values - center
    inv_std = lax.rsqrt(jnp.mean(shifted * shifted, axis=0, keepdims=True) + EPSILON)
    return shifted * inv_std, inv_std


def tile_norm_grad(upstream, scaled, inv_std):
    first = jnp.mean(upstream, axis=0, keepdims=True)
    second = jnp.mean(upstream * scaled, axis=0, keepdims=True)
    return inv_std * (upstream - first - scaled * second)


def norm_tiles(spread_ref, gain_ref, normed_ref):
    gain = column(gain_ref)
    tiles = spread_ref.shape[0] // LANES
    for t in range(tiles):
        at = slice(t * LANES, (t + 1) * LANES)
        scaled, _ = tile_norm(spread_ref[at, :].T)
        normed_ref[:, at] = (scaled * gain).astype(BF16)


def gap(shape):
    return lax.broadcasted_iota(jnp.int32, shape, 1) % SLOT >= SLOT - PIECE


def pack_tiles(tiles):
    free = gap(tiles[0].shape)
    rows = []
    for t in range(9):
        moved = pltpu.roll(tiles[9 + t // 3], SLOT - PIECE - PIECE * (t % 3), 1)
        rows.append(jnp.where(free, moved, tiles[t]))
    return rows


def unpack_tiles(rows):
    free = gap(rows[0].shape)
    place = lax.broadcasted_iota(jnp.int32, rows[0].shape, 1) % SLOT // PIECE
    tiles = [jnp.where(free, 0.0, row) for row in rows]
    for m in range(3):
        tile = jnp.zeros_like(rows[0])
        for p in range(3):
            moved = pltpu.roll(rows[3 * m + p], LANES - (SLOT - PIECE) + PIECE * p, 1)
            tile = jnp.where(place == p, moved, tile)
        tiles.append(tile)
    return tiles


def device_rows(chunk_ref, depth, row):
    return chunk_ref[pl.ds(row, chunk_ref.shape[0] // depth, stride=depth), :]


def put_device_rows(chunk_ref, depth, row, values):
    chunk_ref[pl.ds(row, chunk_ref.shape[0] // depth, stride=depth), :] = values


def group_rows(depth, lo, col, row):
    return pl.ds(depth * (16 * col + lo) + row, 8, stride=2 * depth)


def plane_rows(na, lo, t):
    return slice(8 * (na * lo + 2 * t), 8 * (na * lo + 2 * t) + 16)


def plane_tile(even, odd):
    low = low_half(even.shape)
    upper = jnp.where(low, even, swap_halves(odd))
    lower = jnp.where(low, swap_halves(even), odd)
    return jnp.concatenate([upper, lower], axis=0)


def chunk_tiles(rows):
    upper, lower = rows[0:8], rows[8:16]
    low = low_half(upper.shape)
    return jnp.where(low, upper, swap_halves(lower)), jnp.where(low, swap_halves(upper), lower)


def token_order(na, plane):
    row = lax.broadcasted_iota(jnp.int32, (16 * 2 * na, plane), 0)
    token = lax.broadcasted_iota(jnp.int32, (16 * 2 * na, plane), 1)
    place = row // 8
    core = (place >= 2 * na).astype(jnp.int32)
    place = place - 2 * na * core
    lo = (place >= na).astype(jnp.int32)
    a = place - na * lo
    return (token == SLOT * (row % 8) + na * (2 * lo + core) + a).astype(F32).astype(BF16)


def sides_kernel(
    valid_hbm, acts_hbm, gain_hbm, weight_hbm, out_ref, mask_ref,
    valid_ref, acts_ref, gain_ref, weight_ref, spread_ref, normed_ref, chunk_ref, sems,
):
    na, nb, _ = acts_hbm.shape
    tiles = na // 2
    hidden = weight_hbm.shape[0]
    copies = [
        pltpu.make_async_copy(valid_hbm, valid_ref, sems.at[0]),
        pltpu.make_async_copy(acts_hbm, acts_ref, sems.at[1]),
        pltpu.make_async_copy(gain_hbm, gain_ref, sems.at[2]),
        pltpu.make_async_copy(weight_hbm, weight_ref, sems.at[3]),
    ]
    for copy in copies:
        copy.start()
    copies[0].wait()
    mask = masks(valid_ref, na, nb)
    for t in range(tiles):
        mask_ref[:, t * LANES : (t + 1) * LANES] = mask[t]
    copies[1].wait()
    spread(acts_ref, spread_ref)
    copies[2].wait()
    norm_tiles(spread_ref, gain_ref, normed_ref)
    copies[3].wait()
    projected = matmul(weight_ref[:, 0 : 4 * hidden], normed_ref[...], TN)
    found = []
    for side in range(2):
        base = 2 * side * hidden
        for t in range(tiles):
            at = slice(t * LANES, (t + 1) * LANES)
            gate = jax.nn.sigmoid(projected[base : base + hidden, at])
            value = projected[base + hidden : base + 2 * hidden, at]
            found.append(gate * value * mask[t])
    for t, row in enumerate(pack_tiles(found)):
        put_device_rows(chunk_ref, SIDE_ROWS, t, row)
    put_device_rows(chunk_ref, SIDE_ROWS, 9, jnp.zeros((hidden, LANES), F32))
    out_ref[...] = chunk_ref[...].astype(BF16)


def ready_kernel(
    acts_hbm, gain_hbm, weight_hbm, cotangent_hbm, mask_hbm, out_weight_hbm, out_gain_hbm,
    normed_ref, back_norm_ref, gate_mask_ref, gate_coef_ref, coef_ref,
    acts_ref, gain_ref, weight_ref, cotangent_ref, mask_ref, out_weight_ref, out_gain_ref,
    spread_ref, back_out_ref, sems,
):
    na = acts_ref.shape[0]
    tiles = na // 2
    hidden = out_weight_ref.shape[0]
    copies = [
        pltpu.make_async_copy(acts_hbm, acts_ref, sems.at[0]),
        pltpu.make_async_copy(gain_hbm, gain_ref, sems.at[1]),
        pltpu.make_async_copy(weight_hbm, weight_ref, sems.at[2]),
        pltpu.make_async_copy(cotangent_hbm, cotangent_ref, sems.at[3]),
        pltpu.make_async_copy(mask_hbm, mask_ref, sems.at[4]),
        pltpu.make_async_copy(out_weight_hbm, out_weight_ref, sems.at[5]),
        pltpu.make_async_copy(out_gain_hbm, out_gain_ref, sems.at[6]),
    ]
    for copy in copies:
        copy.start()
    for copy in copies:
        copy.wait()
    spread(acts_ref, spread_ref)
    norm_tiles(spread_ref, gain_ref, normed_ref)
    spread(cotangent_ref, spread_ref)
    projected = matmul(weight_ref[...], normed_ref[...], TN)
    for t in range(tiles):
        at = slice(t * LANES, (t + 1) * LANES)
        mask = mask_ref[:, at]
        gate = jax.nn.sigmoid(projected[4 * hidden :, at])
        gate_mask = gate * mask
        cotangent = spread_ref[at, :].T
        gate_mask_ref[:, at] = gate_mask
        gate_coef_ref[:, at] = cotangent * gate_mask * (1.0 - gate)
        back_out_ref[:, at] = (cotangent * gate_mask).astype(BF16)
        for base in (0, 2 * hidden):
            gate = jax.nn.sigmoid(projected[base : base + hidden, at])
            value = projected[base + hidden : base + 2 * hidden, at]
            coef_ref[base : base + hidden, at] = value * gate * (1.0 - gate) * mask
            coef_ref[base + hidden : base + 2 * hidden, at] = gate * mask
    out_gain = column(out_gain_ref)
    back_norm = matmul(out_weight_ref[...], back_out_ref[...])
    for t in range(tiles):
        at = slice(t * LANES, (t + 1) * LANES)
        back_norm_ref[:, at] = back_norm[:, at] * out_gain
    back_norm_ref[:, tiles * LANES : (tiles + 1) * LANES] = out_gain
    back_norm_ref[:, (tiles + 1) * LANES :] = out_weight_ref[...].astype(F32)


def order_kernel(na, order_ref):
    order_ref[...] = token_order(na, order_ref.shape[1])


def my_rows(ref):
    half = ref.shape[-2] // 2
    return pl.ds(pl.multiple_of(lax.axis_index("core") * half, half), half)


def tri_kernel(
    na, mine_ref, theirs_ref, order_ref, tri_ref, left_ref, right_ref, chunk_ref, tri_chunk_ref
):
    tiles = na // 2
    core = lax.axis_index("core")
    chunk_ref[core] = mine_ref[...].astype(F32)
    chunk_ref[1 - core] = theirs_ref[...].astype(F32)
    half = left_ref.shape[0] // 2
    for side in range(2):
        for pair in range(4):
            at = slice(pair * LANES, (pair + 1) * LANES)
            for lo in range(2):
                even, odd = [
                    unpack_tiles(
                        [chunk_ref[side, group_rows(SIDE_ROWS, lo, col, t), :] for t in range(9)]
                    )
                    for col in (2 * pair, 2 * pair + 1)
                ]
                for t in range(tiles):
                    rows = plane_rows(na, lo, t)
                    rows = slice(side * half + rows.start, side * half + rows.stop)
                    left_ref[rows, at] = plane_tile(even[t], odd[t]).astype(BF16)
                    right_ref[rows, at] = plane_tile(even[tiles + t], odd[tiles + t]).astype(BF16)
    tri = matmul(left_ref[my_rows(left_ref), :], right_ref[...], NT).astype(BF16)
    tri = matmul(tri, order_ref[...])
    for pair in range(4):
        for lo in range(2):
            for t in range(tiles):
                both = chunk_tiles(tri[plane_rows(na, lo, t), pair * LANES : (pair + 1) * LANES])
                for side in range(2):
                    tri_chunk_ref[group_rows(TRI_ROWS, lo, 2 * pair + side, t), :] = both[side]
    tri_ref[...] = tri_chunk_ref[...].astype(BF16)


def middle_kernel(
    tri_ref, normed_ref, back_norm_ref, gate_coef_ref,
    back_ref, gate_ref, out_proj_ref,
    tri_chunk_ref, scaled_ref, normed_out_ref,
):
    tiles = normed_ref.shape[1] // LANES
    tri_chunk_ref[...] = tri_ref[...].astype(F32)
    out_gain = back_norm_ref[:, tiles * LANES : (tiles + 1) * LANES]
    out_weight = back_norm_ref[:, (tiles + 1) * LANES :].astype(BF16)
    inv_out = []
    for t in range(tiles):
        at = slice(t * LANES, (t + 1) * LANES)
        scaled, inv = tile_norm(device_rows(tri_chunk_ref, TRI_ROWS, t))
        inv_out.append(inv)
        scaled_ref[:, at] = scaled
        normed_out_ref[:, at] = (scaled * out_gain).astype(BF16)
    out_proj = matmul(out_weight, normed_out_ref[...], TN)
    out_proj_ref[...] = out_proj
    gate_ref[...] = (out_proj * gate_coef_ref[...]).astype(BF16)
    term = matmul(normed_ref[...], gate_ref[...], NT)
    free = gap(term.shape)
    for t in range(tiles):
        at = slice(t * LANES, (t + 1) * LANES)
        row = tile_norm_grad(back_norm_ref[:, at], scaled_ref[:, at], inv_out[t])
        if t < 4:
            moved = pltpu.roll(term, SLOT - PIECE - PIECE * t, 1) if t < 3 else term
            row = jnp.where(free, moved, row)
        put_device_rows(tri_chunk_ref, TRI_ROWS, t, row)
    back_ref[...] = tri_chunk_ref[...].astype(BF16)


def update_kernel(gate_mask_ref, out_proj_ref, update_ref):
    for t in range(update_ref.shape[0] // 2):
        at = slice(t * LANES, (t + 1) * LANES)
        store_pairs(update_ref, t, gate_mask_ref[:, at] * out_proj_ref[:, at])


def back_kernel(
    na, mine_ref, theirs_ref, left_ref, right_ref, order_ref, out_ref,
    back_chunk_ref, chunk_ref, back_ref, turned_ref, side_ref,
):
    tiles = na // 2
    core = lax.axis_index("core")
    back_chunk_ref[core] = mine_ref[...].astype(F32)
    back_chunk_ref[1 - core] = theirs_ref[...].astype(F32)
    half = back_ref.shape[0] // 2
    free = gap((8, LANES))
    for side in range(2):
        for pair in range(4):
            for lo in range(2):
                for t in range(tiles):
                    even, odd = [
                        jnp.where(free, 0.0, back_chunk_ref[side, group_rows(TRI_ROWS, lo, col, t), :])
                        for col in (2 * pair, 2 * pair + 1)
                    ]
                    rows = plane_rows(na, lo, t)
                    rows = slice(side * half + rows.start, side * half + rows.stop)
                    back_ref[rows, pair * LANES : (pair + 1) * LANES] = plane_tile(even, odd).astype(BF16)
    turned_ref[...] = matmul(back_ref[...], order_ref[...], NT).astype(BF16)
    back_left = matmul(turned_ref[my_rows(turned_ref), :], right_ref[...])
    side_ref[...] = matmul(turned_ref[...], left_ref[...], TN)
    back_right = side_ref[my_rows(side_ref), :]

    place = lax.broadcasted_iota(jnp.int32, (8, LANES), 1) % SLOT // PIECE
    total = jnp.zeros((8, LANES), F32)
    for t in range(4):
        rows = jnp.zeros((8, LANES), F32)
        for side in range(2):
            for m in range(back_chunk_ref.shape[1] // (8 * TRI_ROWS)):
                rows += back_chunk_ref[side, pl.ds(8 * TRI_ROWS * m + t, 8, stride=TRI_ROWS), :]
        rows = jnp.sum(rows, axis=0, keepdims=True)
        rows = jnp.broadcast_to(rows, (8, LANES))
        if t < 3:
            rows = pltpu.roll(rows, LANES - (SLOT - PIECE) + PIECE * t, 1)
        total = jnp.where(place == t, rows, total)
    total = total / (4 * 8 * na)
    for m in range(chunk_ref.shape[0] // (8 * SIDE_ROWS)):
        chunk_ref[pl.ds(8 * SIDE_ROWS * m + 9, 8, stride=SIDE_ROWS), :] = total

    for pair in range(4):
        at = slice(pair * LANES, (pair + 1) * LANES)
        for lo in range(2):
            found = [
                chunk_tiles(product[plane_rows(na, lo, t), at])
                for product in (back_left, back_right)
                for t in range(tiles)
            ]
            for side in range(2):
                for t, row in enumerate(pack_tiles([both[side] for both in found])):
                    chunk_ref[group_rows(SIDE_ROWS, lo, 2 * pair + side, t), :] = row
    out_ref[...] = chunk_ref[...].astype(BF16)


def weight_kernel(
    back_ref, normed_ref, coef_ref, gate_ref, term_ref, back_proj_ref, gate_total_ref,
    chunk_ref, term_chunk_ref,
):
    tiles = normed_ref.shape[1] // LANES
    hidden = normed_ref.shape[0]
    chunk_ref[...] = back_ref[...].astype(F32)
    gate_total_ref[...] = device_rows(chunk_ref, SIDE_ROWS, 9)
    back_proj_ref[4 * hidden :, :] = gate_ref[...]
    upstreams = unpack_tiles([device_rows(chunk_ref, SIDE_ROWS, t) for t in range(9)])
    for side in range(2):
        for t in range(tiles):
            at = slice(t * LANES, (t + 1) * LANES)
            for base in (2 * side * hidden, (2 * side + 1) * hidden):
                rows = slice(base, base + hidden)
                back_proj_ref[rows, at] = (upstreams[tiles * side + t] * coef_ref[rows, at]).astype(BF16)
    term = matmul(normed_ref[...], back_proj_ref[0 : 4 * hidden, :], NT)
    for t in range(4):
        for m in range(hidden // 8):
            term_chunk_ref[weight_rows(m, t), :] = term[8 * m : 8 * m + 8, t * LANES : (t + 1) * LANES]
    term_ref[...] = term_chunk_ref[...].astype(BF16)


def weight_rows(chip, t):
    return pl.ds(2 * (16 * chip + 8 * (t // 2)) + t % 2, 8, stride=2)


def sum_kernel(full_len, parts_ref, out_ref):
    total = jnp.zeros((16, LANES), F32)
    for m in range(parts_ref.shape[0] // 16):
        total += parts_ref[16 * m : 16 * m + 16, :].astype(F32)
    total = total[0:8] + total[8:16]
    total = total + pltpu.roll(total, 4, 0)
    total = total + pltpu.roll(total, 2, 0)
    total = total / full_len
    total = jnp.concatenate([total, total], axis=0).astype(BF16)
    for m in range(out_ref.shape[0] // 16):
        out_ref[16 * m : 16 * m + 16, :] = total


def grad_weight_kernel(mine_ref, theirs_ref, gate_total_ref, out_ref, chunk_ref):
    core = lax.axis_index("core")
    chunk_ref[core] = mine_ref[...].astype(F32)
    chunk_ref[1 - core] = theirs_ref[...].astype(F32)
    for t in range(4):
        out_ref[:, t * LANES : (t + 1) * LANES] = chunk_ref[
            t // 2, pl.ds(t % 2, out_ref.shape[0], stride=2), :
        ]
    out_ref[:, 4 * LANES :] = gate_total_ref[...]


def pair_kernel(acts_ref, gain_ref, weight_ref, back_proj_ref, grad_pair_ref, spread_ref):
    na, nb, _ = acts_ref.shape
    spread(acts_ref, spread_ref)
    gain = column(gain_ref)
    back_normed = matmul(weight_ref[...], back_proj_ref[...])
    for t in range(na // 2):
        at = slice(t * LANES, (t + 1) * LANES)
        scaled, inv = tile_norm(spread_ref[at, :].T)
        store_pairs(grad_pair_ref, t, tile_norm_grad(back_normed[:, at] * gain, scaled, inv))


def local_call(body, outs, scratch, flops, inputs, space=pltpu.VMEM, limit=VMEM_LIMIT):
    return pl.pallas_call(
        body,
        out_shape=outs,
        in_specs=[pl.BlockSpec(memory_space=space)] * inputs,
        out_specs=jax.tree.map(lambda _: pl.BlockSpec(memory_space=pltpu.VMEM), outs),
        scratch_shapes=scratch,
        compiler_params=pltpu.CompilerParams(vmem_limit_bytes=limit),
        cost_estimate=pl.CostEstimate(flops=flops, bytes_accessed=2_000_000, transcendentals=0),
    )


def exchange(chunks, depth, axes):
    devices = chunks.shape[0] // depth
    split = chunks.reshape(devices, depth // 2, 2, chunks.shape[1])
    return lax.all_to_all(split, axes, 0, 0, tiled=True).reshape(chunks.shape)


def other_core(values):
    return lax.ppermute(values, "core", [(0, 1), (1, 0)])


def array(shape, dtype=BF16):
    return jax.ShapeDtypeStruct(shape, dtype)


def per_device(pair_acts, token_valid, norm_gain, proj_weight, out_gain, out_weight, out_cotangent):
    na, _, channels = pair_acts.shape
    hidden = out_weight.shape[0]
    width_all = proj_weight.shape[1]
    full_len = token_valid.shape[0]
    lanes = na // 2 * LANES
    plane = (full_len, 8 * SLOT)
    sides_chunk = (hidden * SIDE_ROWS, LANES)
    tri_chunk = (hidden * TRI_ROWS, LANES)
    term_chunk = (4 * hidden, LANES)
    gain = norm_gain.reshape(1, channels)
    out_gain = out_gain.reshape(1, hidden)
    spread_scratch = pltpu.VMEM((lanes, channels), F32)

    sides, mask = local_call(
        sides_kernel,
        (array(sides_chunk), array((1, lanes), F32)),
        [
            pltpu.SMEM(token_valid.shape, jnp.int32),
            pltpu.VMEM(pair_acts.shape, BF16),
            pltpu.VMEM(gain.shape, F32),
            pltpu.VMEM(proj_weight.shape, BF16),
            spread_scratch,
            pltpu.VMEM((channels, lanes), BF16),
            pltpu.VMEM(sides_chunk, F32),
            pltpu.SemaphoreType.DMA((4,)),
        ],
        100_000_000,
        4,
        pltpu.HBM,
        WHOLE_VMEM,
    )(token_valid, pair_acts, gain, proj_weight)
    mine = exchange(sides, SIDE_ROWS, CHANNEL_AXES)
    order = local_call(functools.partial(order_kernel, na), array(plane), [], 1_000_000_000, 0)()
    normed, back_norm, gate_mask, gate_coef, coef = local_call(
        ready_kernel,
        (
            array((channels, lanes)),
            array((hidden, lanes + 2 * LANES), F32),
            array((channels, lanes), F32),
            array((channels, lanes), F32),
            array((4 * hidden, lanes), F32),
        ),
        [
            pltpu.VMEM(pair_acts.shape, BF16),
            pltpu.VMEM(gain.shape, F32),
            pltpu.VMEM(proj_weight.shape, BF16),
            pltpu.VMEM(out_cotangent.shape, BF16),
            pltpu.VMEM(mask.shape, F32),
            pltpu.VMEM(out_weight.shape, BF16),
            pltpu.VMEM(out_gain.shape, F32),
            spread_scratch,
            pltpu.VMEM((channels, lanes), BF16),
            pltpu.SemaphoreType.DMA((7,)),
        ],
        1_000_000_000,
        7,
        pltpu.HBM,
        READY_VMEM,
    )(pair_acts, gain, proj_weight, out_cotangent, mask, out_weight, out_gain)
    mine, normed, order = lax.optimization_barrier((mine, normed, order))
    tri, left, right = local_call(
        functools.partial(tri_kernel, na),
        (array(tri_chunk), array(plane), array(plane)),
        [pltpu.VMEM((2,) + sides_chunk, F32), pltpu.VMEM(tri_chunk, F32)],
        300_000_000,
        3,
    )(mine, other_core(mine), order)
    tri = exchange(tri, TRI_ROWS, CHANNEL_AXES)
    back, gate, out_proj = local_call(
        middle_kernel,
        (array(tri_chunk), array((channels, lanes)), array((channels, lanes), F32)),
        [
            pltpu.VMEM(tri_chunk, F32),
            pltpu.VMEM((hidden, lanes), F32),
            pltpu.VMEM((hidden, lanes), BF16),
        ],
        100_000_000,
        4,
    )(tri, normed, back_norm, gate_coef)
    back = exchange(back, TRI_ROWS, CHANNEL_AXES)
    update = local_call(update_kernel, array(pair_acts.shape), [], 1_000_000_000, 2)(
        gate_mask, out_proj
    )
    back_sides = local_call(
        functools.partial(back_kernel, na),
        array(sides_chunk),
        [
            pltpu.VMEM((2,) + tri_chunk, F32),
            pltpu.VMEM(sides_chunk, F32),
            pltpu.VMEM(plane, BF16),
            pltpu.VMEM((full_len, full_len), BF16),
            pltpu.VMEM(plane, F32),
        ],
        300_000_000,
        5,
    )(back, other_core(back), left, right, order)
    back_sides = exchange(back_sides, SIDE_ROWS, CHANNEL_AXES)
    term, back_proj, gate_total = local_call(
        weight_kernel,
        (array(term_chunk), array((width_all, lanes)), array((channels, channels), F32)),
        [pltpu.VMEM(sides_chunk, F32), pltpu.VMEM(term_chunk, F32)],
        200_000_000,
        4,
    )(back_sides, normed, coef, gate)
    grad_pair = local_call(
        pair_kernel, array(pair_acts.shape), [spread_scratch], 1_000_000_000, 4
    )(pair_acts, gain, proj_weight, back_proj)
    parts = exchange(term, 2, ALL_AXES)
    sums = local_call(
        functools.partial(sum_kernel, full_len), array((2 * hidden, LANES)), [], 100_000, 1
    )(parts)
    sums = exchange(sums, 2, ("chip", "col"))
    grad_weight = local_call(
        grad_weight_kernel,
        array((channels, width_all), F32),
        [pltpu.VMEM((2, 2 * hidden, LANES), F32)],
        100_000,
        3,
    )(sums, other_core(sums), gate_total)
    return update, grad_pair, grad_weight


def solution(mesh):
    rows, cols = mesh.devices.shape
    split = Mesh(mesh.devices.reshape(rows // 2, 2, cols), ("chip", "core", "col"))
    pairs = P(("chip", "core"), "col", None)
    return jax.shard_map(
        per_device,
        mesh=split,
        in_specs=(pairs, P(), P(), P(), P(), P(), pairs),
        out_specs=(pairs, pairs, P()),
        check_vma=False,
    )
```

```python
import functools

import jax
import jax.numpy as jnp
from jax import lax
from jax.experimental import pallas as pl
from jax.experimental.pallas import tpu as pltpu
from jax.sharding import Mesh
from jax.sharding import PartitionSpec as P

EPSILON = 1e-05
BF16 = jnp.bfloat16
F32 = jnp.float32
ALL_AXES = ("chip", "core", "col")
CHANNEL_AXES = ("col", "chip")
LANES = 128
SLOT = 64
PIECE = 16
SIDE_ROWS = 10
TRI_ROWS = 6
VMEM_LIMIT = 48 * 1024 * 1024
WHOLE_VMEM = 64 * 1024 * 1024 - 65536
READY_VMEM = 62 * 1024 * 1024

NT = (((1,), (1,)), ((), ()))
NN = (((1,), (0,)), ((), ()))
TN = (((0,), (0,)), ((), ()))


def matmul(lhs, rhs, dims=NN):
    return lax.dot_general(lhs, rhs, dims, preferred_element_type=F32)


def column(row_ref):
    return jnp.broadcast_to(row_ref[...], (LANES, LANES)).T


def swap_halves(values):
    return pltpu.roll(values, SLOT, 1)


def low_half(shape):
    return lax.broadcasted_iota(jnp.int32, shape, 1) < SLOT


def spread(pairs_ref, spread_ref):
    na, nb, channels = pairs_ref.shape
    for a in range(na):
        spread_ref[a * SLOT : a * SLOT + nb, :] = pairs_ref[a].astype(F32)
        spread_ref[a * SLOT + nb : (a + 1) * SLOT, :] = jnp.zeros((SLOT - nb, channels), F32)


def store_pairs(out_ref, t, values):
    nb = out_ref.shape[1]
    turned = values.T
    out_ref[2 * t] = turned[0:nb].astype(out_ref.dtype)
    out_ref[2 * t + 1] = turned[SLOT : SLOT + nb].astype(out_ref.dtype)


def masks(valid_ref, na, nb):
    lane = lax.broadcasted_iota(jnp.int32, (1, LANES), 1)
    place = lane % SLOT
    first_row = (2 * lax.axis_index("chip") + lax.axis_index("core")) * na
    first_col = lax.axis_index("col") * nb
    cols = jnp.zeros((1, LANES), jnp.int32)
    for b in range(nb):
        cols = jnp.where(place == b, valid_ref[first_col + b], cols)
    found = []
    for t in range(na // 2):
        rows = jnp.where(lane < SLOT, valid_ref[first_row + 2 * t], valid_ref[first_row + 2 * t + 1])
        found.append((rows * cols).astype(F32))
    return found


def tile_norm(values):
    center = jnp.mean(values, axis=0, keepdims=True)
    shifted = values - center
    inv_std = lax.rsqrt(jnp.mean(shifted * shifted, axis=0, keepdims=True) + EPSILON)
    return shifted * inv_std, inv_std


def tile_norm_grad(upstream, scaled, inv_std):
    first = jnp.mean(upstream, axis=0, keepdims=True)
    second = jnp.mean(upstream * scaled, axis=0, keepdims=True)
    return inv_std * (upstream - first - scaled * second)


def norm_tiles(spread_ref, gain_ref, normed_ref):
    gain = column(gain_ref)
    tiles = spread_ref.shape[0] // LANES
    for t in range(tiles):
        at = slice(t * LANES, (t + 1) * LANES)
        scaled, _ = tile_norm(spread_ref[at, :].T)
        normed_ref[:, at] = (scaled * gain).astype(BF16)


def gap(shape):
    return lax.broadcasted_iota(jnp.int32, shape, 1) % SLOT >= SLOT - PIECE


def pack_tiles(tiles):
    free = gap(tiles[0].shape)
    rows = []
    for t in range(9):
        moved = pltpu.roll(tiles[9 + t // 3], SLOT - PIECE - PIECE * (t % 3), 1)
        rows.append(jnp.where(free, moved, tiles[t]))
    return rows


def unpack_tiles(rows):
    free = gap(rows[0].shape)
    place = lax.broadcasted_iota(jnp.int32, rows[0].shape, 1) % SLOT // PIECE
    tiles = [jnp.where(free, 0.0, row) for row in rows]
    for m in range(3):
        tile = jnp.zeros_like(rows[0])
        for p in range(3):
            moved = pltpu.roll(rows[3 * m + p], LANES - (SLOT - PIECE) + PIECE * p, 1)
            tile = jnp.where(place == p, moved, tile)
        tiles.append(tile)
    return tiles


def device_rows(chunk_ref, depth, row):
    return chunk_ref[pl.ds(row, chunk_ref.shape[0] // depth, stride=depth), :]


def put_device_rows(chunk_ref, depth, row, values):
    chunk_ref[pl.ds(row, chunk_ref.shape[0] // depth, stride=depth), :] = values


def group_rows(depth, lo, col, row):
    return pl.ds(depth * (16 * col + lo) + row, 8, stride=2 * depth)


def plane_rows(na, lo, t):
    return slice(8 * (na * lo + 2 * t), 8 * (na * lo + 2 * t) + 16)


def plane_tile(even, odd):
    low = low_half(even.shape)
    upper = jnp.where(low, even, swap_halves(odd))
    lower = jnp.where(low, swap_halves(even), odd)
    return jnp.concatenate([upper, lower], axis=0)


def chunk_tiles(rows):
    upper, lower = rows[0:8], rows[8:16]
    low = low_half(upper.shape)
    return jnp.where(low, upper, swap_halves(lower)), jnp.where(low, swap_halves(upper), lower)


def token_order(na, plane):
    row = lax.broadcasted_iota(jnp.int32, (16 * 2 * na, plane), 0)
    token = lax.broadcasted_iota(jnp.int32, (16 * 2 * na, plane), 1)
    place = row // 8
    theirs = (place >= 2 * na).astype(jnp.int32)
    place = place - 2 * na * theirs
    core = lax.axis_index("core")
    core = core + theirs * (1 - 2 * core)
    lo = (place >= na).astype(jnp.int32)
    a = place - na * lo
    return (token == SLOT * (row % 8) + na * (2 * lo + core) + a).astype(F32).astype(BF16)


def sides_kernel(
    valid_hbm, acts_hbm, gain_hbm, weight_hbm, out_ref, mask_ref,
    valid_ref, acts_ref, gain_ref, weight_ref, spread_ref, normed_ref, chunk_ref, sems,
):
    na, nb, _ = acts_hbm.shape
    tiles = na // 2
    hidden = weight_hbm.shape[0]
    copies = [
        pltpu.make_async_copy(valid_hbm, valid_ref, sems.at[0]),
        pltpu.make_async_copy(acts_hbm, acts_ref, sems.at[1]),
        pltpu.make_async_copy(gain_hbm, gain_ref, sems.at[2]),
        pltpu.make_async_copy(weight_hbm, weight_ref, sems.at[3]),
    ]
    for copy in copies:
        copy.start()
    copies[0].wait()
    mask = masks(valid_ref, na, nb)
    for t in range(tiles):
        mask_ref[:, t * LANES : (t + 1) * LANES] = mask[t]
    copies[1].wait()
    spread(acts_ref, spread_ref)
    copies[2].wait()
    norm_tiles(spread_ref, gain_ref, normed_ref)
    copies[3].wait()
    projected = matmul(weight_ref[:, 0 : 4 * hidden], normed_ref[...], TN)
    found = []
    for side in range(2):
        base = 2 * side * hidden
        for t in range(tiles):
            at = slice(t * LANES, (t + 1) * LANES)
            gate = jax.nn.sigmoid(projected[base : base + hidden, at])
            value = projected[base + hidden : base + 2 * hidden, at]
            found.append(gate * value * mask[t])
    for t, row in enumerate(pack_tiles(found)):
        put_device_rows(chunk_ref, SIDE_ROWS, t, row)
    put_device_rows(chunk_ref, SIDE_ROWS, 9, jnp.zeros((hidden, LANES), F32))
    out_ref[...] = chunk_ref[...].astype(BF16)


def ready_kernel(
    acts_hbm, gain_hbm, weight_hbm, cotangent_hbm, mask_hbm, out_weight_hbm, out_gain_hbm,
    normed_ref, back_norm_ref, gate_mask_ref, gate_coef_ref, coef_ref,
    acts_ref, gain_ref, weight_ref, cotangent_ref, mask_ref, out_weight_ref, out_gain_ref,
    spread_ref, back_out_ref, sems,
):
    na = acts_ref.shape[0]
    tiles = na // 2
    hidden = out_weight_ref.shape[0]
    copies = [
        pltpu.make_async_copy(acts_hbm, acts_ref, sems.at[0]),
        pltpu.make_async_copy(gain_hbm, gain_ref, sems.at[1]),
        pltpu.make_async_copy(weight_hbm, weight_ref, sems.at[2]),
        pltpu.make_async_copy(cotangent_hbm, cotangent_ref, sems.at[3]),
        pltpu.make_async_copy(mask_hbm, mask_ref, sems.at[4]),
        pltpu.make_async_copy(out_weight_hbm, out_weight_ref, sems.at[5]),
        pltpu.make_async_copy(out_gain_hbm, out_gain_ref, sems.at[6]),
    ]
    for copy in copies:
        copy.start()
    for copy in copies:
        copy.wait()
    spread(acts_ref, spread_ref)
    norm_tiles(spread_ref, gain_ref, normed_ref)
    spread(cotangent_ref, spread_ref)
    projected = matmul(weight_ref[...], normed_ref[...], TN)
    for t in range(tiles):
        at = slice(t * LANES, (t + 1) * LANES)
        mask = mask_ref[:, at]
        gate = jax.nn.sigmoid(projected[4 * hidden :, at])
        gate_mask = gate * mask
        cotangent = spread_ref[at, :].T
        gate_mask_ref[:, at] = gate_mask
        gate_coef_ref[:, at] = cotangent * gate_mask * (1.0 - gate)
        back_out_ref[:, at] = (cotangent * gate_mask).astype(BF16)
        for base in (0, 2 * hidden):
            gate = jax.nn.sigmoid(projected[base : base + hidden, at])
            value = projected[base + hidden : base + 2 * hidden, at]
            coef_ref[base : base + hidden, at] = value * gate * (1.0 - gate) * mask
            coef_ref[base + hidden : base + 2 * hidden, at] = gate * mask
    out_gain = column(out_gain_ref)
    back_norm = matmul(out_weight_ref[...], back_out_ref[...])
    for t in range(tiles):
        at = slice(t * LANES, (t + 1) * LANES)
        back_norm_ref[:, at] = back_norm[:, at] * out_gain
    back_norm_ref[:, tiles * LANES : (tiles + 1) * LANES] = out_gain
    back_norm_ref[:, (tiles + 1) * LANES :] = out_weight_ref[...].astype(F32)


def order_kernel(na, order_ref):
    order_ref[...] = token_order(na, order_ref.shape[1])


def side_planes(na, chunk_ref, left_ref, right_ref, first):
    tiles = na // 2
    for pair in range(4):
        at = slice(pair * LANES, (pair + 1) * LANES)
        for lo in range(2):
            even, odd = [
                unpack_tiles([chunk_ref[group_rows(SIDE_ROWS, lo, col, t), :] for t in range(9)])
                for col in (2 * pair, 2 * pair + 1)
            ]
            for t in range(tiles):
                rows = plane_rows(na, lo, t)
                rows = slice(first + rows.start, first + rows.stop)
                left_ref[rows, at] = plane_tile(even[t], odd[t]).astype(BF16)
                right_ref[rows, at] = plane_tile(even[tiles + t], odd[tiles + t]).astype(BF16)


def own_sides_kernel(na, mine_ref, left_ref, right_ref, chunk_ref):
    chunk_ref[...] = mine_ref[...].astype(F32)
    side_planes(na, chunk_ref, left_ref, right_ref, 0)


def tri_kernel(
    na, theirs_ref, left_mine_ref, right_mine_ref, order_ref, tri_ref, left_ref, right_ref,
    chunk_ref, tri_chunk_ref,
):
    tiles = na // 2
    half = left_mine_ref.shape[0]
    chunk_ref[...] = theirs_ref[...].astype(F32)
    left_ref[0:half, :] = left_mine_ref[...]
    right_ref[0:half, :] = right_mine_ref[...]
    side_planes(na, chunk_ref, left_ref, right_ref, half)
    tri = matmul(left_mine_ref[...], right_ref[...], NT).astype(BF16)
    tri = matmul(tri, order_ref[...])
    for pair in range(4):
        for lo in range(2):
            for t in range(tiles):
                both = chunk_tiles(tri[plane_rows(na, lo, t), pair * LANES : (pair + 1) * LANES])
                for side in range(2):
                    tri_chunk_ref[group_rows(TRI_ROWS, lo, 2 * pair + side, t), :] = both[side]
    tri_ref[...] = tri_chunk_ref[...].astype(BF16)


def middle_kernel(
    tri_ref, normed_ref, back_norm_ref, gate_coef_ref,
    back_ref, gate_ref, out_proj_ref,
    tri_chunk_ref, scaled_ref, normed_out_ref,
):
    tiles = normed_ref.shape[1] // LANES
    tri_chunk_ref[...] = tri_ref[...].astype(F32)
    out_gain = back_norm_ref[:, tiles * LANES : (tiles + 1) * LANES]
    out_weight = back_norm_ref[:, (tiles + 1) * LANES :].astype(BF16)
    inv_out = []
    for t in range(tiles):
        at = slice(t * LANES, (t + 1) * LANES)
        scaled, inv = tile_norm(device_rows(tri_chunk_ref, TRI_ROWS, t))
        inv_out.append(inv)
        scaled_ref[:, at] = scaled
        normed_out_ref[:, at] = (scaled * out_gain).astype(BF16)
    out_proj = matmul(out_weight, normed_out_ref[...], TN)
    out_proj_ref[...] = out_proj
    gate_ref[...] = (out_proj * gate_coef_ref[...]).astype(BF16)
    term = matmul(normed_ref[...], gate_ref[...], NT)
    free = gap(term.shape)
    for t in range(tiles):
        at = slice(t * LANES, (t + 1) * LANES)
        row = tile_norm_grad(back_norm_ref[:, at], scaled_ref[:, at], inv_out[t])
        if t < 4:
            moved = pltpu.roll(term, SLOT - PIECE - PIECE * t, 1) if t < 3 else term
            row = jnp.where(free, moved, row)
        put_device_rows(tri_chunk_ref, TRI_ROWS, t, row)
    back_ref[...] = tri_chunk_ref[...].astype(BF16)


def update_kernel(gate_mask_ref, out_proj_ref, update_ref):
    for t in range(update_ref.shape[0] // 2):
        at = slice(t * LANES, (t + 1) * LANES)
        store_pairs(update_ref, t, gate_mask_ref[:, at] * out_proj_ref[:, at])


def back_plane(na, chunk_ref, plane_ref):
    free = gap((8, LANES))
    for pair in range(4):
        for lo in range(2):
            for t in range(na // 2):
                even, odd = [
                    jnp.where(free, 0.0, chunk_ref[group_rows(TRI_ROWS, lo, col, t), :])
                    for col in (2 * pair, 2 * pair + 1)
                ]
                plane_ref[plane_rows(na, lo, t), pair * LANES : (pair + 1) * LANES] = plane_tile(
                    even, odd
                ).astype(BF16)


def gap_total(chunk_ref):
    place = lax.broadcasted_iota(jnp.int32, (8, LANES), 1) % SLOT // PIECE
    total = jnp.zeros((8, LANES), F32)
    for t in range(4):
        rows = jnp.zeros((8, LANES), F32)
        for m in range(chunk_ref.shape[0] // (8 * TRI_ROWS)):
            rows += chunk_ref[pl.ds(8 * TRI_ROWS * m + t, 8, stride=TRI_ROWS), :]
        rows = jnp.broadcast_to(jnp.sum(rows, axis=0, keepdims=True), (8, LANES))
        if t < 3:
            rows = pltpu.roll(rows, LANES - (SLOT - PIECE) + PIECE * t, 1)
        total = jnp.where(place == t, rows, total)
    return total


def own_back_kernel(
    na, mine_ref, right_ref, order_ref, turned_ref, back_left_ref, total_ref, chunk_ref, plane_ref
):
    chunk_ref[...] = mine_ref[...].astype(F32)
    back_plane(na, chunk_ref, plane_ref)
    turned_ref[...] = matmul(plane_ref[...], order_ref[...], NT).astype(BF16)
    back_left_ref[...] = matmul(turned_ref[...], right_ref[...])
    total_ref[...] = gap_total(chunk_ref)


def back_kernel(
    na, theirs_ref, turned_mine_ref, back_left_ref, total_ref, left_ref, order_ref, out_ref,
    back_chunk_ref, chunk_ref, plane_ref, turned_ref,
):
    tiles = na // 2
    half = turned_mine_ref.shape[0]
    back_chunk_ref[...] = theirs_ref[...].astype(F32)
    back_plane(na, back_chunk_ref, plane_ref)
    turned_ref[0:half, :] = turned_mine_ref[...]
    turned_ref[half:, :] = matmul(plane_ref[...], order_ref[...], NT).astype(BF16)
    back_right = matmul(turned_ref[:, 0:half], left_ref[...], TN)
    total = (total_ref[...] + gap_total(back_chunk_ref)) / (4 * 8 * na)
    for m in range(chunk_ref.shape[0] // (8 * SIDE_ROWS)):
        chunk_ref[pl.ds(8 * SIDE_ROWS * m + 9, 8, stride=SIDE_ROWS), :] = total
    for pair in range(4):
        at = slice(pair * LANES, (pair + 1) * LANES)
        for lo in range(2):
            found = [chunk_tiles(back_left_ref[plane_rows(na, lo, t), at]) for t in range(tiles)]
            found += [chunk_tiles(back_right[plane_rows(na, lo, t), at]) for t in range(tiles)]
            for side in range(2):
                for t, row in enumerate(pack_tiles([both[side] for both in found])):
                    chunk_ref[group_rows(SIDE_ROWS, lo, 2 * pair + side, t), :] = row
    out_ref[...] = chunk_ref[...].astype(BF16)


def weight_kernel(
    back_ref, normed_ref, coef_ref, gate_ref, term_ref, back_proj_ref, gate_total_ref,
    chunk_ref, term_chunk_ref,
):
    tiles = normed_ref.shape[1] // LANES
    hidden = normed_ref.shape[0]
    chunk_ref[...] = back_ref[...].astype(F32)
    gate_total_ref[...] = device_rows(chunk_ref, SIDE_ROWS, 9)
    back_proj_ref[4 * hidden :, :] = gate_ref[...]
    upstreams = unpack_tiles([device_rows(chunk_ref, SIDE_ROWS, t) for t in range(9)])
    for side in range(2):
        for t in range(tiles):
            at = slice(t * LANES, (t + 1) * LANES)
            for base in (2 * side * hidden, (2 * side + 1) * hidden):
                rows = slice(base, base + hidden)
                back_proj_ref[rows, at] = (upstreams[tiles * side + t] * coef_ref[rows, at]).astype(BF16)
    term = matmul(normed_ref[...], back_proj_ref[0 : 4 * hidden, :], NT)
    for t in range(4):
        for m in range(hidden // 8):
            term_chunk_ref[weight_rows(m, t), :] = term[8 * m : 8 * m + 8, t * LANES : (t + 1) * LANES]
    term_ref[...] = term_chunk_ref[...].astype(BF16)


def weight_rows(chip, t):
    return pl.ds(2 * (16 * chip + 8 * (t // 2)) + t % 2, 8, stride=2)


def sum_kernel(full_len, parts_ref, out_ref):
    total = jnp.zeros((16, LANES), F32)
    for m in range(parts_ref.shape[0] // 16):
        total += parts_ref[16 * m : 16 * m + 16, :].astype(F32)
    total = total[0:8] + total[8:16]
    total = total + pltpu.roll(total, 4, 0)
    total = total + pltpu.roll(total, 2, 0)
    total = total / full_len
    total = jnp.concatenate([total, total], axis=0).astype(BF16)
    for m in range(out_ref.shape[0] // 16):
        out_ref[16 * m : 16 * m + 16, :] = total


def grad_weight_kernel(sums_ref, gate_total_ref, out_ref, chunk_ref):
    chunk_ref[...] = sums_ref[...].astype(F32)
    for t in range(4):
        for m in range(out_ref.shape[0] // 8):
            out_ref[8 * m : 8 * m + 8, t * LANES : (t + 1) * LANES] = chunk_ref[weight_rows(m, t), :]
    out_ref[:, 4 * LANES :] = gate_total_ref[...]


def pair_kernel(acts_ref, gain_ref, weight_ref, back_proj_ref, grad_pair_ref, spread_ref):
    na, nb, _ = acts_ref.shape
    spread(acts_ref, spread_ref)
    gain = column(gain_ref)
    back_normed = matmul(weight_ref[...], back_proj_ref[...])
    for t in range(na // 2):
        at = slice(t * LANES, (t + 1) * LANES)
        scaled, inv = tile_norm(spread_ref[at, :].T)
        store_pairs(grad_pair_ref, t, tile_norm_grad(back_normed[:, at] * gain, scaled, inv))


def local_call(body, outs, scratch, flops, inputs, space=pltpu.VMEM, limit=VMEM_LIMIT):
    return pl.pallas_call(
        body,
        out_shape=outs,
        in_specs=[pl.BlockSpec(memory_space=space)] * inputs,
        out_specs=jax.tree.map(lambda _: pl.BlockSpec(memory_space=pltpu.VMEM), outs),
        scratch_shapes=scratch,
        compiler_params=pltpu.CompilerParams(vmem_limit_bytes=limit),
        cost_estimate=pl.CostEstimate(flops=flops, bytes_accessed=2_000_000, transcendentals=0),
    )


def exchange(chunks, depth, axes):
    devices = chunks.shape[0] // depth
    split = chunks.reshape(devices, depth // 2, 2, chunks.shape[1])
    return lax.all_to_all(split, axes, 0, 0, tiled=True).reshape(chunks.shape)


def other_core(values):
    return lax.ppermute(values, "core", [(0, 1), (1, 0)])


def array(shape, dtype=BF16):
    return jax.ShapeDtypeStruct(shape, dtype)


def per_device(pair_acts, token_valid, norm_gain, proj_weight, out_gain, out_weight, out_cotangent):
    na, _, channels = pair_acts.shape
    hidden = out_weight.shape[0]
    width_all = proj_weight.shape[1]
    full_len = token_valid.shape[0]
    lanes = na // 2 * LANES
    plane = (full_len, 8 * SLOT)
    sides_chunk = (hidden * SIDE_ROWS, LANES)
    tri_chunk = (hidden * TRI_ROWS, LANES)
    term_chunk = (4 * hidden, LANES)
    gain = norm_gain.reshape(1, channels)
    out_gain = out_gain.reshape(1, hidden)
    spread_scratch = pltpu.VMEM((lanes, channels), F32)

    sides, mask = local_call(
        sides_kernel,
        (array(sides_chunk), array((1, lanes), F32)),
        [
            pltpu.SMEM(token_valid.shape, jnp.int32),
            pltpu.VMEM(pair_acts.shape, BF16),
            pltpu.VMEM(gain.shape, F32),
            pltpu.VMEM(proj_weight.shape, BF16),
            spread_scratch,
            pltpu.VMEM((channels, lanes), BF16),
            pltpu.VMEM(sides_chunk, F32),
            pltpu.SemaphoreType.DMA((4,)),
        ],
        100_000_000,
        4,
        pltpu.HBM,
        WHOLE_VMEM,
    )(token_valid, pair_acts, gain, proj_weight)
    mine = exchange(sides, SIDE_ROWS, CHANNEL_AXES)
    order = local_call(functools.partial(order_kernel, na), array(plane), [], 1_000_000_000, 0)()
    normed, back_norm, gate_mask, gate_coef, coef = local_call(
        ready_kernel,
        (
            array((channels, lanes)),
            array((hidden, lanes + 2 * LANES), F32),
            array((channels, lanes), F32),
            array((channels, lanes), F32),
            array((4 * hidden, lanes), F32),
        ),
        [
            pltpu.VMEM(pair_acts.shape, BF16),
            pltpu.VMEM(gain.shape, F32),
            pltpu.VMEM(proj_weight.shape, BF16),
            pltpu.VMEM(out_cotangent.shape, BF16),
            pltpu.VMEM(mask.shape, F32),
            pltpu.VMEM(out_weight.shape, BF16),
            pltpu.VMEM(out_gain.shape, F32),
            spread_scratch,
            pltpu.VMEM((channels, lanes), BF16),
            pltpu.SemaphoreType.DMA((7,)),
        ],
        1_000_000_000,
        7,
        pltpu.HBM,
        READY_VMEM,
    )(pair_acts, gain, proj_weight, out_cotangent, mask, out_weight, out_gain)
    mine, normed, order = lax.optimization_barrier((mine, normed, order))
    half_plane = (full_len // 2, plane[1])
    theirs = other_core(mine)
    left_mine, right_mine = local_call(
        functools.partial(own_sides_kernel, na),
        (array(half_plane), array(half_plane)),
        [pltpu.VMEM(sides_chunk, F32)],
        1_000_000_000,
        1,
    )(mine)
    tri, left, right = local_call(
        functools.partial(tri_kernel, na),
        (array(tri_chunk), array(plane), array(plane)),
        [pltpu.VMEM(sides_chunk, F32), pltpu.VMEM(tri_chunk, F32)],
        300_000_000,
        4,
    )(theirs, left_mine, right_mine, order)
    tri = exchange(tri, TRI_ROWS, CHANNEL_AXES)
    back, gate, out_proj = local_call(
        middle_kernel,
        (array(tri_chunk), array((channels, lanes)), array((channels, lanes), F32)),
        [
            pltpu.VMEM(tri_chunk, F32),
            pltpu.VMEM((hidden, lanes), F32),
            pltpu.VMEM((hidden, lanes), BF16),
        ],
        100_000_000,
        4,
    )(tri, normed, back_norm, gate_coef)
    back = exchange(back, TRI_ROWS, CHANNEL_AXES)
    update = local_call(update_kernel, array(pair_acts.shape), [], 1_000_000_000, 2)(
        gate_mask, out_proj
    )
    theirs = other_core(back)
    turned, back_left, total = local_call(
        functools.partial(own_back_kernel, na),
        (array((full_len // 2, full_len)), array(half_plane, F32), array((8, LANES), F32)),
        [pltpu.VMEM(tri_chunk, F32), pltpu.VMEM(half_plane, BF16)],
        1_000_000_000,
        3,
    )(back, right, order)
    back_sides = local_call(
        functools.partial(back_kernel, na),
        array(sides_chunk),
        [
            pltpu.VMEM(tri_chunk, F32),
            pltpu.VMEM(sides_chunk, F32),
            pltpu.VMEM(half_plane, BF16),
            pltpu.VMEM((full_len, full_len), BF16),
        ],
        300_000_000,
        6,
    )(theirs, turned, back_left, total, left, order)
    back_sides = exchange(back_sides, SIDE_ROWS, CHANNEL_AXES)
    term, back_proj, gate_total = local_call(
        weight_kernel,
        (array(term_chunk), array((width_all, lanes)), array((channels, channels), F32)),
        [pltpu.VMEM(sides_chunk, F32), pltpu.VMEM(term_chunk, F32)],
        200_000_000,
        4,
    )(back_sides, normed, coef, gate)
    grad_pair = local_call(
        pair_kernel, array(pair_acts.shape), [spread_scratch], 1_000_000_000, 4
    )(pair_acts, gain, proj_weight, back_proj)
    parts = exchange(term, 2, ALL_AXES)
    sums = local_call(functools.partial(sum_kernel, full_len), array(term_chunk), [], 100_000, 1)(parts)
    sums = exchange(sums, 2, ALL_AXES)
    grad_weight = local_call(
        grad_weight_kernel,
        array((channels, width_all), F32),
        [pltpu.VMEM(term_chunk, F32)],
        100_000,
        2,
    )(sums, gate_total)
    return update, grad_pair, grad_weight


def solution(mesh):
    rows, cols = mesh.devices.shape
    split = Mesh(mesh.devices.reshape(rows // 2, 2, cols), ("chip", "core", "col"))
    pairs = P(("chip", "core"), "col", None)
    return jax.shard_map(
        per_device,
        mesh=split,
        in_specs=(pairs, P(), P(), P(), P(), P(), pairs),
        out_specs=(pairs, pairs, P()),
        check_vma=False,
    )
```

```python
import functools

import jax
import jax.numpy as jnp
from jax import lax
from jax.experimental import pallas as pl
from jax.experimental.pallas import tpu as pltpu
from jax.sharding import Mesh
from jax.sharding import PartitionSpec as P

EPSILON = 1e-05
BF16 = jnp.bfloat16
F32 = jnp.float32
ALL_AXES = ("zh", "x", "col", "core")
CHANNEL_AXES = ("x", "zh", "col")
LANES = 128
SLOT = 64
PIECE = 16
SIDE_ROWS = 10
TRI_ROWS = 6
VMEM_LIMIT = 48 * 1024 * 1024
WHOLE_VMEM = 64 * 1024 * 1024 - 65536
READY_VMEM = 62 * 1024 * 1024

NT = (((1,), (1,)), ((), ()))
NN = (((1,), (0,)), ((), ()))
TN = (((0,), (0,)), ((), ()))


def matmul(lhs, rhs, dims=NN):
    return lax.dot_general(lhs, rhs, dims, preferred_element_type=F32)


def column(row_ref):
    return jnp.broadcast_to(row_ref[...], (LANES, LANES)).T


def swap_halves(values):
    return pltpu.roll(values, SLOT, 1)


def low_half(shape):
    return lax.broadcasted_iota(jnp.int32, shape, 1) < SLOT


def spread(pairs_ref, spread_ref):
    na, nb, channels = pairs_ref.shape
    for a in range(na):
        spread_ref[a * SLOT : a * SLOT + nb, :] = pairs_ref[a].astype(F32)
        spread_ref[a * SLOT + nb : (a + 1) * SLOT, :] = jnp.zeros((SLOT - nb, channels), F32)


def store_pairs(out_ref, t, values):
    nb = out_ref.shape[1]
    turned = values.T
    out_ref[2 * t] = turned[0:nb].astype(out_ref.dtype)
    out_ref[2 * t + 1] = turned[SLOT : SLOT + nb].astype(out_ref.dtype)


def masks(valid_ref, na, nb):
    lane = lax.broadcasted_iota(jnp.int32, (1, LANES), 1)
    place = lane % SLOT
    first_row = lax.axis_index(("x", "zh", "core")) * na
    first_col = lax.axis_index("col") * nb
    cols = jnp.zeros((1, LANES), jnp.int32)
    for b in range(nb):
        cols = jnp.where(place == b, valid_ref[first_col + b], cols)
    found = []
    for t in range(na // 2):
        rows = jnp.where(lane < SLOT, valid_ref[first_row + 2 * t], valid_ref[first_row + 2 * t + 1])
        found.append((rows * cols).astype(F32))
    return found


def tile_norm(values):
    center = jnp.mean(values, axis=0, keepdims=True)
    shifted = values - center
    inv_std = lax.rsqrt(jnp.mean(shifted * shifted, axis=0, keepdims=True) + EPSILON)
    return shifted * inv_std, inv_std


def tile_norm_grad(upstream, scaled, inv_std):
    first = jnp.mean(upstream, axis=0, keepdims=True)
    second = jnp.mean(upstream * scaled, axis=0, keepdims=True)
    return inv_std * (upstream - first - scaled * second)


def norm_tiles(spread_ref, gain_ref, normed_ref):
    gain = column(gain_ref)
    tiles = spread_ref.shape[0] // LANES
    for t in range(tiles):
        at = slice(t * LANES, (t + 1) * LANES)
        scaled, _ = tile_norm(spread_ref[at, :].T)
        normed_ref[:, at] = (scaled * gain).astype(BF16)


def gap(shape):
    return lax.broadcasted_iota(jnp.int32, shape, 1) % SLOT >= SLOT - PIECE


def pack_tiles(tiles):
    free = gap(tiles[0].shape)
    rows = []
    for t in range(9):
        moved = pltpu.roll(tiles[9 + t // 3], SLOT - PIECE - PIECE * (t % 3), 1)
        rows.append(jnp.where(free, moved, tiles[t]))
    return rows


def unpack_tiles(rows):
    free = gap(rows[0].shape)
    place = lax.broadcasted_iota(jnp.int32, rows[0].shape, 1) % SLOT // PIECE
    tiles = [jnp.where(free, 0.0, row) for row in rows]
    for m in range(3):
        tile = jnp.zeros_like(rows[0])
        for p in range(3):
            moved = pltpu.roll(rows[3 * m + p], LANES - (SLOT - PIECE) + PIECE * p, 1)
            tile = jnp.where(place == p, moved, tile)
        tiles.append(tile)
    return tiles


def device_rows(chunk_ref, depth, row):
    return chunk_ref[pl.ds(row, chunk_ref.shape[0] // depth, stride=depth), :]


def put_device_rows(chunk_ref, depth, row, values):
    chunk_ref[pl.ds(row, chunk_ref.shape[0] // depth, stride=depth), :] = values


def group_rows(depth, lo, col, row):
    return pl.ds(depth * (64 * lo + col) + row, 8, stride=8 * depth)


def plane_rows(na, lo, t):
    return slice(8 * (na * lo + 2 * t), 8 * (na * lo + 2 * t) + 16)


def plane_tile(even, odd):
    low = low_half(even.shape)
    upper = jnp.where(low, even, swap_halves(odd))
    lower = jnp.where(low, swap_halves(even), odd)
    return jnp.concatenate([upper, lower], axis=0)


def chunk_tiles(rows):
    upper, lower = rows[0:8], rows[8:16]
    low = low_half(upper.shape)
    return jnp.where(low, upper, swap_halves(lower)), jnp.where(low, swap_halves(upper), lower)


def token_order(na, plane):
    row = lax.broadcasted_iota(jnp.int32, (16 * 2 * na, plane), 0)
    token = lax.broadcasted_iota(jnp.int32, (16 * 2 * na, plane), 1)
    place = row // 8
    theirs = (place >= 2 * na).astype(jnp.int32)
    place = place - 2 * na * theirs
    core = lax.axis_index("core")
    core = core + theirs * (1 - 2 * core)
    lo = (place >= na).astype(jnp.int32)
    a = place - na * lo
    hi = row % 8
    found = SLOT * (4 * lo + hi // 2) + na * (2 * (hi % 2) + core) + a
    return (token == found).astype(F32).astype(BF16)


def sides_kernel(
    valid_hbm, acts_hbm, gain_hbm, weight_hbm, out_ref, mask_ref,
    valid_ref, acts_ref, gain_ref, weight_ref, spread_ref, normed_ref, chunk_ref, sems,
):
    na, nb, _ = acts_hbm.shape
    tiles = na // 2
    hidden = weight_hbm.shape[0]
    copies = [
        pltpu.make_async_copy(valid_hbm, valid_ref, sems.at[0]),
        pltpu.make_async_copy(acts_hbm, acts_ref, sems.at[1]),
        pltpu.make_async_copy(gain_hbm, gain_ref, sems.at[2]),
        pltpu.make_async_copy(weight_hbm, weight_ref, sems.at[3]),
    ]
    for copy in copies:
        copy.start()
    copies[0].wait()
    mask = masks(valid_ref, na, nb)
    for t in range(tiles):
        mask_ref[:, t * LANES : (t + 1) * LANES] = mask[t]
    copies[1].wait()
    spread(acts_ref, spread_ref)
    copies[2].wait()
    norm_tiles(spread_ref, gain_ref, normed_ref)
    copies[3].wait()
    projected = matmul(weight_ref[:, 0 : 4 * hidden], normed_ref[...], TN)
    found = []
    for side in range(2):
        base = 2 * side * hidden
        for t in range(tiles):
            at = slice(t * LANES, (t + 1) * LANES)
            gate = jax.nn.sigmoid(projected[base : base + hidden, at])
            value = projected[base + hidden : base + 2 * hidden, at]
            found.append(gate * value * mask[t])
    for t, row in enumerate(pack_tiles(found)):
        put_device_rows(chunk_ref, SIDE_ROWS, t, row)
    put_device_rows(chunk_ref, SIDE_ROWS, 9, jnp.zeros((hidden, LANES), F32))
    out_ref[...] = chunk_ref[...].astype(BF16)


def ready_kernel(
    acts_hbm, gain_hbm, weight_hbm, cotangent_hbm, mask_hbm, out_weight_hbm, out_gain_hbm,
    normed_ref, back_norm_ref, gate_mask_ref, gate_coef_ref, coef_ref,
    acts_ref, gain_ref, weight_ref, cotangent_ref, mask_ref, out_weight_ref, out_gain_ref,
    spread_ref, back_out_ref, sems,
):
    na = acts_ref.shape[0]
    tiles = na // 2
    hidden = out_weight_ref.shape[0]
    copies = [
        pltpu.make_async_copy(acts_hbm, acts_ref, sems.at[0]),
        pltpu.make_async_copy(gain_hbm, gain_ref, sems.at[1]),
        pltpu.make_async_copy(weight_hbm, weight_ref, sems.at[2]),
        pltpu.make_async_copy(cotangent_hbm, cotangent_ref, sems.at[3]),
        pltpu.make_async_copy(mask_hbm, mask_ref, sems.at[4]),
        pltpu.make_async_copy(out_weight_hbm, out_weight_ref, sems.at[5]),
        pltpu.make_async_copy(out_gain_hbm, out_gain_ref, sems.at[6]),
    ]
    for copy in copies:
        copy.start()
    for copy in copies:
        copy.wait()
    spread(acts_ref, spread_ref)
    norm_tiles(spread_ref, gain_ref, normed_ref)
    spread(cotangent_ref, spread_ref)
    projected = matmul(weight_ref[...], normed_ref[...], TN)
    for t in range(tiles):
        at = slice(t * LANES, (t + 1) * LANES)
        mask = mask_ref[:, at]
        gate = jax.nn.sigmoid(projected[4 * hidden :, at])
        gate_mask = gate * mask
        cotangent = spread_ref[at, :].T
        gate_mask_ref[:, at] = gate_mask
        gate_coef_ref[:, at] = cotangent * gate_mask * (1.0 - gate)
        back_out_ref[:, at] = (cotangent * gate_mask).astype(BF16)
        for base in (0, 2 * hidden):
            gate = jax.nn.sigmoid(projected[base : base + hidden, at])
            value = projected[base + hidden : base + 2 * hidden, at]
            coef_ref[base : base + hidden, at] = value * gate * (1.0 - gate) * mask
            coef_ref[base + hidden : base + 2 * hidden, at] = gate * mask
    out_gain = column(out_gain_ref)
    back_norm = matmul(out_weight_ref[...], back_out_ref[...])
    for t in range(tiles):
        at = slice(t * LANES, (t + 1) * LANES)
        back_norm_ref[:, at] = back_norm[:, at] * out_gain
    back_norm_ref[:, tiles * LANES : (tiles + 1) * LANES] = out_gain
    back_norm_ref[:, (tiles + 1) * LANES :] = out_weight_ref[...].astype(F32)


def order_kernel(na, order_ref):
    order_ref[...] = token_order(na, order_ref.shape[1])


def side_planes(na, chunk_ref, left_ref, right_ref, first):
    tiles = na // 2
    for pair in range(4):
        at = slice(pair * LANES, (pair + 1) * LANES)
        for lo in range(2):
            even, odd = [
                unpack_tiles([chunk_ref[group_rows(SIDE_ROWS, lo, col, t), :] for t in range(9)])
                for col in (2 * pair, 2 * pair + 1)
            ]
            for t in range(tiles):
                rows = plane_rows(na, lo, t)
                rows = slice(first + rows.start, first + rows.stop)
                left_ref[rows, at] = plane_tile(even[t], odd[t]).astype(BF16)
                right_ref[rows, at] = plane_tile(even[tiles + t], odd[tiles + t]).astype(BF16)


def own_sides_kernel(na, mine_ref, left_ref, right_ref, chunk_ref):
    chunk_ref[...] = mine_ref[...].astype(F32)
    side_planes(na, chunk_ref, left_ref, right_ref, 0)


def tri_kernel(
    na, theirs_ref, left_mine_ref, right_mine_ref, order_ref, tri_ref, left_ref, right_ref,
    chunk_ref, tri_chunk_ref,
):
    tiles = na // 2
    half = left_mine_ref.shape[0]
    chunk_ref[...] = theirs_ref[...].astype(F32)
    left_ref[0:half, :] = left_mine_ref[...]
    right_ref[0:half, :] = right_mine_ref[...]
    side_planes(na, chunk_ref, left_ref, right_ref, half)
    tri = matmul(left_mine_ref[...], right_ref[...], NT).astype(BF16)
    tri = matmul(tri, order_ref[...])
    for pair in range(4):
        for lo in range(2):
            for t in range(tiles):
                both = chunk_tiles(tri[plane_rows(na, lo, t), pair * LANES : (pair + 1) * LANES])
                for side in range(2):
                    tri_chunk_ref[group_rows(TRI_ROWS, lo, 2 * pair + side, t), :] = both[side]
    tri_ref[...] = tri_chunk_ref[...].astype(BF16)


def middle_kernel(
    tri_ref, normed_ref, back_norm_ref, gate_coef_ref,
    back_ref, gate_ref, out_proj_ref,
    tri_chunk_ref, scaled_ref, normed_out_ref,
):
    tiles = normed_ref.shape[1] // LANES
    tri_chunk_ref[...] = tri_ref[...].astype(F32)
    out_gain = back_norm_ref[:, tiles * LANES : (tiles + 1) * LANES]
    out_weight = back_norm_ref[:, (tiles + 1) * LANES :].astype(BF16)
    inv_out = []
    for t in range(tiles):
        at = slice(t * LANES, (t + 1) * LANES)
        scaled, inv = tile_norm(device_rows(tri_chunk_ref, TRI_ROWS, t))
        inv_out.append(inv)
        scaled_ref[:, at] = scaled
        normed_out_ref[:, at] = (scaled * out_gain).astype(BF16)
    out_proj = matmul(out_weight, normed_out_ref[...], TN)
    out_proj_ref[...] = out_proj
    gate_ref[...] = (out_proj * gate_coef_ref[...]).astype(BF16)
    term = matmul(normed_ref[...], gate_ref[...], NT)
    free = gap(term.shape)
    for t in range(tiles):
        at = slice(t * LANES, (t + 1) * LANES)
        row = tile_norm_grad(back_norm_ref[:, at], scaled_ref[:, at], inv_out[t])
        if t < 4:
            moved = pltpu.roll(term, SLOT - PIECE - PIECE * t, 1) if t < 3 else term
            row = jnp.where(free, moved, row)
        put_device_rows(tri_chunk_ref, TRI_ROWS, t, row)
    back_ref[...] = tri_chunk_ref[...].astype(BF16)


def update_kernel(gate_mask_ref, out_proj_ref, update_ref):
    for t in range(update_ref.shape[0] // 2):
        at = slice(t * LANES, (t + 1) * LANES)
        store_pairs(update_ref, t, gate_mask_ref[:, at] * out_proj_ref[:, at])


def back_plane(na, chunk_ref, plane_ref):
    free = gap((8, LANES))
    for pair in range(4):
        for lo in range(2):
            for t in range(na // 2):
                even, odd = [
                    jnp.where(free, 0.0, chunk_ref[group_rows(TRI_ROWS, lo, col, t), :])
                    for col in (2 * pair, 2 * pair + 1)
                ]
                plane_ref[plane_rows(na, lo, t), pair * LANES : (pair + 1) * LANES] = plane_tile(
                    even, odd
                ).astype(BF16)


def gap_total(chunk_ref):
    place = lax.broadcasted_iota(jnp.int32, (8, LANES), 1) % SLOT // PIECE
    total = jnp.zeros((8, LANES), F32)
    for t in range(4):
        rows = jnp.zeros((8, LANES), F32)
        for m in range(chunk_ref.shape[0] // (8 * TRI_ROWS)):
            rows += chunk_ref[pl.ds(8 * TRI_ROWS * m + t, 8, stride=TRI_ROWS), :]
        rows = jnp.broadcast_to(jnp.sum(rows, axis=0, keepdims=True), (8, LANES))
        if t < 3:
            rows = pltpu.roll(rows, LANES - (SLOT - PIECE) + PIECE * t, 1)
        total = jnp.where(place == t, rows, total)
    return total


def own_back_kernel(
    na, mine_ref, right_ref, order_ref, turned_ref, back_left_ref, total_ref, chunk_ref, plane_ref
):
    chunk_ref[...] = mine_ref[...].astype(F32)
    back_plane(na, chunk_ref, plane_ref)
    turned_ref[...] = matmul(plane_ref[...], order_ref[...], NT).astype(BF16)
    back_left_ref[...] = matmul(turned_ref[...], right_ref[...])
    total_ref[...] = gap_total(chunk_ref)


def back_kernel(
    na, theirs_ref, turned_mine_ref, back_left_ref, total_ref, left_ref, order_ref, out_ref,
    back_chunk_ref, chunk_ref, plane_ref, turned_ref,
):
    tiles = na // 2
    half = turned_mine_ref.shape[0]
    back_chunk_ref[...] = theirs_ref[...].astype(F32)
    back_plane(na, back_chunk_ref, plane_ref)
    turned_ref[0:half, :] = turned_mine_ref[...]
    turned_ref[half:, :] = matmul(plane_ref[...], order_ref[...], NT).astype(BF16)
    back_right = matmul(turned_ref[:, 0:half], left_ref[...], TN)
    total = (total_ref[...] + gap_total(back_chunk_ref)) / (4 * 8 * na)
    for m in range(chunk_ref.shape[0] // (8 * SIDE_ROWS)):
        chunk_ref[pl.ds(8 * SIDE_ROWS * m + 9, 8, stride=SIDE_ROWS), :] = total
    for pair in range(4):
        at = slice(pair * LANES, (pair + 1) * LANES)
        for lo in range(2):
            found = [chunk_tiles(back_left_ref[plane_rows(na, lo, t), at]) for t in range(tiles)]
            found += [chunk_tiles(back_right[plane_rows(na, lo, t), at]) for t in range(tiles)]
            for side in range(2):
                for t, row in enumerate(pack_tiles([both[side] for both in found])):
                    chunk_ref[group_rows(SIDE_ROWS, lo, 2 * pair + side, t), :] = row
    out_ref[...] = chunk_ref[...].astype(BF16)


def weight_kernel(
    back_ref, normed_ref, coef_ref, gate_ref, term_ref, back_proj_ref, gate_total_ref,
    chunk_ref, term_chunk_ref,
):
    tiles = normed_ref.shape[1] // LANES
    hidden = normed_ref.shape[0]
    chunk_ref[...] = back_ref[...].astype(F32)
    gate_total_ref[...] = device_rows(chunk_ref, SIDE_ROWS, 9)
    back_proj_ref[4 * hidden :, :] = gate_ref[...]
    upstreams = unpack_tiles([device_rows(chunk_ref, SIDE_ROWS, t) for t in range(9)])
    for side in range(2):
        for t in range(tiles):
            at = slice(t * LANES, (t + 1) * LANES)
            for base in (2 * side * hidden, (2 * side + 1) * hidden):
                rows = slice(base, base + hidden)
                back_proj_ref[rows, at] = (upstreams[tiles * side + t] * coef_ref[rows, at]).astype(BF16)
    term = matmul(normed_ref[...], back_proj_ref[0 : 4 * hidden, :], NT)
    for t in range(4):
        put_device_rows(term_chunk_ref, 4, t, term[:, t * LANES : (t + 1) * LANES])
    term_ref[...] = term_chunk_ref[...].astype(BF16)


def sum_kernel(full_len, parts_ref, out_ref):
    total = jnp.zeros((16, LANES), F32)
    for m in range(parts_ref.shape[0] // 16):
        total += parts_ref[16 * m : 16 * m + 16, :].astype(F32)
    total = total[0:8] + total[8:16]
    total = total + pltpu.roll(total, 4, 0)
    total = total + pltpu.roll(total, 2, 0)
    total = total / full_len
    total = jnp.concatenate([total, total], axis=0).astype(BF16)
    for m in range(out_ref.shape[0] // 16):
        out_ref[16 * m : 16 * m + 16, :] = total


def grad_weight_kernel(sums_ref, gate_total_ref, out_ref, chunk_ref):
    chunk_ref[...] = sums_ref[...].astype(F32)
    for t in range(4):
        out_ref[:, t * LANES : (t + 1) * LANES] = device_rows(chunk_ref, 4, t)
    out_ref[:, 4 * LANES :] = gate_total_ref[...]


def pair_kernel(acts_ref, gain_ref, weight_ref, back_proj_ref, grad_pair_ref, spread_ref):
    na, nb, _ = acts_ref.shape
    spread(acts_ref, spread_ref)
    gain = column(gain_ref)
    back_normed = matmul(weight_ref[...], back_proj_ref[...])
    for t in range(na // 2):
        at = slice(t * LANES, (t + 1) * LANES)
        scaled, inv = tile_norm(spread_ref[at, :].T)
        store_pairs(grad_pair_ref, t, tile_norm_grad(back_normed[:, at] * gain, scaled, inv))


def local_call(body, outs, scratch, flops, inputs, space=pltpu.VMEM, limit=VMEM_LIMIT):
    return pl.pallas_call(
        body,
        out_shape=outs,
        in_specs=[pl.BlockSpec(memory_space=space)] * inputs,
        out_specs=jax.tree.map(lambda _: pl.BlockSpec(memory_space=pltpu.VMEM), outs),
        scratch_shapes=scratch,
        compiler_params=pltpu.CompilerParams(vmem_limit_bytes=limit),
        cost_estimate=pl.CostEstimate(flops=flops, bytes_accessed=2_000_000, transcendentals=0),
    )


def exchange(chunks, depth, axes):
    devices = chunks.shape[0] // depth
    split = chunks.reshape(devices, depth // 2, 2, chunks.shape[1])
    return lax.all_to_all(split, axes, 0, 0, tiled=True).reshape(chunks.shape)


def other_core(values):
    return lax.ppermute(values, "core", [(0, 1), (1, 0)])


def array(shape, dtype=BF16):
    return jax.ShapeDtypeStruct(shape, dtype)


def per_device(pair_acts, token_valid, norm_gain, proj_weight, out_gain, out_weight, out_cotangent):
    na, _, channels = pair_acts.shape
    hidden = out_weight.shape[0]
    width_all = proj_weight.shape[1]
    full_len = token_valid.shape[0]
    lanes = na // 2 * LANES
    plane = (full_len, 8 * SLOT)
    sides_chunk = (hidden * SIDE_ROWS, LANES)
    tri_chunk = (hidden * TRI_ROWS, LANES)
    term_chunk = (4 * hidden, LANES)
    gain = norm_gain.reshape(1, channels)
    out_gain = out_gain.reshape(1, hidden)
    spread_scratch = pltpu.VMEM((lanes, channels), F32)

    sides, mask = local_call(
        sides_kernel,
        (array(sides_chunk), array((1, lanes), F32)),
        [
            pltpu.SMEM(token_valid.shape, jnp.int32),
            pltpu.VMEM(pair_acts.shape, BF16),
            pltpu.VMEM(gain.shape, F32),
            pltpu.VMEM(proj_weight.shape, BF16),
            spread_scratch,
            pltpu.VMEM((channels, lanes), BF16),
            pltpu.VMEM(sides_chunk, F32),
            pltpu.SemaphoreType.DMA((4,)),
        ],
        100_000_000,
        4,
        pltpu.HBM,
        WHOLE_VMEM,
    )(token_valid, pair_acts, gain, proj_weight)
    mine = exchange(sides, SIDE_ROWS, CHANNEL_AXES)
    order = local_call(functools.partial(order_kernel, na), array(plane), [], 1_000_000_000, 0)()
    normed, back_norm, gate_mask, gate_coef, coef = local_call(
        ready_kernel,
        (
            array((channels, lanes)),
            array((hidden, lanes + 2 * LANES), F32),
            array((channels, lanes), F32),
            array((channels, lanes), F32),
            array((4 * hidden, lanes), F32),
        ),
        [
            pltpu.VMEM(pair_acts.shape, BF16),
            pltpu.VMEM(gain.shape, F32),
            pltpu.VMEM(proj_weight.shape, BF16),
            pltpu.VMEM(out_cotangent.shape, BF16),
            pltpu.VMEM(mask.shape, F32),
            pltpu.VMEM(out_weight.shape, BF16),
            pltpu.VMEM(out_gain.shape, F32),
            spread_scratch,
            pltpu.VMEM((channels, lanes), BF16),
            pltpu.SemaphoreType.DMA((7,)),
        ],
        1_000_000_000,
        7,
        pltpu.HBM,
        READY_VMEM,
    )(pair_acts, gain, proj_weight, out_cotangent, mask, out_weight, out_gain)
    mine, normed, order = lax.optimization_barrier((mine, normed, order))
    half_plane = (full_len // 2, plane[1])
    theirs = other_core(mine)
    left_mine, right_mine = local_call(
        functools.partial(own_sides_kernel, na),
        (array(half_plane), array(half_plane)),
        [pltpu.VMEM(sides_chunk, F32)],
        1_000_000_000,
        1,
    )(mine)
    tri, left, right = local_call(
        functools.partial(tri_kernel, na),
        (array(tri_chunk), array(plane), array(plane)),
        [pltpu.VMEM(sides_chunk, F32), pltpu.VMEM(tri_chunk, F32)],
        300_000_000,
        4,
    )(theirs, left_mine, right_mine, order)
    tri = exchange(tri, TRI_ROWS, CHANNEL_AXES)
    back, gate, out_proj = local_call(
        middle_kernel,
        (array(tri_chunk), array((channels, lanes)), array((channels, lanes), F32)),
        [
            pltpu.VMEM(tri_chunk, F32),
            pltpu.VMEM((hidden, lanes), F32),
            pltpu.VMEM((hidden, lanes), BF16),
        ],
        100_000_000,
        4,
    )(tri, normed, back_norm, gate_coef)
    back = exchange(back, TRI_ROWS, CHANNEL_AXES)
    update = local_call(update_kernel, array(pair_acts.shape), [], 1_000_000_000, 2)(
        gate_mask, out_proj
    )
    theirs = other_core(back)
    turned, back_left, total = local_call(
        functools.partial(own_back_kernel, na),
        (array((full_len // 2, full_len)), array(half_plane, F32), array((8, LANES), F32)),
        [pltpu.VMEM(tri_chunk, F32), pltpu.VMEM(half_plane, BF16)],
        1_000_000_000,
        3,
    )(back, right, order)
    back_sides = local_call(
        functools.partial(back_kernel, na),
        array(sides_chunk),
        [
            pltpu.VMEM(tri_chunk, F32),
            pltpu.VMEM(sides_chunk, F32),
            pltpu.VMEM(half_plane, BF16),
            pltpu.VMEM((full_len, full_len), BF16),
        ],
        300_000_000,
        6,
    )(theirs, turned, back_left, total, left, order)
    back_sides = exchange(back_sides, SIDE_ROWS, CHANNEL_AXES)
    term, back_proj, gate_total = local_call(
        weight_kernel,
        (array(term_chunk), array((width_all, lanes)), array((channels, channels), F32)),
        [pltpu.VMEM(sides_chunk, F32), pltpu.VMEM(term_chunk, F32)],
        200_000_000,
        4,
    )(back_sides, normed, coef, gate)
    grad_pair = local_call(
        pair_kernel, array(pair_acts.shape), [spread_scratch], 1_000_000_000, 4
    )(pair_acts, gain, proj_weight, back_proj)
    parts = exchange(term, 2, ALL_AXES)
    sums = local_call(functools.partial(sum_kernel, full_len), array(term_chunk), [], 100_000, 1)(parts)
    sums = exchange(sums, 2, ALL_AXES)
    grad_weight = local_call(
        grad_weight_kernel,
        array((channels, width_all), F32),
        [pltpu.VMEM(term_chunk, F32)],
        100_000,
        2,
    )(sums, gate_total)
    return update, grad_pair, grad_weight


def solution(mesh):
    rows, cols = mesh.devices.shape
    split = Mesh(mesh.devices.reshape(rows // 8, 4, 2, cols), ("x", "zh", "core", "col"))
    pairs = P(("x", "zh", "core"), "col", None)
    return jax.shard_map(
        per_device,
        mesh=split,
        in_specs=(pairs, P(), P(), P(), P(), P(), pairs),
        out_specs=(pairs, pairs, P()),
        check_vma=False,
    )
```

```python
import functools

import jax
import jax.numpy as jnp
from jax import lax
from jax.experimental import pallas as pl
from jax.experimental.pallas import tpu as pltpu
from jax.sharding import Mesh
from jax.sharding import PartitionSpec as P

EPSILON = 1e-05
BF16 = jnp.bfloat16
F32 = jnp.float32
ALL_AXES = ("chip", "core", "col")
CHANNEL_AXES = ("col", "chip")
LANES = 128
SLOT = 64
PIECE = 16
SIDE_ROWS = 10
TRI_ROWS = 6
VMEM_LIMIT = 48 * 1024 * 1024
WHOLE_VMEM = 64 * 1024 * 1024 - 65536
READY_VMEM = 62 * 1024 * 1024

NT = (((1,), (1,)), ((), ()))
NN = (((1,), (0,)), ((), ()))
TN = (((0,), (0,)), ((), ()))


def matmul(lhs, rhs, dims=NN):
    return lax.dot_general(lhs, rhs, dims, preferred_element_type=F32)


def column(row_ref):
    return jnp.broadcast_to(row_ref[...], (LANES, LANES)).T


def swap_halves(values):
    return pltpu.roll(values, SLOT, 1)


def low_half(shape):
    return lax.broadcasted_iota(jnp.int32, shape, 1) < SLOT


def spread(pairs_ref, spread_ref):
    na, nb, channels = pairs_ref.shape
    for a in range(na):
        spread_ref[a * SLOT : a * SLOT + nb, :] = pairs_ref[a].astype(F32)
        spread_ref[a * SLOT + nb : (a + 1) * SLOT, :] = jnp.zeros((SLOT - nb, channels), F32)


def store_pairs(out_ref, t, values):
    nb = out_ref.shape[1]
    turned = values.T
    out_ref[2 * t] = turned[0:nb].astype(out_ref.dtype)
    out_ref[2 * t + 1] = turned[SLOT : SLOT + nb].astype(out_ref.dtype)


def masks(valid_ref, na, nb):
    lane = lax.broadcasted_iota(jnp.int32, (1, LANES), 1)
    place = lane % SLOT
    first_row = (2 * lax.axis_index("chip") + lax.axis_index("core")) * na
    first_col = lax.axis_index("col") * nb
    cols = jnp.zeros((1, LANES), jnp.int32)
    for b in range(nb):
        cols = jnp.where(place == b, valid_ref[first_col + b], cols)
    found = []
    for t in range(na // 2):
        rows = jnp.where(lane < SLOT, valid_ref[first_row + 2 * t], valid_ref[first_row + 2 * t + 1])
        found.append((rows * cols).astype(F32))
    return found


def tile_norm(values):
    center = jnp.mean(values, axis=0, keepdims=True)
    shifted = values - center
    inv_std = lax.rsqrt(jnp.mean(shifted * shifted, axis=0, keepdims=True) + EPSILON)
    return shifted * inv_std, inv_std


def tile_norm_grad(upstream, scaled, inv_std):
    first = jnp.mean(upstream, axis=0, keepdims=True)
    second = jnp.mean(upstream * scaled, axis=0, keepdims=True)
    return inv_std * (upstream - first - scaled * second)


def norm_tiles(spread_ref, gain_ref, normed_ref):
    gain = column(gain_ref)
    tiles = spread_ref.shape[0] // LANES
    for t in range(tiles):
        at = slice(t * LANES, (t + 1) * LANES)
        scaled, _ = tile_norm(spread_ref[at, :].T)
        normed_ref[:, at] = (scaled * gain).astype(BF16)


def gap(shape):
    return lax.broadcasted_iota(jnp.int32, shape, 1) % SLOT >= SLOT - PIECE


def pack_tiles(tiles):
    free = gap(tiles[0].shape)
    rows = []
    for t in range(9):
        moved = pltpu.roll(tiles[9 + t // 3], SLOT - PIECE - PIECE * (t % 3), 1)
        rows.append(jnp.where(free, moved, tiles[t]))
    return rows


def unpack_tiles(rows):
    free = gap(rows[0].shape)
    place = lax.broadcasted_iota(jnp.int32, rows[0].shape, 1) % SLOT // PIECE
    tiles = [jnp.where(free, 0.0, row) for row in rows]
    for m in range(3):
        tile = jnp.zeros_like(rows[0])
        for p in range(3):
            moved = pltpu.roll(rows[3 * m + p], LANES - (SLOT - PIECE) + PIECE * p, 1)
            tile = jnp.where(place == p, moved, tile)
        tiles.append(tile)
    return tiles


def device_rows(chunk_ref, depth, row):
    return chunk_ref[pl.ds(row, chunk_ref.shape[0] // depth, stride=depth), :]


def put_device_rows(chunk_ref, depth, row, values):
    chunk_ref[pl.ds(row, chunk_ref.shape[0] // depth, stride=depth), :] = values


def group_rows(depth, lo, col, row):
    return pl.ds(depth * (16 * col + lo) + row, 8, stride=2 * depth)


def plane_rows(na, lo, t):
    return slice(8 * (na * lo + 2 * t), 8 * (na * lo + 2 * t) + 16)


def plane_tile(even, odd):
    low = low_half(even.shape)
    upper = jnp.where(low, even, swap_halves(odd))
    lower = jnp.where(low, swap_halves(even), odd)
    return jnp.concatenate([upper, lower], axis=0)


def chunk_tiles(rows):
    upper, lower = rows[0:8], rows[8:16]
    low = low_half(upper.shape)
    return jnp.where(low, upper, swap_halves(lower)), jnp.where(low, swap_halves(upper), lower)


def token_order(na, plane):
    row = lax.broadcasted_iota(jnp.int32, (16 * 2 * na, plane), 0)
    token = lax.broadcasted_iota(jnp.int32, (16 * 2 * na, plane), 1)
    place = row // 8
    theirs = (place >= 2 * na).astype(jnp.int32)
    place = place - 2 * na * theirs
    core = lax.axis_index("core")
    core = core + theirs * (1 - 2 * core)
    lo = (place >= na).astype(jnp.int32)
    a = place - na * lo
    return (token == SLOT * (row % 8) + na * (2 * lo + core) + a).astype(F32).astype(BF16)


def sides_kernel(
    valid_hbm, acts_hbm, gain_hbm, weight_hbm, out_ref, mask_ref,
    valid_ref, acts_ref, gain_ref, weight_ref, spread_ref, normed_ref, chunk_ref, sems,
):
    na, nb, _ = acts_hbm.shape
    tiles = na // 2
    hidden = weight_hbm.shape[0]
    copies = [
        pltpu.make_async_copy(valid_hbm, valid_ref, sems.at[0]),
        pltpu.make_async_copy(acts_hbm, acts_ref, sems.at[1]),
        pltpu.make_async_copy(gain_hbm, gain_ref, sems.at[2]),
        pltpu.make_async_copy(weight_hbm, weight_ref, sems.at[3]),
    ]
    for copy in copies:
        copy.start()
    copies[0].wait()
    mask = masks(valid_ref, na, nb)
    for t in range(tiles):
        mask_ref[:, t * LANES : (t + 1) * LANES] = mask[t]
    copies[1].wait()
    spread(acts_ref, spread_ref)
    copies[2].wait()
    norm_tiles(spread_ref, gain_ref, normed_ref)
    copies[3].wait()
    projected = matmul(weight_ref[:, 0 : 4 * hidden], normed_ref[...], TN)
    found = []
    for side in range(2):
        base = 2 * side * hidden
        for t in range(tiles):
            at = slice(t * LANES, (t + 1) * LANES)
            gate = jax.nn.sigmoid(projected[base : base + hidden, at])
            value = projected[base + hidden : base + 2 * hidden, at]
            found.append(gate * value * mask[t])
    for t, row in enumerate(pack_tiles(found)):
        put_device_rows(chunk_ref, SIDE_ROWS, t, row)
    put_device_rows(chunk_ref, SIDE_ROWS, 9, jnp.zeros((hidden, LANES), F32))
    out_ref[...] = chunk_ref[...].astype(BF16)


def ready_kernel(
    acts_hbm, gain_hbm, weight_hbm, cotangent_hbm, mask_hbm, out_weight_hbm, out_gain_hbm,
    normed_ref, back_norm_ref, gate_mask_ref, gate_coef_ref, coef_ref,
    acts_ref, gain_ref, weight_ref, cotangent_ref, mask_ref, out_weight_ref, out_gain_ref,
    spread_ref, back_out_ref, sems,
):
    na = acts_ref.shape[0]
    tiles = na // 2
    hidden = out_weight_ref.shape[0]
    copies = [
        pltpu.make_async_copy(acts_hbm, acts_ref, sems.at[0]),
        pltpu.make_async_copy(gain_hbm, gain_ref, sems.at[1]),
        pltpu.make_async_copy(weight_hbm, weight_ref, sems.at[2]),
        pltpu.make_async_copy(cotangent_hbm, cotangent_ref, sems.at[3]),
        pltpu.make_async_copy(mask_hbm, mask_ref, sems.at[4]),
        pltpu.make_async_copy(out_weight_hbm, out_weight_ref, sems.at[5]),
        pltpu.make_async_copy(out_gain_hbm, out_gain_ref, sems.at[6]),
    ]
    for copy in copies:
        copy.start()
    for copy in copies:
        copy.wait()
    spread(acts_ref, spread_ref)
    norm_tiles(spread_ref, gain_ref, normed_ref)
    spread(cotangent_ref, spread_ref)
    projected = matmul(weight_ref[...], normed_ref[...], TN)
    for t in range(tiles):
        at = slice(t * LANES, (t + 1) * LANES)
        mask = mask_ref[:, at]
        gate = jax.nn.sigmoid(projected[4 * hidden :, at])
        gate_mask = gate * mask
        cotangent = spread_ref[at, :].T
        gate_mask_ref[:, at] = gate_mask
        gate_coef_ref[:, at] = cotangent * gate_mask * (1.0 - gate)
        back_out_ref[:, at] = (cotangent * gate_mask).astype(BF16)
        for base in (0, 2 * hidden):
            gate = jax.nn.sigmoid(projected[base : base + hidden, at])
            value = projected[base + hidden : base + 2 * hidden, at]
            coef_ref[base : base + hidden, at] = value * gate * (1.0 - gate) * mask
            coef_ref[base + hidden : base + 2 * hidden, at] = gate * mask
    out_gain = column(out_gain_ref)
    back_norm = matmul(out_weight_ref[...], back_out_ref[...])
    for t in range(tiles):
        at = slice(t * LANES, (t + 1) * LANES)
        back_norm_ref[:, at] = back_norm[:, at] * out_gain
    back_norm_ref[:, tiles * LANES : (tiles + 1) * LANES] = out_gain
    back_norm_ref[:, (tiles + 1) * LANES :] = out_weight_ref[...].astype(F32)


def order_kernel(na, order_ref):
    order_ref[...] = token_order(na, order_ref.shape[1])


def side_rows(chunk_ref, lo, pair):
    return [
        unpack_tiles([chunk_ref[group_rows(SIDE_ROWS, lo, col, t), :] for t in range(9)])
        for col in (2 * pair, 2 * pair + 1)
    ]


def side_plane(na, chunk_ref, sides):
    tiles = na // 2
    for pair in range(4):
        at = slice(pair * LANES, (pair + 1) * LANES)
        for lo in range(2):
            even, odd = side_rows(chunk_ref, lo, pair)
            for side, plane_ref in sides.items():
                for t in range(tiles):
                    tile = plane_tile(even[side * tiles + t], odd[side * tiles + t])
                    plane_ref[plane_rows(na, lo, t), at] = tile.astype(BF16)


def token_sums(left_ref, right_ref, order_ref, rows):
    tri = matmul(left_ref[...], right_ref[...], NT).astype(BF16)
    return matmul(tri, order_ref[rows, :])


def own_sides_kernel(na, mine_ref, order_ref, left_ref, right_ref, tri_ref, chunk_ref):
    chunk_ref[...] = mine_ref[...].astype(F32)
    side_plane(na, chunk_ref, {0: left_ref, 1: right_ref})
    tri_ref[...] = token_sums(left_ref, right_ref, order_ref, slice(0, left_ref.shape[0]))


def left_kernel(na, theirs_ref, left_ref, chunk_ref):
    chunk_ref[...] = theirs_ref[...].astype(F32)
    side_plane(na, chunk_ref, {0: left_ref})


def tri_kernel(
    na, theirs_ref, left_ref, right_mine_ref, tri_mine_ref, order_ref, tri_ref, right_ref,
    chunk_ref, tri_chunk_ref,
):
    tiles = na // 2
    half = left_ref.shape[0]
    chunk_ref[...] = theirs_ref[...].astype(F32)
    right_ref[0:half, :] = right_mine_ref[...]
    theirs = right_ref.at[half : 2 * half]
    side_plane(na, chunk_ref, {1: theirs})
    tri = tri_mine_ref[...] + token_sums(left_ref, theirs, order_ref, slice(half, 2 * half))
    for pair in range(4):
        for lo in range(2):
            for t in range(tiles):
                both = chunk_tiles(tri[plane_rows(na, lo, t), pair * LANES : (pair + 1) * LANES])
                for side in range(2):
                    tri_chunk_ref[group_rows(TRI_ROWS, lo, 2 * pair + side, t), :] = both[side]
    tri_ref[...] = tri_chunk_ref[...].astype(BF16)


def middle_kernel(
    tri_ref, normed_ref, back_norm_ref, gate_coef_ref,
    back_ref, gate_ref, out_proj_ref,
    tri_chunk_ref, scaled_ref, normed_out_ref,
):
    tiles = normed_ref.shape[1] // LANES
    tri_chunk_ref[...] = tri_ref[...].astype(F32)
    out_gain = back_norm_ref[:, tiles * LANES : (tiles + 1) * LANES]
    out_weight = back_norm_ref[:, (tiles + 1) * LANES :].astype(BF16)
    inv_out = []
    for t in range(tiles):
        at = slice(t * LANES, (t + 1) * LANES)
        scaled, inv = tile_norm(device_rows(tri_chunk_ref, TRI_ROWS, t))
        inv_out.append(inv)
        scaled_ref[:, at] = scaled
        normed_out_ref[:, at] = (scaled * out_gain).astype(BF16)
    out_proj = matmul(out_weight, normed_out_ref[...], TN)
    out_proj_ref[...] = out_proj
    gate_ref[...] = (out_proj * gate_coef_ref[...]).astype(BF16)
    term = matmul(normed_ref[...], gate_ref[...], NT)
    free = gap(term.shape)
    for t in range(tiles):
        at = slice(t * LANES, (t + 1) * LANES)
        row = tile_norm_grad(back_norm_ref[:, at], scaled_ref[:, at], inv_out[t])
        if t < 4:
            moved = pltpu.roll(term, SLOT - PIECE - PIECE * t, 1) if t < 3 else term
            row = jnp.where(free, moved, row)
        put_device_rows(tri_chunk_ref, TRI_ROWS, t, row)
    back_ref[...] = tri_chunk_ref[...].astype(BF16)


def update_kernel(gate_mask_ref, out_proj_ref, update_ref):
    for t in range(update_ref.shape[0] // 2):
        at = slice(t * LANES, (t + 1) * LANES)
        store_pairs(update_ref, t, gate_mask_ref[:, at] * out_proj_ref[:, at])


def back_plane(na, chunk_ref, plane_ref):
    free = gap((8, LANES))
    for pair in range(4):
        for lo in range(2):
            for t in range(na // 2):
                even, odd = [
                    jnp.where(free, 0.0, chunk_ref[group_rows(TRI_ROWS, lo, col, t), :])
                    for col in (2 * pair, 2 * pair + 1)
                ]
                plane_ref[plane_rows(na, lo, t), pair * LANES : (pair + 1) * LANES] = plane_tile(
                    even, odd
                ).astype(BF16)


def gap_total(chunk_ref):
    place = lax.broadcasted_iota(jnp.int32, (8, LANES), 1) % SLOT // PIECE
    total = jnp.zeros((8, LANES), F32)
    for t in range(4):
        rows = jnp.zeros((8, LANES), F32)
        for m in range(chunk_ref.shape[0] // (8 * TRI_ROWS)):
            rows += chunk_ref[pl.ds(8 * TRI_ROWS * m + t, 8, stride=TRI_ROWS), :]
        rows = jnp.broadcast_to(jnp.sum(rows, axis=0, keepdims=True), (8, LANES))
        if t < 3:
            rows = pltpu.roll(rows, LANES - (SLOT - PIECE) + PIECE * t, 1)
        total = jnp.where(place == t, rows, total)
    return total


def own_back_kernel(
    na, mine_ref, left_ref, right_ref, order_ref, back_left_ref, back_right_ref, total_ref,
    chunk_ref, plane_ref, turned_ref,
):
    half = left_ref.shape[0]
    chunk_ref[...] = mine_ref[...].astype(F32)
    back_plane(na, chunk_ref, plane_ref)
    turned_ref[...] = matmul(plane_ref[...], order_ref[...], NT).astype(BF16)
    back_left_ref[...] = matmul(turned_ref[...], right_ref[...])
    back_right_ref[...] = matmul(turned_ref[:, 0:half], left_ref[...], TN)
    total_ref[...] = gap_total(chunk_ref)


def back_kernel(
    na, theirs_ref, back_left_ref, back_right_ref, total_ref, left_ref, order_ref, out_ref,
    back_chunk_ref, chunk_ref, plane_ref, turned_ref,
):
    tiles = na // 2
    half = left_ref.shape[0]
    back_chunk_ref[...] = theirs_ref[...].astype(F32)
    back_plane(na, back_chunk_ref, plane_ref)
    turned_ref[...] = matmul(plane_ref[...], order_ref[0:half, :], NT).astype(BF16)
    back_right = back_right_ref[...] + matmul(turned_ref[...], left_ref[...], TN)
    total = (total_ref[...] + gap_total(back_chunk_ref)) / (4 * 8 * na)
    for m in range(chunk_ref.shape[0] // (8 * SIDE_ROWS)):
        chunk_ref[pl.ds(8 * SIDE_ROWS * m + 9, 8, stride=SIDE_ROWS), :] = total
    for pair in range(4):
        at = slice(pair * LANES, (pair + 1) * LANES)
        for lo in range(2):
            found = [chunk_tiles(back_left_ref[plane_rows(na, lo, t), at]) for t in range(tiles)]
            found += [chunk_tiles(back_right[plane_rows(na, lo, t), at]) for t in range(tiles)]
            for side in range(2):
                for t, row in enumerate(pack_tiles([both[side] for both in found])):
                    chunk_ref[group_rows(SIDE_ROWS, lo, 2 * pair + side, t), :] = row
    out_ref[...] = chunk_ref[...].astype(BF16)


def weight_kernel(
    back_ref, normed_ref, coef_ref, gate_ref, term_ref, back_proj_ref, gate_total_ref,
    chunk_ref, term_chunk_ref,
):
    tiles = normed_ref.shape[1] // LANES
    hidden = normed_ref.shape[0]
    chunk_ref[...] = back_ref[...].astype(F32)
    gate_total_ref[...] = device_rows(chunk_ref, SIDE_ROWS, 9)
    back_proj_ref[4 * hidden :, :] = gate_ref[...]
    upstreams = unpack_tiles([device_rows(chunk_ref, SIDE_ROWS, t) for t in range(9)])
    for side in range(2):
        for t in range(tiles):
            at = slice(t * LANES, (t + 1) * LANES)
            for base in (2 * side * hidden, (2 * side + 1) * hidden):
                rows = slice(base, base + hidden)
                back_proj_ref[rows, at] = (upstreams[tiles * side + t] * coef_ref[rows, at]).astype(BF16)
    term = matmul(normed_ref[...], back_proj_ref[0 : 4 * hidden, :], NT)
    for t in range(4):
        for m in range(hidden // 8):
            term_chunk_ref[weight_rows(m, t), :] = term[8 * m : 8 * m + 8, t * LANES : (t + 1) * LANES]
    term_ref[...] = term_chunk_ref[...].astype(BF16)


def weight_rows(chip, t):
    return pl.ds(2 * (16 * chip + 8 * (t // 2)) + t % 2, 8, stride=2)


def sum_kernel(full_len, parts_ref, out_ref):
    total = jnp.zeros((16, LANES), F32)
    for m in range(parts_ref.shape[0] // 16):
        total += parts_ref[16 * m : 16 * m + 16, :].astype(F32)
    total = total[0:8] + total[8:16]
    total = total + pltpu.roll(total, 4, 0)
    total = total + pltpu.roll(total, 2, 0)
    total = total / full_len
    total = jnp.concatenate([total, total], axis=0).astype(BF16)
    for m in range(out_ref.shape[0] // 16):
        out_ref[16 * m : 16 * m + 16, :] = total


def grad_weight_kernel(sums_ref, gate_total_ref, out_ref, chunk_ref):
    chunk_ref[...] = sums_ref[...].astype(F32)
    for t in range(4):
        for m in range(out_ref.shape[0] // 8):
            out_ref[8 * m : 8 * m + 8, t * LANES : (t + 1) * LANES] = chunk_ref[weight_rows(m, t), :]
    out_ref[:, 4 * LANES :] = gate_total_ref[...]


def pair_kernel(acts_ref, gain_ref, weight_ref, back_proj_ref, grad_pair_ref, spread_ref):
    na, nb, _ = acts_ref.shape
    spread(acts_ref, spread_ref)
    gain = column(gain_ref)
    back_normed = matmul(weight_ref[...], back_proj_ref[...])
    for t in range(na // 2):
        at = slice(t * LANES, (t + 1) * LANES)
        scaled, inv = tile_norm(spread_ref[at, :].T)
        store_pairs(grad_pair_ref, t, tile_norm_grad(back_normed[:, at] * gain, scaled, inv))


def local_call(body, outs, scratch, flops, inputs, space=pltpu.VMEM, limit=VMEM_LIMIT):
    return pl.pallas_call(
        body,
        out_shape=outs,
        in_specs=[pl.BlockSpec(memory_space=space)] * inputs,
        out_specs=jax.tree.map(lambda _: pl.BlockSpec(memory_space=pltpu.VMEM), outs),
        scratch_shapes=scratch,
        compiler_params=pltpu.CompilerParams(vmem_limit_bytes=limit),
        cost_estimate=pl.CostEstimate(flops=flops, bytes_accessed=2_000_000, transcendentals=0),
    )


def exchange(chunks, depth, axes):
    devices = chunks.shape[0] // depth
    split = chunks.reshape(devices, depth // 2, 2, chunks.shape[1])
    return lax.all_to_all(split, axes, 0, 0, tiled=True).reshape(chunks.shape)


def other_core(values):
    return lax.ppermute(values, "core", [(0, 1), (1, 0)])


def array(shape, dtype=BF16):
    return jax.ShapeDtypeStruct(shape, dtype)


def per_device(pair_acts, token_valid, norm_gain, proj_weight, out_gain, out_weight, out_cotangent):
    na, _, channels = pair_acts.shape
    hidden = out_weight.shape[0]
    width_all = proj_weight.shape[1]
    full_len = token_valid.shape[0]
    lanes = na // 2 * LANES
    plane = (full_len, 8 * SLOT)
    sides_chunk = (hidden * SIDE_ROWS, LANES)
    tri_chunk = (hidden * TRI_ROWS, LANES)
    term_chunk = (4 * hidden, LANES)
    gain = norm_gain.reshape(1, channels)
    out_gain = out_gain.reshape(1, hidden)
    spread_scratch = pltpu.VMEM((lanes, channels), F32)

    sides, mask = local_call(
        sides_kernel,
        (array(sides_chunk), array((1, lanes), F32)),
        [
            pltpu.SMEM(token_valid.shape, jnp.int32),
            pltpu.VMEM(pair_acts.shape, BF16),
            pltpu.VMEM(gain.shape, F32),
            pltpu.VMEM(proj_weight.shape, BF16),
            spread_scratch,
            pltpu.VMEM((channels, lanes), BF16),
            pltpu.VMEM(sides_chunk, F32),
            pltpu.SemaphoreType.DMA((4,)),
        ],
        100_000_000,
        4,
        pltpu.HBM,
        WHOLE_VMEM,
    )(token_valid, pair_acts, gain, proj_weight)
    mine = exchange(sides, SIDE_ROWS, CHANNEL_AXES)
    order = local_call(functools.partial(order_kernel, na), array(plane), [], 1_000_000_000, 0)()
    normed, back_norm, gate_mask, gate_coef, coef = local_call(
        ready_kernel,
        (
            array((channels, lanes)),
            array((hidden, lanes + 2 * LANES), F32),
            array((channels, lanes), F32),
            array((channels, lanes), F32),
            array((4 * hidden, lanes), F32),
        ),
        [
            pltpu.VMEM(pair_acts.shape, BF16),
            pltpu.VMEM(gain.shape, F32),
            pltpu.VMEM(proj_weight.shape, BF16),
            pltpu.VMEM(out_cotangent.shape, BF16),
            pltpu.VMEM(mask.shape, F32),
            pltpu.VMEM(out_weight.shape, BF16),
            pltpu.VMEM(out_gain.shape, F32),
            spread_scratch,
            pltpu.VMEM((channels, lanes), BF16),
            pltpu.SemaphoreType.DMA((7,)),
        ],
        1_000_000_000,
        7,
        pltpu.HBM,
        READY_VMEM,
    )(pair_acts, gain, proj_weight, out_cotangent, mask, out_weight, out_gain)
    mine, normed, order = lax.optimization_barrier((mine, normed, order))
    half_plane = (full_len // 2, plane[1])
    theirs = other_core(mine)
    left_mine, right_mine, tri_mine = local_call(
        functools.partial(own_sides_kernel, na),
        (array(half_plane), array(half_plane), array(half_plane, F32)),
        [pltpu.VMEM(sides_chunk, F32)],
        1_000_000_000,
        2,
    )(mine, order)
    tri, right = local_call(
        functools.partial(tri_kernel, na),
        (array(tri_chunk), array(plane)),
        [pltpu.VMEM(sides_chunk, F32), pltpu.VMEM(tri_chunk, F32)],
        300_000_000,
        5,
    )(theirs, left_mine, right_mine, tri_mine, order)
    tri = exchange(tri, TRI_ROWS, CHANNEL_AXES)
    back, gate, out_proj = local_call(
        middle_kernel,
        (array(tri_chunk), array((channels, lanes)), array((channels, lanes), F32)),
        [
            pltpu.VMEM(tri_chunk, F32),
            pltpu.VMEM((hidden, lanes), F32),
            pltpu.VMEM((hidden, lanes), BF16),
        ],
        100_000_000,
        4,
    )(tri, normed, back_norm, gate_coef)
    back = exchange(back, TRI_ROWS, CHANNEL_AXES)
    side_theirs, back = lax.optimization_barrier((theirs, back))
    update = local_call(update_kernel, array(pair_acts.shape), [], 1_000_000_000, 2)(
        gate_mask, out_proj
    )
    theirs = other_core(back)
    left_theirs = local_call(
        functools.partial(left_kernel, na),
        array(half_plane),
        [pltpu.VMEM(sides_chunk, F32)],
        1_000_000_000,
        1,
    )(side_theirs)
    back_left, back_right, total = local_call(
        functools.partial(own_back_kernel, na),
        (array(half_plane, F32), array(half_plane, F32), array((8, LANES), F32)),
        [
            pltpu.VMEM(tri_chunk, F32),
            pltpu.VMEM(half_plane, BF16),
            pltpu.VMEM((full_len // 2, full_len), BF16),
        ],
        1_000_000_000,
        4,
    )(back, left_mine, right, order)
    back_sides = local_call(
        functools.partial(back_kernel, na),
        array(sides_chunk),
        [
            pltpu.VMEM(tri_chunk, F32),
            pltpu.VMEM(sides_chunk, F32),
            pltpu.VMEM(half_plane, BF16),
            pltpu.VMEM((full_len // 2, full_len // 2), BF16),
        ],
        300_000_000,
        6,
    )(theirs, back_left, back_right, total, left_theirs, order)
    back_sides = exchange(back_sides, SIDE_ROWS, CHANNEL_AXES)
    term, back_proj, gate_total = local_call(
        weight_kernel,
        (array(term_chunk), array((width_all, lanes)), array((channels, channels), F32)),
        [pltpu.VMEM(sides_chunk, F32), pltpu.VMEM(term_chunk, F32)],
        200_000_000,
        4,
    )(back_sides, normed, coef, gate)
    grad_pair = local_call(
        pair_kernel, array(pair_acts.shape), [spread_scratch], 1_000_000_000, 4
    )(pair_acts, gain, proj_weight, back_proj)
    parts = exchange(term, 2, ALL_AXES)
    sums = local_call(functools.partial(sum_kernel, full_len), array(term_chunk), [], 100_000, 1)(parts)
    sums = exchange(sums, 2, ALL_AXES)
    grad_weight = local_call(
        grad_weight_kernel,
        array((channels, width_all), F32),
        [pltpu.VMEM(term_chunk, F32)],
        100_000,
        2,
    )(sums, gate_total)
    return update, grad_pair, grad_weight


def solution(mesh):
    rows, cols = mesh.devices.shape
    split = Mesh(mesh.devices.reshape(rows // 2, 2, cols), ("chip", "core", "col"))
    pairs = P(("chip", "core"), "col", None)
    return jax.shard_map(
        per_device,
        mesh=split,
        in_specs=(pairs, P(), P(), P(), P(), P(), pairs),
        out_specs=(pairs, pairs, P()),
        check_vma=False,
    )
```

```python
import functools

import jax
import jax.numpy as jnp
from jax import lax
from jax.experimental import pallas as pl
from jax.experimental.pallas import tpu as pltpu
from jax.sharding import Mesh
from jax.sharding import PartitionSpec as P

EPSILON = 1e-05
BF16 = jnp.bfloat16
F32 = jnp.float32
ALL_AXES = ("chip", "core", "col")
CHANNEL_AXES = ("col", "chip")
LANES = 128
SLOT = 64
PIECE = 16
SIDE_ROWS = 10
TRI_ROWS = 6
VMEM_LIMIT = 48 * 1024 * 1024
WHOLE_VMEM = 64 * 1024 * 1024 - 65536
READY_VMEM = 62 * 1024 * 1024

NT = (((1,), (1,)), ((), ()))
NN = (((1,), (0,)), ((), ()))
TN = (((0,), (0,)), ((), ()))


def matmul(lhs, rhs, dims=NN):
    return lax.dot_general(lhs, rhs, dims, preferred_element_type=F32)


def column(row_ref):
    return jnp.broadcast_to(row_ref[...], (LANES, LANES)).T


def swap_halves(values):
    return pltpu.roll(values, SLOT, 1)


def low_half(shape):
    return lax.broadcasted_iota(jnp.int32, shape, 1) < SLOT


def spread(pairs_ref, spread_ref):
    na, nb, channels = pairs_ref.shape
    for a in range(na):
        spread_ref[a * SLOT : a * SLOT + nb, :] = pairs_ref[a]
        spread_ref[a * SLOT + nb : (a + 1) * SLOT, :] = jnp.zeros((SLOT - nb, channels), BF16)


def store_pairs(out_ref, t, values):
    nb = out_ref.shape[1]
    turned = values.T
    out_ref[2 * t] = turned[0:nb].astype(out_ref.dtype)
    out_ref[2 * t + 1] = turned[SLOT : SLOT + nb].astype(out_ref.dtype)


def masks(valid_ref, na, nb):
    lane = lax.broadcasted_iota(jnp.int32, (1, LANES), 1)
    place = lane % SLOT
    first_row = (2 * lax.axis_index("chip") + lax.axis_index("core")) * na
    first_col = lax.axis_index("col") * nb
    cols = jnp.zeros((1, LANES), jnp.int32)
    for b in range(nb):
        cols = jnp.where(place == b, valid_ref[first_col + b], cols)
    found = []
    for t in range(na // 2):
        rows = jnp.where(lane < SLOT, valid_ref[first_row + 2 * t], valid_ref[first_row + 2 * t + 1])
        found.append((rows * cols).astype(F32))
    return found


def tile_norm(values):
    center = jnp.mean(values, axis=0, keepdims=True)
    shifted = values - center
    inv_std = lax.rsqrt(jnp.mean(shifted * shifted, axis=0, keepdims=True) + EPSILON)
    return shifted * inv_std, inv_std


def tile_norm_grad(upstream, scaled, inv_std):
    first = jnp.mean(upstream, axis=0, keepdims=True)
    second = jnp.mean(upstream * scaled, axis=0, keepdims=True)
    return inv_std * (upstream - first - scaled * second)


def norm_tiles(spread_ref, gain_ref, normed_ref):
    gain = column(gain_ref)
    tiles = spread_ref.shape[0] // LANES
    for t in range(tiles):
        at = slice(t * LANES, (t + 1) * LANES)
        scaled, _ = tile_norm(spread_ref[at, :].T.astype(F32))
        normed_ref[:, at] = (scaled * gain).astype(BF16)


def gap(shape):
    return lax.broadcasted_iota(jnp.int32, shape, 1) % SLOT >= SLOT - PIECE


def pack_tiles(tiles):
    free = gap(tiles[0].shape)
    rows = []
    for t in range(9):
        moved = pltpu.roll(tiles[9 + t // 3], SLOT - PIECE - PIECE * (t % 3), 1)
        rows.append(jnp.where(free, moved, tiles[t]))
    return rows


def unpack_tiles(rows):
    free = gap(rows[0].shape)
    place = lax.broadcasted_iota(jnp.int32, rows[0].shape, 1) % SLOT // PIECE
    tiles = [jnp.where(free, 0.0, row) for row in rows]
    for m in range(3):
        tile = jnp.zeros_like(rows[0])
        for p in range(3):
            moved = pltpu.roll(rows[3 * m + p], LANES - (SLOT - PIECE) + PIECE * p, 1)
            tile = jnp.where(place == p, moved, tile)
        tiles.append(tile)
    return tiles


def device_rows(chunk_ref, depth, row):
    return chunk_ref[pl.ds(row, chunk_ref.shape[0] // depth, stride=depth), :]


def put_device_rows(chunk_ref, depth, row, values):
    chunk_ref[pl.ds(row, chunk_ref.shape[0] // depth, stride=depth), :] = values


def group_rows(depth, lo, col, row):
    return pl.ds(depth * (16 * col + lo) + row, 8, stride=2 * depth)


def plane_rows(na, lo, t):
    return slice(8 * (na * lo + 2 * t), 8 * (na * lo + 2 * t) + 16)


def plane_tile(even, odd):
    low = low_half(even.shape)
    upper = jnp.where(low, even, swap_halves(odd))
    lower = jnp.where(low, swap_halves(even), odd)
    return jnp.concatenate([upper, lower], axis=0)


def chunk_tiles(rows):
    upper, lower = rows[0:8], rows[8:16]
    low = low_half(upper.shape)
    return jnp.where(low, upper, swap_halves(lower)), jnp.where(low, swap_halves(upper), lower)


def token_order(na, plane):
    row = lax.broadcasted_iota(jnp.int32, (16 * 2 * na, plane), 0)
    token = lax.broadcasted_iota(jnp.int32, (16 * 2 * na, plane), 1)
    place = row // 8
    theirs = (place >= 2 * na).astype(jnp.int32)
    place = place - 2 * na * theirs
    core = lax.axis_index("core")
    core = core + theirs * (1 - 2 * core)
    lo = (place >= na).astype(jnp.int32)
    a = place - na * lo
    return (token == SLOT * (row % 8) + na * (2 * lo + core) + a).astype(F32).astype(BF16)


def sides_kernel(
    valid_hbm, acts_hbm, gain_hbm, weight_hbm, out_ref, mask_ref,
    valid_ref, acts_ref, gain_ref, weight_ref, spread_ref, normed_ref, chunk_ref, sems,
):
    na, nb, _ = acts_hbm.shape
    tiles = na // 2
    hidden = weight_hbm.shape[0]
    copies = [
        pltpu.make_async_copy(valid_hbm, valid_ref, sems.at[0]),
        pltpu.make_async_copy(acts_hbm, acts_ref, sems.at[1]),
        pltpu.make_async_copy(gain_hbm, gain_ref, sems.at[2]),
        pltpu.make_async_copy(weight_hbm, weight_ref, sems.at[3]),
    ]
    for copy in copies:
        copy.start()
    copies[0].wait()
    mask = masks(valid_ref, na, nb)
    for t in range(tiles):
        mask_ref[:, t * LANES : (t + 1) * LANES] = mask[t]
    copies[1].wait()
    spread(acts_ref, spread_ref)
    copies[2].wait()
    norm_tiles(spread_ref, gain_ref, normed_ref)
    copies[3].wait()
    projected = matmul(weight_ref[:, 0 : 4 * hidden], normed_ref[...], TN)
    found = []
    for side in range(2):
        base = 2 * side * hidden
        for t in range(tiles):
            at = slice(t * LANES, (t + 1) * LANES)
            gate = jax.nn.sigmoid(projected[base : base + hidden, at])
            value = projected[base + hidden : base + 2 * hidden, at]
            found.append(gate * value * mask[t])
    for t, row in enumerate(pack_tiles(found)):
        put_device_rows(chunk_ref, SIDE_ROWS, t, row)
    put_device_rows(chunk_ref, SIDE_ROWS, 9, jnp.zeros((hidden, LANES), F32))
    out_ref[...] = chunk_ref[...].astype(BF16)


def ready_kernel(
    acts_hbm, gain_hbm, weight_hbm, cotangent_hbm, mask_hbm, out_weight_hbm, out_gain_hbm,
    normed_ref, back_norm_ref, gate_mask_ref, gate_coef_ref, coef_ref,
    acts_ref, gain_ref, weight_ref, cotangent_ref, mask_ref, out_weight_ref, out_gain_ref,
    spread_ref, back_out_ref, sems,
):
    na = acts_ref.shape[0]
    tiles = na // 2
    hidden = out_weight_ref.shape[0]
    copies = [
        pltpu.make_async_copy(acts_hbm, acts_ref, sems.at[0]),
        pltpu.make_async_copy(gain_hbm, gain_ref, sems.at[1]),
        pltpu.make_async_copy(weight_hbm, weight_ref, sems.at[2]),
        pltpu.make_async_copy(cotangent_hbm, cotangent_ref, sems.at[3]),
        pltpu.make_async_copy(mask_hbm, mask_ref, sems.at[4]),
        pltpu.make_async_copy(out_weight_hbm, out_weight_ref, sems.at[5]),
        pltpu.make_async_copy(out_gain_hbm, out_gain_ref, sems.at[6]),
    ]
    for copy in copies:
        copy.start()
    for copy in copies:
        copy.wait()
    spread(acts_ref, spread_ref)
    norm_tiles(spread_ref, gain_ref, normed_ref)
    spread(cotangent_ref, spread_ref)
    projected = matmul(weight_ref[...], normed_ref[...], TN)
    for t in range(tiles):
        at = slice(t * LANES, (t + 1) * LANES)
        mask = mask_ref[:, at]
        gate = jax.nn.sigmoid(projected[4 * hidden :, at])
        gate_mask = gate * mask
        cotangent = spread_ref[at, :].T.astype(F32)
        gate_mask_ref[:, at] = gate_mask
        gate_coef_ref[:, at] = cotangent * gate_mask * (1.0 - gate)
        back_out_ref[:, at] = (cotangent * gate_mask).astype(BF16)
        for base in (0, 2 * hidden):
            gate = jax.nn.sigmoid(projected[base : base + hidden, at])
            value = projected[base + hidden : base + 2 * hidden, at]
            coef_ref[base : base + hidden, at] = value * gate * (1.0 - gate) * mask
            coef_ref[base + hidden : base + 2 * hidden, at] = gate * mask
    out_gain = column(out_gain_ref)
    back_norm = matmul(out_weight_ref[...], back_out_ref[...])
    for t in range(tiles):
        at = slice(t * LANES, (t + 1) * LANES)
        back_norm_ref[:, at] = back_norm[:, at] * out_gain
    back_norm_ref[:, tiles * LANES : (tiles + 1) * LANES] = out_gain
    back_norm_ref[:, (tiles + 1) * LANES :] = out_weight_ref[...].astype(F32)


def order_kernel(na, order_ref):
    order_ref[...] = token_order(na, order_ref.shape[1])


def side_rows(chunk_ref, lo, pair):
    return [
        unpack_tiles([chunk_ref[group_rows(SIDE_ROWS, lo, col, t), :] for t in range(9)])
        for col in (2 * pair, 2 * pair + 1)
    ]


def side_plane(na, chunk_ref, sides):
    tiles = na // 2
    for pair in range(4):
        at = slice(pair * LANES, (pair + 1) * LANES)
        for lo in range(2):
            even, odd = side_rows(chunk_ref, lo, pair)
            for side, plane_ref in sides.items():
                for t in range(tiles):
                    tile = plane_tile(even[side * tiles + t], odd[side * tiles + t])
                    plane_ref[plane_rows(na, lo, t), at] = tile.astype(BF16)


def token_sums(left_ref, right_ref, order_ref, rows):
    tri = matmul(left_ref[...], right_ref[...], NT).astype(BF16)
    return matmul(tri, order_ref[rows, :])


def own_sides_kernel(na, mine_ref, order_ref, left_ref, right_ref, tri_ref, chunk_ref):
    chunk_ref[...] = mine_ref[...].astype(F32)
    side_plane(na, chunk_ref, {0: left_ref, 1: right_ref})
    tri_ref[...] = token_sums(left_ref, right_ref, order_ref, slice(0, left_ref.shape[0]))


def left_kernel(na, theirs_ref, left_ref, chunk_ref):
    chunk_ref[...] = theirs_ref[...].astype(F32)
    side_plane(na, chunk_ref, {0: left_ref})


def tri_kernel(
    na, theirs_ref, left_ref, right_mine_ref, tri_mine_ref, order_ref, tri_ref, right_ref,
    chunk_ref, tri_chunk_ref,
):
    tiles = na // 2
    half = left_ref.shape[0]
    chunk_ref[...] = theirs_ref[...].astype(F32)
    right_ref[0:half, :] = right_mine_ref[...]
    theirs = right_ref.at[half : 2 * half]
    side_plane(na, chunk_ref, {1: theirs})
    tri = tri_mine_ref[...] + token_sums(left_ref, theirs, order_ref, slice(half, 2 * half))
    for pair in range(4):
        for lo in range(2):
            for t in range(tiles):
                both = chunk_tiles(tri[plane_rows(na, lo, t), pair * LANES : (pair + 1) * LANES])
                for side in range(2):
                    tri_chunk_ref[group_rows(TRI_ROWS, lo, 2 * pair + side, t), :] = both[side]
    tri_ref[...] = tri_chunk_ref[...].astype(BF16)


def middle_kernel(
    tri_ref, normed_ref, back_norm_ref, gate_coef_ref,
    back_ref, gate_ref, out_proj_ref,
    tri_chunk_ref, scaled_ref, normed_out_ref,
):
    tiles = normed_ref.shape[1] // LANES
    tri_chunk_ref[...] = tri_ref[...].astype(F32)
    out_gain = back_norm_ref[:, tiles * LANES : (tiles + 1) * LANES]
    out_weight = back_norm_ref[:, (tiles + 1) * LANES :].astype(BF16)
    inv_out = []
    for t in range(tiles):
        at = slice(t * LANES, (t + 1) * LANES)
        scaled, inv = tile_norm(device_rows(tri_chunk_ref, TRI_ROWS, t))
        inv_out.append(inv)
        scaled_ref[:, at] = scaled
        normed_out_ref[:, at] = (scaled * out_gain).astype(BF16)
    out_proj = matmul(out_weight, normed_out_ref[...], TN)
    out_proj_ref[...] = out_proj
    gate_ref[...] = (out_proj * gate_coef_ref[...]).astype(BF16)
    term = matmul(normed_ref[...], gate_ref[...], NT)
    free = gap(term.shape)
    for t in range(tiles):
        at = slice(t * LANES, (t + 1) * LANES)
        row = tile_norm_grad(back_norm_ref[:, at], scaled_ref[:, at], inv_out[t])
        if t < 4:
            moved = pltpu.roll(term, SLOT - PIECE - PIECE * t, 1) if t < 3 else term
            row = jnp.where(free, moved, row)
        put_device_rows(tri_chunk_ref, TRI_ROWS, t, row)
    back_ref[...] = tri_chunk_ref[...].astype(BF16)


def update_kernel(gate_mask_ref, out_proj_ref, update_ref):
    for t in range(update_ref.shape[0] // 2):
        at = slice(t * LANES, (t + 1) * LANES)
        store_pairs(update_ref, t, gate_mask_ref[:, at] * out_proj_ref[:, at])


def back_plane(na, chunk_ref, plane_ref):
    free = gap((8, LANES))
    for pair in range(4):
        for lo in range(2):
            for t in range(na // 2):
                even, odd = [
                    jnp.where(free, 0.0, chunk_ref[group_rows(TRI_ROWS, lo, col, t), :])
                    for col in (2 * pair, 2 * pair + 1)
                ]
                plane_ref[plane_rows(na, lo, t), pair * LANES : (pair + 1) * LANES] = plane_tile(
                    even, odd
                ).astype(BF16)


def gap_total(chunk_ref):
    place = lax.broadcasted_iota(jnp.int32, (8, LANES), 1) % SLOT // PIECE
    total = jnp.zeros((8, LANES), F32)
    for t in range(4):
        rows = jnp.zeros((8, LANES), F32)
        for m in range(chunk_ref.shape[0] // (8 * TRI_ROWS)):
            rows += chunk_ref[pl.ds(8 * TRI_ROWS * m + t, 8, stride=TRI_ROWS), :]
        rows = jnp.broadcast_to(jnp.sum(rows, axis=0, keepdims=True), (8, LANES))
        if t < 3:
            rows = pltpu.roll(rows, LANES - (SLOT - PIECE) + PIECE * t, 1)
        total = jnp.where(place == t, rows, total)
    return total


def own_back_kernel(
    na, mine_ref, left_ref, right_ref, order_ref, back_left_ref, back_right_ref, total_ref,
    chunk_ref, plane_ref, turned_ref,
):
    half = left_ref.shape[0]
    chunk_ref[...] = mine_ref[...].astype(F32)
    back_plane(na, chunk_ref, plane_ref)
    turned_ref[...] = matmul(plane_ref[...], order_ref[...], NT).astype(BF16)
    back_left_ref[...] = matmul(turned_ref[...], right_ref[...])
    back_right_ref[...] = matmul(turned_ref[:, 0:half], left_ref[...], TN)
    total_ref[...] = gap_total(chunk_ref)


def back_kernel(
    na, theirs_ref, back_left_ref, back_right_ref, total_ref, left_ref, order_ref, out_ref,
    back_chunk_ref, chunk_ref, plane_ref, turned_ref,
):
    tiles = na // 2
    half = left_ref.shape[0]
    back_chunk_ref[...] = theirs_ref[...].astype(F32)
    back_plane(na, back_chunk_ref, plane_ref)
    turned_ref[...] = matmul(plane_ref[...], order_ref[0:half, :], NT).astype(BF16)
    back_right = back_right_ref[...] + matmul(turned_ref[...], left_ref[...], TN)
    total = (total_ref[...] + gap_total(back_chunk_ref)) / (4 * 8 * na)
    for m in range(chunk_ref.shape[0] // (8 * SIDE_ROWS)):
        chunk_ref[pl.ds(8 * SIDE_ROWS * m + 9, 8, stride=SIDE_ROWS), :] = total
    for pair in range(4):
        at = slice(pair * LANES, (pair + 1) * LANES)
        for lo in range(2):
            found = [chunk_tiles(back_left_ref[plane_rows(na, lo, t), at]) for t in range(tiles)]
            found += [chunk_tiles(back_right[plane_rows(na, lo, t), at]) for t in range(tiles)]
            for side in range(2):
                for t, row in enumerate(pack_tiles([both[side] for both in found])):
                    chunk_ref[group_rows(SIDE_ROWS, lo, 2 * pair + side, t), :] = row
    out_ref[...] = chunk_ref[...].astype(BF16)


def weight_kernel(
    back_ref, normed_ref, coef_ref, gate_ref, term_ref, back_proj_ref, gate_total_ref,
    chunk_ref, term_chunk_ref,
):
    tiles = normed_ref.shape[1] // LANES
    hidden = normed_ref.shape[0]
    chunk_ref[...] = back_ref[...].astype(F32)
    gate_total_ref[...] = device_rows(chunk_ref, SIDE_ROWS, 9)
    back_proj_ref[4 * hidden :, :] = gate_ref[...]
    upstreams = unpack_tiles([device_rows(chunk_ref, SIDE_ROWS, t) for t in range(9)])
    for side in range(2):
        for t in range(tiles):
            at = slice(t * LANES, (t + 1) * LANES)
            for base in (2 * side * hidden, (2 * side + 1) * hidden):
                rows = slice(base, base + hidden)
                back_proj_ref[rows, at] = (upstreams[tiles * side + t] * coef_ref[rows, at]).astype(BF16)
    term = matmul(normed_ref[...], back_proj_ref[0 : 4 * hidden, :], NT)
    for t in range(4):
        for m in range(hidden // 8):
            term_chunk_ref[weight_rows(m, t), :] = term[8 * m : 8 * m + 8, t * LANES : (t + 1) * LANES]
    term_ref[...] = term_chunk_ref[...].astype(BF16)


def weight_rows(chip, t):
    return pl.ds(2 * (16 * chip + 8 * (t // 2)) + t % 2, 8, stride=2)


def sum_kernel(full_len, parts_ref, out_ref):
    total = jnp.zeros((16, LANES), F32)
    for m in range(parts_ref.shape[0] // 16):
        total += parts_ref[16 * m : 16 * m + 16, :].astype(F32)
    total = total[0:8] + total[8:16]
    total = total + pltpu.roll(total, 4, 0)
    total = total + pltpu.roll(total, 2, 0)
    total = total / full_len
    total = jnp.concatenate([total, total], axis=0).astype(BF16)
    for m in range(out_ref.shape[0] // 16):
        out_ref[16 * m : 16 * m + 16, :] = total


def grad_weight_kernel(sums_ref, gate_total_ref, out_ref, chunk_ref):
    chunk_ref[...] = sums_ref[...].astype(F32)
    for t in range(4):
        for m in range(out_ref.shape[0] // 8):
            out_ref[8 * m : 8 * m + 8, t * LANES : (t + 1) * LANES] = chunk_ref[weight_rows(m, t), :]
    out_ref[:, 4 * LANES :] = gate_total_ref[...]


def pair_kernel(acts_ref, gain_ref, weight_ref, back_proj_ref, grad_pair_ref, spread_ref):
    na, nb, _ = acts_ref.shape
    spread(acts_ref, spread_ref)
    gain = column(gain_ref)
    back_normed = matmul(weight_ref[...], back_proj_ref[...])
    for t in range(na // 2):
        at = slice(t * LANES, (t + 1) * LANES)
        scaled, inv = tile_norm(spread_ref[at, :].T.astype(F32))
        store_pairs(grad_pair_ref, t, tile_norm_grad(back_normed[:, at] * gain, scaled, inv))


def local_call(body, outs, scratch, flops, inputs, space=pltpu.VMEM, limit=VMEM_LIMIT):
    return pl.pallas_call(
        body,
        out_shape=outs,
        in_specs=[pl.BlockSpec(memory_space=space)] * inputs,
        out_specs=jax.tree.map(lambda _: pl.BlockSpec(memory_space=pltpu.VMEM), outs),
        scratch_shapes=scratch,
        compiler_params=pltpu.CompilerParams(vmem_limit_bytes=limit),
        cost_estimate=pl.CostEstimate(flops=flops, bytes_accessed=2_000_000, transcendentals=0),
    )


def exchange(chunks, depth, axes):
    devices = chunks.shape[0] // depth
    split = chunks.reshape(devices, depth // 2, 2, chunks.shape[1])
    return lax.all_to_all(split, axes, 0, 0, tiled=True).reshape(chunks.shape)


def other_core(values):
    return lax.ppermute(values, "core", [(0, 1), (1, 0)])


def array(shape, dtype=BF16):
    return jax.ShapeDtypeStruct(shape, dtype)


def per_device(pair_acts, token_valid, norm_gain, proj_weight, out_gain, out_weight, out_cotangent):
    na, _, channels = pair_acts.shape
    hidden = out_weight.shape[0]
    width_all = proj_weight.shape[1]
    full_len = token_valid.shape[0]
    lanes = na // 2 * LANES
    plane = (full_len, 8 * SLOT)
    sides_chunk = (hidden * SIDE_ROWS, LANES)
    tri_chunk = (hidden * TRI_ROWS, LANES)
    term_chunk = (4 * hidden, LANES)
    gain = norm_gain.reshape(1, channels)
    out_gain = out_gain.reshape(1, hidden)
    spread_scratch = pltpu.VMEM((lanes, channels), BF16)

    sides, mask = local_call(
        sides_kernel,
        (array(sides_chunk), array((1, lanes), F32)),
        [
            pltpu.SMEM(token_valid.shape, jnp.int32),
            pltpu.VMEM(pair_acts.shape, BF16),
            pltpu.VMEM(gain.shape, F32),
            pltpu.VMEM(proj_weight.shape, BF16),
            spread_scratch,
            pltpu.VMEM((channels, lanes), BF16),
            pltpu.VMEM(sides_chunk, F32),
            pltpu.SemaphoreType.DMA((4,)),
        ],
        100_000_000,
        4,
        pltpu.HBM,
        WHOLE_VMEM,
    )(token_valid, pair_acts, gain, proj_weight)
    mine = exchange(sides, SIDE_ROWS, CHANNEL_AXES)
    order = local_call(functools.partial(order_kernel, na), array(plane), [], 1_000_000_000, 0)()
    normed, back_norm, gate_mask, gate_coef, coef = local_call(
        ready_kernel,
        (
            array((channels, lanes)),
            array((hidden, lanes + 2 * LANES), F32),
            array((channels, lanes), F32),
            array((channels, lanes), F32),
            array((4 * hidden, lanes), F32),
        ),
        [
            pltpu.VMEM(pair_acts.shape, BF16),
            pltpu.VMEM(gain.shape, F32),
            pltpu.VMEM(proj_weight.shape, BF16),
            pltpu.VMEM(out_cotangent.shape, BF16),
            pltpu.VMEM(mask.shape, F32),
            pltpu.VMEM(out_weight.shape, BF16),
            pltpu.VMEM(out_gain.shape, F32),
            spread_scratch,
            pltpu.VMEM((channels, lanes), BF16),
            pltpu.SemaphoreType.DMA((7,)),
        ],
        1_000_000_000,
        7,
        pltpu.HBM,
        READY_VMEM,
    )(pair_acts, gain, proj_weight, out_cotangent, mask, out_weight, out_gain)
    mine, normed, order = lax.optimization_barrier((mine, normed, order))
    half_plane = (full_len // 2, plane[1])
    theirs = other_core(mine)
    left_mine, right_mine, tri_mine = local_call(
        functools.partial(own_sides_kernel, na),
        (array(half_plane), array(half_plane), array(half_plane, F32)),
        [pltpu.VMEM(sides_chunk, F32)],
        1_000_000_000,
        2,
    )(mine, order)
    tri, right = local_call(
        functools.partial(tri_kernel, na),
        (array(tri_chunk), array(plane)),
        [pltpu.VMEM(sides_chunk, F32), pltpu.VMEM(tri_chunk, F32)],
        300_000_000,
        5,
    )(theirs, left_mine, right_mine, tri_mine, order)
    tri = exchange(tri, TRI_ROWS, CHANNEL_AXES)
    back, gate, out_proj = local_call(
        middle_kernel,
        (array(tri_chunk), array((channels, lanes)), array((channels, lanes), F32)),
        [
            pltpu.VMEM(tri_chunk, F32),
            pltpu.VMEM((hidden, lanes), F32),
            pltpu.VMEM((hidden, lanes), BF16),
        ],
        100_000_000,
        4,
    )(tri, normed, back_norm, gate_coef)
    back = exchange(back, TRI_ROWS, CHANNEL_AXES)
    side_theirs, back = lax.optimization_barrier((theirs, back))
    update = local_call(update_kernel, array(pair_acts.shape), [], 1_000_000_000, 2)(
        gate_mask, out_proj
    )
    theirs = other_core(back)
    left_theirs = local_call(
        functools.partial(left_kernel, na),
        array(half_plane),
        [pltpu.VMEM(sides_chunk, F32)],
        1_000_000_000,
        1,
    )(side_theirs)
    back_left, back_right, total = local_call(
        functools.partial(own_back_kernel, na),
        (array(half_plane, F32), array(half_plane, F32), array((8, LANES), F32)),
        [
            pltpu.VMEM(tri_chunk, F32),
            pltpu.VMEM(half_plane, BF16),
            pltpu.VMEM((full_len // 2, full_len), BF16),
        ],
        1_000_000_000,
        4,
    )(back, left_mine, right, order)
    back_sides = local_call(
        functools.partial(back_kernel, na),
        array(sides_chunk),
        [
            pltpu.VMEM(tri_chunk, F32),
            pltpu.VMEM(sides_chunk, F32),
            pltpu.VMEM(half_plane, BF16),
            pltpu.VMEM((full_len // 2, full_len // 2), BF16),
        ],
        300_000_000,
        6,
    )(theirs, back_left, back_right, total, left_theirs, order)
    back_sides = exchange(back_sides, SIDE_ROWS, CHANNEL_AXES)
    term, back_proj, gate_total = local_call(
        weight_kernel,
        (array(term_chunk), array((width_all, lanes)), array((channels, channels), F32)),
        [pltpu.VMEM(sides_chunk, F32), pltpu.VMEM(term_chunk, F32)],
        200_000_000,
        4,
    )(back_sides, normed, coef, gate)
    grad_pair = local_call(
        pair_kernel, array(pair_acts.shape), [spread_scratch], 1_000_000_000, 4
    )(pair_acts, gain, proj_weight, back_proj)
    parts = exchange(term, 2, ALL_AXES)
    sums = local_call(functools.partial(sum_kernel, full_len), array(term_chunk), [], 100_000, 1)(parts)
    sums = exchange(sums, 2, ALL_AXES)
    grad_weight = local_call(
        grad_weight_kernel,
        array((channels, width_all), F32),
        [pltpu.VMEM(term_chunk, F32)],
        100_000,
        2,
    )(sums, gate_total)
    return update, grad_pair, grad_weight


def solution(mesh):
    rows, cols = mesh.devices.shape
    split = Mesh(mesh.devices.reshape(rows // 2, 2, cols), ("chip", "core", "col"))
    pairs = P(("chip", "core"), "col", None)
    return jax.shard_map(
        per_device,
        mesh=split,
        in_specs=(pairs, P(), P(), P(), P(), P(), pairs),
        out_specs=(pairs, pairs, P()),
        check_vma=False,
    )
```

```python
import functools

import jax
import jax.numpy as jnp
from jax import lax
from jax.experimental import pallas as pl
from jax.experimental.pallas import tpu as pltpu
from jax.sharding import Mesh
from jax.sharding import PartitionSpec as P

EPSILON = 1e-05
BF16 = jnp.bfloat16
F32 = jnp.float32
ALL_AXES = ("zh", "x", "col", "core")
CHANNEL_AXES = ("col", "x", "zh")
LANES = 128
SLOT = 64
PIECE = 16
SIDE_ROWS = 10
TRI_ROWS = 6
VMEM_LIMIT = 48 * 1024 * 1024
WHOLE_VMEM = 64 * 1024 * 1024 - 65536
READY_VMEM = 62 * 1024 * 1024

NT = (((1,), (1,)), ((), ()))
NN = (((1,), (0,)), ((), ()))
TN = (((0,), (0,)), ((), ()))


def matmul(lhs, rhs, dims=NN):
    return lax.dot_general(lhs, rhs, dims, preferred_element_type=F32)


def column(row_ref):
    return jnp.broadcast_to(row_ref[...], (LANES, LANES)).T


def swap_halves(values):
    return pltpu.roll(values, SLOT, 1)


def low_half(shape):
    return lax.broadcasted_iota(jnp.int32, shape, 1) < SLOT


def spread(pairs_ref, spread_ref):
    na, nb, channels = pairs_ref.shape
    for a in range(na):
        spread_ref[a * SLOT : a * SLOT + nb, :] = pairs_ref[a]
        spread_ref[a * SLOT + nb : (a + 1) * SLOT, :] = jnp.zeros((SLOT - nb, channels), BF16)


def store_pairs(out_ref, t, values):
    nb = out_ref.shape[1]
    turned = values.T
    out_ref[2 * t] = turned[0:nb].astype(out_ref.dtype)
    out_ref[2 * t + 1] = turned[SLOT : SLOT + nb].astype(out_ref.dtype)


def masks(valid_ref, na, nb):
    lane = lax.broadcasted_iota(jnp.int32, (1, LANES), 1)
    place = lane % SLOT
    first_row = lax.axis_index(("x", "zh", "core")) * na
    first_col = lax.axis_index("col") * nb
    cols = jnp.zeros((1, LANES), jnp.int32)
    for b in range(nb):
        cols = jnp.where(place == b, valid_ref[first_col + b], cols)
    found = []
    for t in range(na // 2):
        rows = jnp.where(lane < SLOT, valid_ref[first_row + 2 * t], valid_ref[first_row + 2 * t + 1])
        found.append((rows * cols).astype(F32))
    return found


def tile_norm(values):
    center = jnp.mean(values, axis=0, keepdims=True)
    shifted = values - center
    inv_std = lax.rsqrt(jnp.mean(shifted * shifted, axis=0, keepdims=True) + EPSILON)
    return shifted * inv_std, inv_std


def tile_norm_grad(upstream, scaled, inv_std):
    first = jnp.mean(upstream, axis=0, keepdims=True)
    second = jnp.mean(upstream * scaled, axis=0, keepdims=True)
    return inv_std * (upstream - first - scaled * second)


def norm_tiles(spread_ref, gain_ref, normed_ref):
    gain = column(gain_ref)
    tiles = spread_ref.shape[0] // LANES
    for t in range(tiles):
        at = slice(t * LANES, (t + 1) * LANES)
        scaled, _ = tile_norm(spread_ref[at, :].T.astype(F32))
        normed_ref[:, at] = (scaled * gain).astype(BF16)


def gap(shape):
    return lax.broadcasted_iota(jnp.int32, shape, 1) % SLOT >= SLOT - PIECE


def pack_tiles(tiles):
    free = gap(tiles[0].shape)
    rows = []
    for t in range(9):
        moved = pltpu.roll(tiles[9 + t // 3], SLOT - PIECE - PIECE * (t % 3), 1)
        rows.append(jnp.where(free, moved, tiles[t]))
    return rows


def unpack_tiles(rows):
    free = gap(rows[0].shape)
    place = lax.broadcasted_iota(jnp.int32, rows[0].shape, 1) % SLOT // PIECE
    tiles = [jnp.where(free, 0.0, row) for row in rows]
    for m in range(3):
        tile = jnp.zeros_like(rows[0])
        for p in range(3):
            moved = pltpu.roll(rows[3 * m + p], LANES - (SLOT - PIECE) + PIECE * p, 1)
            tile = jnp.where(place == p, moved, tile)
        tiles.append(tile)
    return tiles


def device_rows(chunk_ref, depth, row):
    return chunk_ref[pl.ds(row, chunk_ref.shape[0] // depth, stride=depth), :]


def put_device_rows(chunk_ref, depth, row, values):
    chunk_ref[pl.ds(row, chunk_ref.shape[0] // depth, stride=depth), :] = values


def group_rows(depth, lo, col, row):
    return pl.ds(depth * (16 * col + lo) + row, 8, stride=2 * depth)


def plane_rows(na, lo, t):
    return slice(8 * (na * lo + 2 * t), 8 * (na * lo + 2 * t) + 16)


def plane_tile(even, odd):
    low = low_half(even.shape)
    upper = jnp.where(low, even, swap_halves(odd))
    lower = jnp.where(low, swap_halves(even), odd)
    return jnp.concatenate([upper, lower], axis=0)


def chunk_tiles(rows):
    upper, lower = rows[0:8], rows[8:16]
    low = low_half(upper.shape)
    return jnp.where(low, upper, swap_halves(lower)), jnp.where(low, swap_halves(upper), lower)


def token_order(na, plane):
    row = lax.broadcasted_iota(jnp.int32, (16 * 2 * na, plane), 0)
    token = lax.broadcasted_iota(jnp.int32, (16 * 2 * na, plane), 1)
    place = row // 8
    theirs = (place >= 2 * na).astype(jnp.int32)
    place = place - 2 * na * theirs
    core = lax.axis_index("core")
    core = core + theirs * (1 - 2 * core)
    lo = (place >= na).astype(jnp.int32)
    a = place - na * lo
    return (token == SLOT * (row % 8) + na * (2 * lo + core) + a).astype(F32).astype(BF16)


def sides_kernel(
    valid_hbm, acts_hbm, gain_hbm, weight_hbm, out_ref, mask_ref,
    valid_ref, acts_ref, gain_ref, weight_ref, spread_ref, normed_ref, chunk_ref, sems,
):
    na, nb, _ = acts_hbm.shape
    tiles = na // 2
    hidden = weight_hbm.shape[0]
    copies = [
        pltpu.make_async_copy(valid_hbm, valid_ref, sems.at[0]),
        pltpu.make_async_copy(acts_hbm, acts_ref, sems.at[1]),
        pltpu.make_async_copy(gain_hbm, gain_ref, sems.at[2]),
        pltpu.make_async_copy(weight_hbm, weight_ref, sems.at[3]),
    ]
    for copy in copies:
        copy.start()
    copies[0].wait()
    mask = masks(valid_ref, na, nb)
    for t in range(tiles):
        mask_ref[:, t * LANES : (t + 1) * LANES] = mask[t]
    copies[1].wait()
    spread(acts_ref, spread_ref)
    copies[2].wait()
    norm_tiles(spread_ref, gain_ref, normed_ref)
    copies[3].wait()
    projected = matmul(weight_ref[:, 0 : 4 * hidden], normed_ref[...], TN)
    found = []
    for side in range(2):
        base = 2 * side * hidden
        for t in range(tiles):
            at = slice(t * LANES, (t + 1) * LANES)
            gate = jax.nn.sigmoid(projected[base : base + hidden, at])
            value = projected[base + hidden : base + 2 * hidden, at]
            found.append(gate * value * mask[t])
    for t, row in enumerate(pack_tiles(found)):
        put_device_rows(chunk_ref, SIDE_ROWS, t, row)
    put_device_rows(chunk_ref, SIDE_ROWS, 9, jnp.zeros((hidden, LANES), F32))
    out_ref[...] = chunk_ref[...].astype(BF16)


def ready_kernel(
    acts_hbm, gain_hbm, weight_hbm, cotangent_hbm, mask_hbm, out_weight_hbm, out_gain_hbm,
    normed_ref, back_norm_ref, gate_mask_ref, gate_coef_ref, coef_ref,
    acts_ref, gain_ref, weight_ref, cotangent_ref, mask_ref, out_weight_ref, out_gain_ref,
    spread_ref, back_out_ref, sems,
):
    na = acts_ref.shape[0]
    tiles = na // 2
    hidden = out_weight_ref.shape[0]
    copies = [
        pltpu.make_async_copy(acts_hbm, acts_ref, sems.at[0]),
        pltpu.make_async_copy(gain_hbm, gain_ref, sems.at[1]),
        pltpu.make_async_copy(weight_hbm, weight_ref, sems.at[2]),
        pltpu.make_async_copy(cotangent_hbm, cotangent_ref, sems.at[3]),
        pltpu.make_async_copy(mask_hbm, mask_ref, sems.at[4]),
        pltpu.make_async_copy(out_weight_hbm, out_weight_ref, sems.at[5]),
        pltpu.make_async_copy(out_gain_hbm, out_gain_ref, sems.at[6]),
    ]
    for copy in copies:
        copy.start()
    for copy in copies:
        copy.wait()
    spread(acts_ref, spread_ref)
    norm_tiles(spread_ref, gain_ref, normed_ref)
    spread(cotangent_ref, spread_ref)
    projected = matmul(weight_ref[...], normed_ref[...], TN)
    for t in range(tiles):
        at = slice(t * LANES, (t + 1) * LANES)
        mask = mask_ref[:, at]
        gate = jax.nn.sigmoid(projected[4 * hidden :, at])
        gate_mask = gate * mask
        cotangent = spread_ref[at, :].T.astype(F32)
        gate_mask_ref[:, at] = gate_mask
        gate_coef_ref[:, at] = cotangent * gate_mask * (1.0 - gate)
        back_out_ref[:, at] = (cotangent * gate_mask).astype(BF16)
        for base in (0, 2 * hidden):
            gate = jax.nn.sigmoid(projected[base : base + hidden, at])
            value = projected[base + hidden : base + 2 * hidden, at]
            coef_ref[base : base + hidden, at] = value * gate * (1.0 - gate) * mask
            coef_ref[base + hidden : base + 2 * hidden, at] = gate * mask
    out_gain = column(out_gain_ref)
    back_norm = matmul(out_weight_ref[...], back_out_ref[...])
    for t in range(tiles):
        at = slice(t * LANES, (t + 1) * LANES)
        back_norm_ref[:, at] = back_norm[:, at] * out_gain
    back_norm_ref[:, tiles * LANES : (tiles + 1) * LANES] = out_gain
    back_norm_ref[:, (tiles + 1) * LANES :] = out_weight_ref[...].astype(F32)


def order_kernel(na, order_ref):
    order_ref[...] = token_order(na, order_ref.shape[1])


def side_rows(chunk_ref, lo, pair):
    return [
        unpack_tiles([chunk_ref[group_rows(SIDE_ROWS, lo, col, t), :] for t in range(9)])
        for col in (2 * pair, 2 * pair + 1)
    ]


def side_plane(na, chunk_ref, sides):
    tiles = na // 2
    for pair in range(4):
        at = slice(pair * LANES, (pair + 1) * LANES)
        for lo in range(2):
            even, odd = side_rows(chunk_ref, lo, pair)
            for side, plane_ref in sides.items():
                for t in range(tiles):
                    tile = plane_tile(even[side * tiles + t], odd[side * tiles + t])
                    plane_ref[plane_rows(na, lo, t), at] = tile.astype(BF16)


def token_sums(left_ref, right_ref, order_ref, rows):
    tri = matmul(left_ref[...], right_ref[...], NT).astype(BF16)
    return matmul(tri, order_ref[rows, :])


def own_sides_kernel(na, mine_ref, order_ref, left_ref, right_ref, tri_ref, chunk_ref):
    chunk_ref[...] = mine_ref[...].astype(F32)
    side_plane(na, chunk_ref, {0: left_ref, 1: right_ref})
    tri_ref[...] = token_sums(left_ref, right_ref, order_ref, slice(0, left_ref.shape[0]))


def left_kernel(na, theirs_ref, left_ref, chunk_ref):
    chunk_ref[...] = theirs_ref[...].astype(F32)
    side_plane(na, chunk_ref, {0: left_ref})


def tri_kernel(
    na, theirs_ref, left_ref, right_mine_ref, tri_mine_ref, order_ref, tri_ref, right_ref,
    chunk_ref, tri_chunk_ref,
):
    tiles = na // 2
    half = left_ref.shape[0]
    chunk_ref[...] = theirs_ref[...].astype(F32)
    right_ref[0:half, :] = right_mine_ref[...]
    theirs = right_ref.at[half : 2 * half]
    side_plane(na, chunk_ref, {1: theirs})
    tri = tri_mine_ref[...] + token_sums(left_ref, theirs, order_ref, slice(half, 2 * half))
    for pair in range(4):
        for lo in range(2):
            for t in range(tiles):
                both = chunk_tiles(tri[plane_rows(na, lo, t), pair * LANES : (pair + 1) * LANES])
                for side in range(2):
                    tri_chunk_ref[group_rows(TRI_ROWS, lo, 2 * pair + side, t), :] = both[side]
    tri_ref[...] = tri_chunk_ref[...].astype(BF16)


def middle_kernel(
    tri_ref, normed_ref, back_norm_ref, gate_coef_ref,
    back_ref, gate_ref, out_proj_ref,
    tri_chunk_ref, scaled_ref, normed_out_ref,
):
    tiles = normed_ref.shape[1] // LANES
    tri_chunk_ref[...] = tri_ref[...].astype(F32)
    out_gain = back_norm_ref[:, tiles * LANES : (tiles + 1) * LANES]
    out_weight = back_norm_ref[:, (tiles + 1) * LANES :].astype(BF16)
    inv_out = []
    for t in range(tiles):
        at = slice(t * LANES, (t + 1) * LANES)
        scaled, inv = tile_norm(device_rows(tri_chunk_ref, TRI_ROWS, t))
        inv_out.append(inv)
        scaled_ref[:, at] = scaled
        normed_out_ref[:, at] = (scaled * out_gain).astype(BF16)
    out_proj = matmul(out_weight, normed_out_ref[...], TN)
    out_proj_ref[...] = out_proj
    gate_ref[...] = (out_proj * gate_coef_ref[...]).astype(BF16)
    term = matmul(normed_ref[...], gate_ref[...], NT)
    free = gap(term.shape)
    for t in range(tiles):
        at = slice(t * LANES, (t + 1) * LANES)
        row = tile_norm_grad(back_norm_ref[:, at], scaled_ref[:, at], inv_out[t])
        if t < 4:
            moved = pltpu.roll(term, SLOT - PIECE - PIECE * t, 1) if t < 3 else term
            row = jnp.where(free, moved, row)
        put_device_rows(tri_chunk_ref, TRI_ROWS, t, row)
    back_ref[...] = tri_chunk_ref[...].astype(BF16)


def update_kernel(gate_mask_ref, out_proj_ref, update_ref):
    for t in range(update_ref.shape[0] // 2):
        at = slice(t * LANES, (t + 1) * LANES)
        store_pairs(update_ref, t, gate_mask_ref[:, at] * out_proj_ref[:, at])


def back_plane(na, chunk_ref, plane_ref):
    free = gap((8, LANES))
    for pair in range(4):
        for lo in range(2):
            for t in range(na // 2):
                even, odd = [
                    jnp.where(free, 0.0, chunk_ref[group_rows(TRI_ROWS, lo, col, t), :])
                    for col in (2 * pair, 2 * pair + 1)
                ]
                plane_ref[plane_rows(na, lo, t), pair * LANES : (pair + 1) * LANES] = plane_tile(
                    even, odd
                ).astype(BF16)


def gap_total(chunk_ref):
    place = lax.broadcasted_iota(jnp.int32, (8, LANES), 1) % SLOT // PIECE
    total = jnp.zeros((8, LANES), F32)
    for t in range(4):
        rows = jnp.zeros((8, LANES), F32)
        for m in range(chunk_ref.shape[0] // (8 * TRI_ROWS)):
            rows += chunk_ref[pl.ds(8 * TRI_ROWS * m + t, 8, stride=TRI_ROWS), :]
        rows = jnp.broadcast_to(jnp.sum(rows, axis=0, keepdims=True), (8, LANES))
        if t < 3:
            rows = pltpu.roll(rows, LANES - (SLOT - PIECE) + PIECE * t, 1)
        total = jnp.where(place == t, rows, total)
    return total


def own_back_kernel(
    na, mine_ref, left_ref, right_ref, order_ref, back_left_ref, back_right_ref, total_ref,
    chunk_ref, plane_ref, turned_ref,
):
    half = left_ref.shape[0]
    chunk_ref[...] = mine_ref[...].astype(F32)
    back_plane(na, chunk_ref, plane_ref)
    turned_ref[...] = matmul(plane_ref[...], order_ref[...], NT).astype(BF16)
    back_left_ref[...] = matmul(turned_ref[...], right_ref[...])
    back_right_ref[...] = matmul(turned_ref[:, 0:half], left_ref[...], TN)
    total_ref[...] = gap_total(chunk_ref)


def back_kernel(
    na, theirs_ref, back_left_ref, back_right_ref, total_ref, left_ref, order_ref, out_ref,
    back_chunk_ref, chunk_ref, plane_ref, turned_ref,
):
    tiles = na // 2
    half = left_ref.shape[0]
    back_chunk_ref[...] = theirs_ref[...].astype(F32)
    back_plane(na, back_chunk_ref, plane_ref)
    turned_ref[...] = matmul(plane_ref[...], order_ref[0:half, :], NT).astype(BF16)
    back_right = back_right_ref[...] + matmul(turned_ref[...], left_ref[...], TN)
    total = (total_ref[...] + gap_total(back_chunk_ref)) / (4 * 8 * na)
    for m in range(chunk_ref.shape[0] // (8 * SIDE_ROWS)):
        chunk_ref[pl.ds(8 * SIDE_ROWS * m + 9, 8, stride=SIDE_ROWS), :] = total
    for pair in range(4):
        at = slice(pair * LANES, (pair + 1) * LANES)
        for lo in range(2):
            found = [chunk_tiles(back_left_ref[plane_rows(na, lo, t), at]) for t in range(tiles)]
            found += [chunk_tiles(back_right[plane_rows(na, lo, t), at]) for t in range(tiles)]
            for side in range(2):
                for t, row in enumerate(pack_tiles([both[side] for both in found])):
                    chunk_ref[group_rows(SIDE_ROWS, lo, 2 * pair + side, t), :] = row
    out_ref[...] = chunk_ref[...].astype(BF16)


def weight_kernel(
    back_ref, normed_ref, coef_ref, gate_ref, term_ref, back_proj_ref, gate_total_ref,
    chunk_ref, term_chunk_ref,
):
    tiles = normed_ref.shape[1] // LANES
    hidden = normed_ref.shape[0]
    chunk_ref[...] = back_ref[...].astype(F32)
    gate_total_ref[...] = device_rows(chunk_ref, SIDE_ROWS, 9)
    back_proj_ref[4 * hidden :, :] = gate_ref[...]
    upstreams = unpack_tiles([device_rows(chunk_ref, SIDE_ROWS, t) for t in range(9)])
    for side in range(2):
        for t in range(tiles):
            at = slice(t * LANES, (t + 1) * LANES)
            for base in (2 * side * hidden, (2 * side + 1) * hidden):
                rows = slice(base, base + hidden)
                back_proj_ref[rows, at] = (upstreams[tiles * side + t] * coef_ref[rows, at]).astype(BF16)
    term = matmul(normed_ref[...], back_proj_ref[0 : 4 * hidden, :], NT)
    for t in range(4):
        put_device_rows(term_chunk_ref, 4, t, term[:, t * LANES : (t + 1) * LANES])
    term_ref[...] = term_chunk_ref[...].astype(BF16)


def sum_kernel(full_len, parts_ref, out_ref):
    total = jnp.zeros((16, LANES), F32)
    for m in range(parts_ref.shape[0] // 16):
        total += parts_ref[16 * m : 16 * m + 16, :].astype(F32)
    total = total[0:8] + total[8:16]
    total = total + pltpu.roll(total, 4, 0)
    total = total + pltpu.roll(total, 2, 0)
    total = total / full_len
    total = jnp.concatenate([total, total], axis=0).astype(BF16)
    for m in range(out_ref.shape[0] // 16):
        out_ref[16 * m : 16 * m + 16, :] = total


def grad_weight_kernel(sums_ref, gate_total_ref, out_ref, chunk_ref):
    chunk_ref[...] = sums_ref[...].astype(F32)
    for t in range(4):
        out_ref[:, t * LANES : (t + 1) * LANES] = device_rows(chunk_ref, 4, t)
    out_ref[:, 4 * LANES :] = gate_total_ref[...]


def pair_kernel(acts_ref, gain_ref, weight_ref, back_proj_ref, grad_pair_ref, spread_ref):
    na, nb, _ = acts_ref.shape
    spread(acts_ref, spread_ref)
    gain = column(gain_ref)
    back_normed = matmul(weight_ref[...], back_proj_ref[...])
    for t in range(na // 2):
        at = slice(t * LANES, (t + 1) * LANES)
        scaled, inv = tile_norm(spread_ref[at, :].T.astype(F32))
        store_pairs(grad_pair_ref, t, tile_norm_grad(back_normed[:, at] * gain, scaled, inv))


def local_call(body, outs, scratch, flops, inputs, space=pltpu.VMEM, limit=VMEM_LIMIT):
    return pl.pallas_call(
        body,
        out_shape=outs,
        in_specs=[pl.BlockSpec(memory_space=space)] * inputs,
        out_specs=jax.tree.map(lambda _: pl.BlockSpec(memory_space=pltpu.VMEM), outs),
        scratch_shapes=scratch,
        compiler_params=pltpu.CompilerParams(vmem_limit_bytes=limit),
        cost_estimate=pl.CostEstimate(flops=flops, bytes_accessed=2_000_000, transcendentals=0),
    )


def exchange(chunks, depth, axes):
    devices = chunks.shape[0] // depth
    split = chunks.reshape(devices, depth // 2, 2, chunks.shape[1])
    return lax.all_to_all(split, axes, 0, 0, tiled=True).reshape(chunks.shape)


def other_core(values):
    return lax.ppermute(values, "core", [(0, 1), (1, 0)])


def array(shape, dtype=BF16):
    return jax.ShapeDtypeStruct(shape, dtype)


def per_device(pair_acts, token_valid, norm_gain, proj_weight, out_gain, out_weight, out_cotangent):
    na, _, channels = pair_acts.shape
    hidden = out_weight.shape[0]
    width_all = proj_weight.shape[1]
    full_len = token_valid.shape[0]
    lanes = na // 2 * LANES
    plane = (full_len, 8 * SLOT)
    sides_chunk = (hidden * SIDE_ROWS, LANES)
    tri_chunk = (hidden * TRI_ROWS, LANES)
    term_chunk = (4 * hidden, LANES)
    gain = norm_gain.reshape(1, channels)
    out_gain = out_gain.reshape(1, hidden)
    spread_scratch = pltpu.VMEM((lanes, channels), BF16)

    sides, mask = local_call(
        sides_kernel,
        (array(sides_chunk), array((1, lanes), F32)),
        [
            pltpu.SMEM(token_valid.shape, jnp.int32),
            pltpu.VMEM(pair_acts.shape, BF16),
            pltpu.VMEM(gain.shape, F32),
            pltpu.VMEM(proj_weight.shape, BF16),
            spread_scratch,
            pltpu.VMEM((channels, lanes), BF16),
            pltpu.VMEM(sides_chunk, F32),
            pltpu.SemaphoreType.DMA((4,)),
        ],
        100_000_000,
        4,
        pltpu.HBM,
        WHOLE_VMEM,
    )(token_valid, pair_acts, gain, proj_weight)
    mine = exchange(sides, SIDE_ROWS, CHANNEL_AXES)
    order = local_call(functools.partial(order_kernel, na), array(plane), [], 1_000_000_000, 0)()
    normed, back_norm, gate_mask, gate_coef, coef = local_call(
        ready_kernel,
        (
            array((channels, lanes)),
            array((hidden, lanes + 2 * LANES), F32),
            array((channels, lanes), F32),
            array((channels, lanes), F32),
            array((4 * hidden, lanes), F32),
        ),
        [
            pltpu.VMEM(pair_acts.shape, BF16),
            pltpu.VMEM(gain.shape, F32),
            pltpu.VMEM(proj_weight.shape, BF16),
            pltpu.VMEM(out_cotangent.shape, BF16),
            pltpu.VMEM(mask.shape, F32),
            pltpu.VMEM(out_weight.shape, BF16),
            pltpu.VMEM(out_gain.shape, F32),
            spread_scratch,
            pltpu.VMEM((channels, lanes), BF16),
            pltpu.SemaphoreType.DMA((7,)),
        ],
        1_000_000_000,
        7,
        pltpu.HBM,
        READY_VMEM,
    )(pair_acts, gain, proj_weight, out_cotangent, mask, out_weight, out_gain)
    mine, normed, order = lax.optimization_barrier((mine, normed, order))
    half_plane = (full_len // 2, plane[1])
    theirs = other_core(mine)
    left_mine, right_mine, tri_mine = local_call(
        functools.partial(own_sides_kernel, na),
        (array(half_plane), array(half_plane), array(half_plane, F32)),
        [pltpu.VMEM(sides_chunk, F32)],
        1_000_000_000,
        2,
    )(mine, order)
    tri, right = local_call(
        functools.partial(tri_kernel, na),
        (array(tri_chunk), array(plane)),
        [pltpu.VMEM(sides_chunk, F32), pltpu.VMEM(tri_chunk, F32)],
        300_000_000,
        5,
    )(theirs, left_mine, right_mine, tri_mine, order)
    tri = exchange(tri, TRI_ROWS, CHANNEL_AXES)
    back, gate, out_proj = local_call(
        middle_kernel,
        (array(tri_chunk), array((channels, lanes)), array((channels, lanes), F32)),
        [
            pltpu.VMEM(tri_chunk, F32),
            pltpu.VMEM((hidden, lanes), F32),
            pltpu.VMEM((hidden, lanes), BF16),
        ],
        100_000_000,
        4,
    )(tri, normed, back_norm, gate_coef)
    back = exchange(back, TRI_ROWS, CHANNEL_AXES)
    side_theirs, back = lax.optimization_barrier((theirs, back))
    update = local_call(update_kernel, array(pair_acts.shape), [], 1_000_000_000, 2)(
        gate_mask, out_proj
    )
    theirs = other_core(back)
    left_theirs = local_call(
        functools.partial(left_kernel, na),
        array(half_plane),
        [pltpu.VMEM(sides_chunk, F32)],
        1_000_000_000,
        1,
    )(side_theirs)
    back_left, back_right, total = local_call(
        functools.partial(own_back_kernel, na),
        (array(half_plane, F32), array(half_plane, F32), array((8, LANES), F32)),
        [
            pltpu.VMEM(tri_chunk, F32),
            pltpu.VMEM(half_plane, BF16),
            pltpu.VMEM((full_len // 2, full_len), BF16),
        ],
        1_000_000_000,
        4,
    )(back, left_mine, right, order)
    back_sides = local_call(
        functools.partial(back_kernel, na),
        array(sides_chunk),
        [
            pltpu.VMEM(tri_chunk, F32),
            pltpu.VMEM(sides_chunk, F32),
            pltpu.VMEM(half_plane, BF16),
            pltpu.VMEM((full_len // 2, full_len // 2), BF16),
        ],
        300_000_000,
        6,
    )(theirs, back_left, back_right, total, left_theirs, order)
    back_sides = exchange(back_sides, SIDE_ROWS, CHANNEL_AXES)
    term, back_proj, gate_total = local_call(
        weight_kernel,
        (array(term_chunk), array((width_all, lanes)), array((channels, channels), F32)),
        [pltpu.VMEM(sides_chunk, F32), pltpu.VMEM(term_chunk, F32)],
        200_000_000,
        4,
    )(back_sides, normed, coef, gate)
    grad_pair = local_call(
        pair_kernel, array(pair_acts.shape), [spread_scratch], 1_000_000_000, 4
    )(pair_acts, gain, proj_weight, back_proj)
    parts = exchange(term, 2, ALL_AXES)
    sums = local_call(functools.partial(sum_kernel, full_len), array(term_chunk), [], 100_000, 1)(parts)
    sums = exchange(sums, 2, ALL_AXES)
    grad_weight = local_call(
        grad_weight_kernel,
        array((channels, width_all), F32),
        [pltpu.VMEM(term_chunk, F32)],
        100_000,
        2,
    )(sums, gate_total)
    return update, grad_pair, grad_weight


def solution(mesh):
    rows, cols = mesh.devices.shape
    split = Mesh(mesh.devices.reshape(rows // 8, 4, 2, cols), ("x", "zh", "core", "col"))
    pairs = P(("x", "zh", "core"), "col", None)
    return jax.shard_map(
        per_device,
        mesh=split,
        in_specs=(pairs, P(), P(), P(), P(), P(), pairs),
        out_specs=(pairs, pairs, P()),
        check_vma=False,
    )
```

```python
import functools

import jax
import jax.numpy as jnp
from jax import lax
from jax.experimental import pallas as pl
from jax.experimental.pallas import tpu as pltpu
from jax.sharding import Mesh
from jax.sharding import PartitionSpec as P

EPSILON = 1e-05
BF16 = jnp.bfloat16
F32 = jnp.float32
ALL_AXES = ("chip", "core", "col")
CHANNEL_AXES = ("col", "chip")
LANES = 128
SLOT = 64
PIECE = 16
SIDE_ROWS = 10
TRI_ROWS = 6
VMEM_LIMIT = 48 * 1024 * 1024
WHOLE_VMEM = 64 * 1024 * 1024 - 65536
READY_VMEM = 62 * 1024 * 1024

NT = (((1,), (1,)), ((), ()))
NN = (((1,), (0,)), ((), ()))
TN = (((0,), (0,)), ((), ()))


def matmul(lhs, rhs, dims=NN):
    return lax.dot_general(lhs, rhs, dims, preferred_element_type=F32)


def column(row_ref):
    return jnp.broadcast_to(row_ref[...], (LANES, LANES)).T


def swap_halves(values):
    return pltpu.roll(values, SLOT, 1)


def low_half(shape):
    return lax.broadcasted_iota(jnp.int32, shape, 1) < SLOT


def spread(pairs_ref, spread_ref):
    na, nb, channels = pairs_ref.shape
    for a in range(na):
        spread_ref[a * SLOT : a * SLOT + nb, :] = pairs_ref[a]
        spread_ref[a * SLOT + nb : (a + 1) * SLOT, :] = jnp.zeros((SLOT - nb, channels), BF16)


def store_pairs(out_ref, t, values):
    nb = out_ref.shape[1]
    turned = values.T
    out_ref[2 * t] = turned[0:nb].astype(out_ref.dtype)
    out_ref[2 * t + 1] = turned[SLOT : SLOT + nb].astype(out_ref.dtype)


def masks(valid_ref, na, nb):
    lane = lax.broadcasted_iota(jnp.int32, (1, LANES), 1)
    place = lane % SLOT
    first_row = (2 * lax.axis_index("chip") + lax.axis_index("core")) * na
    first_col = lax.axis_index("col") * nb
    cols = jnp.zeros((1, LANES), jnp.int32)
    for b in range(nb):
        cols = jnp.where(place == b, valid_ref[first_col + b], cols)
    found = []
    for t in range(na // 2):
        rows = jnp.where(lane < SLOT, valid_ref[first_row + 2 * t], valid_ref[first_row + 2 * t + 1])
        found.append((rows * cols).astype(F32))
    return found


def tile_norm(values):
    center = jnp.mean(values, axis=0, keepdims=True)
    shifted = values - center
    inv_std = lax.rsqrt(jnp.mean(shifted * shifted, axis=0, keepdims=True) + EPSILON)
    return shifted * inv_std, inv_std


def tile_norm_grad(upstream, scaled, inv_std):
    first = jnp.mean(upstream, axis=0, keepdims=True)
    second = jnp.mean(upstream * scaled, axis=0, keepdims=True)
    return inv_std * (upstream - first - scaled * second)


def norm_tiles(spread_ref, gain_ref, normed_ref):
    gain = column(gain_ref)
    tiles = spread_ref.shape[0] // LANES
    for t in range(tiles):
        at = slice(t * LANES, (t + 1) * LANES)
        scaled, _ = tile_norm(spread_ref[at, :].T.astype(F32))
        normed_ref[:, at] = (scaled * gain).astype(BF16)


def gap(shape):
    return lax.broadcasted_iota(jnp.int32, shape, 1) % SLOT >= SLOT - PIECE


def pack_tiles(tiles):
    free = gap(tiles[0].shape)
    rows = []
    for t in range(9):
        moved = pltpu.roll(tiles[9 + t // 3], SLOT - PIECE - PIECE * (t % 3), 1)
        rows.append(jnp.where(free, moved, tiles[t]))
    return rows


def unpack_tiles(rows):
    free = gap(rows[0].shape)
    place = lax.broadcasted_iota(jnp.int32, rows[0].shape, 1) % SLOT // PIECE
    tiles = [jnp.where(free, 0.0, row) for row in rows]
    for m in range(3):
        tile = jnp.zeros_like(rows[0])
        for p in range(3):
            moved = pltpu.roll(rows[3 * m + p], LANES - (SLOT - PIECE) + PIECE * p, 1)
            tile = jnp.where(place == p, moved, tile)
        tiles.append(tile)
    return tiles


def device_rows(chunk_ref, depth, row):
    return chunk_ref[pl.ds(row, chunk_ref.shape[0] // depth, stride=depth), :]


def put_device_rows(chunk_ref, depth, row, values):
    chunk_ref[pl.ds(row, chunk_ref.shape[0] // depth, stride=depth), :] = values


def group_rows(depth, lo, col, row):
    return pl.ds(depth * (16 * col + lo) + row, 8, stride=2 * depth)


def plane_rows(na, lo, t):
    return slice(8 * (na * lo + 2 * t), 8 * (na * lo + 2 * t) + 16)


def plane_tile(even, odd):
    low = low_half(even.shape)
    upper = jnp.where(low, even, swap_halves(odd))
    lower = jnp.where(low, swap_halves(even), odd)
    return jnp.concatenate([upper, lower], axis=0)


def chunk_tiles(rows):
    upper, lower = rows[0:8], rows[8:16]
    low = low_half(upper.shape)
    return jnp.where(low, upper, swap_halves(lower)), jnp.where(low, swap_halves(upper), lower)


def token_order(na, plane):
    row = lax.broadcasted_iota(jnp.int32, (16 * 2 * na, plane), 0)
    token = lax.broadcasted_iota(jnp.int32, (16 * 2 * na, plane), 1)
    place = row // 8
    theirs = (place >= 2 * na).astype(jnp.int32)
    place = place - 2 * na * theirs
    core = lax.axis_index("core")
    core = core + theirs * (1 - 2 * core)
    lo = (place >= na).astype(jnp.int32)
    a = place - na * lo
    return (token == SLOT * (row % 8) + na * (2 * lo + core) + a).astype(F32).astype(BF16)


def sides_kernel(
    valid_hbm, acts_hbm, gain_hbm, weight_hbm, out_ref, mask_ref,
    valid_ref, acts_ref, gain_ref, weight_ref, spread_ref, normed_ref, chunk_ref, sems,
):
    na, nb, _ = acts_hbm.shape
    tiles = na // 2
    hidden = weight_hbm.shape[0]
    copies = [
        pltpu.make_async_copy(valid_hbm, valid_ref, sems.at[0]),
        pltpu.make_async_copy(acts_hbm, acts_ref, sems.at[1]),
        pltpu.make_async_copy(gain_hbm, gain_ref, sems.at[2]),
        pltpu.make_async_copy(weight_hbm, weight_ref, sems.at[3]),
    ]
    for copy in copies:
        copy.start()
    copies[0].wait()
    mask = masks(valid_ref, na, nb)
    for t in range(tiles):
        mask_ref[:, t * LANES : (t + 1) * LANES] = mask[t]
    copies[1].wait()
    spread(acts_ref, spread_ref)
    copies[2].wait()
    norm_tiles(spread_ref, gain_ref, normed_ref)
    copies[3].wait()
    projected = matmul(weight_ref[:, 0 : 4 * hidden], normed_ref[...], TN)
    found = []
    for side in range(2):
        base = 2 * side * hidden
        for t in range(tiles):
            at = slice(t * LANES, (t + 1) * LANES)
            gate = jax.nn.sigmoid(projected[base : base + hidden, at])
            value = projected[base + hidden : base + 2 * hidden, at]
            found.append(gate * value * mask[t])
    for t, row in enumerate(pack_tiles(found)):
        put_device_rows(chunk_ref, SIDE_ROWS, t, row)
    put_device_rows(chunk_ref, SIDE_ROWS, 9, jnp.zeros((hidden, LANES), F32))
    out_ref[...] = chunk_ref[...].astype(BF16)


def ready_kernel(
    acts_hbm, gain_hbm, weight_hbm, cotangent_hbm, mask_hbm, out_weight_hbm, out_gain_hbm,
    normed_ref, back_norm_ref, gate_mask_ref, gate_coef_ref, coef_ref,
    acts_ref, gain_ref, weight_ref, cotangent_ref, mask_ref, out_weight_ref, out_gain_ref,
    spread_ref, back_out_ref, sems,
):
    na = acts_ref.shape[0]
    tiles = na // 2
    hidden = out_weight_ref.shape[0]
    copies = [
        pltpu.make_async_copy(acts_hbm, acts_ref, sems.at[0]),
        pltpu.make_async_copy(gain_hbm, gain_ref, sems.at[1]),
        pltpu.make_async_copy(weight_hbm, weight_ref, sems.at[2]),
        pltpu.make_async_copy(cotangent_hbm, cotangent_ref, sems.at[3]),
        pltpu.make_async_copy(mask_hbm, mask_ref, sems.at[4]),
        pltpu.make_async_copy(out_weight_hbm, out_weight_ref, sems.at[5]),
        pltpu.make_async_copy(out_gain_hbm, out_gain_ref, sems.at[6]),
    ]
    for copy in copies:
        copy.start()
    for copy in copies:
        copy.wait()
    spread(acts_ref, spread_ref)
    norm_tiles(spread_ref, gain_ref, normed_ref)
    spread(cotangent_ref, spread_ref)
    projected = matmul(weight_ref[...], normed_ref[...], TN)
    for t in range(tiles):
        at = slice(t * LANES, (t + 1) * LANES)
        mask = mask_ref[:, at]
        gate = jax.nn.sigmoid(projected[4 * hidden :, at])
        gate_mask = gate * mask
        cotangent = spread_ref[at, :].T.astype(F32)
        gate_mask_ref[:, at] = gate_mask
        gate_coef_ref[:, at] = cotangent * gate_mask * (1.0 - gate)
        back_out_ref[:, at] = (cotangent * gate_mask).astype(BF16)
        for base in (0, 2 * hidden):
            gate = jax.nn.sigmoid(projected[base : base + hidden, at])
            value = projected[base + hidden : base + 2 * hidden, at]
            coef_ref[base : base + hidden, at] = value * gate * (1.0 - gate) * mask
            coef_ref[base + hidden : base + 2 * hidden, at] = gate * mask
    out_gain = column(out_gain_ref)
    back_norm = matmul(out_weight_ref[...], back_out_ref[...])
    for t in range(tiles):
        at = slice(t * LANES, (t + 1) * LANES)
        back_norm_ref[:, at] = back_norm[:, at] * out_gain
    back_norm_ref[:, tiles * LANES : (tiles + 1) * LANES] = out_gain
    back_norm_ref[:, (tiles + 1) * LANES :] = out_weight_ref[...].astype(F32)


def order_kernel(na, order_ref):
    order_ref[...] = token_order(na, order_ref.shape[1])


def side_rows(chunk_ref, lo, pair):
    return [
        unpack_tiles([chunk_ref[group_rows(SIDE_ROWS, lo, col, t), :] for t in range(9)])
        for col in (2 * pair, 2 * pair + 1)
    ]


def side_plane(na, chunk_ref, sides):
    tiles = na // 2
    for pair in range(4):
        at = slice(pair * LANES, (pair + 1) * LANES)
        for lo in range(2):
            even, odd = side_rows(chunk_ref, lo, pair)
            for side, plane_ref in sides.items():
                for t in range(tiles):
                    tile = plane_tile(even[side * tiles + t], odd[side * tiles + t])
                    plane_ref[plane_rows(na, lo, t), at] = tile.astype(BF16)


def token_sums(left_ref, right_ref, order_ref, rows):
    tri = matmul(left_ref[...], right_ref[...], NT).astype(BF16)
    return matmul(tri, order_ref[rows, :])


def own_sides_kernel(na, mine_ref, order_ref, left_ref, right_ref, tri_ref, chunk_ref):
    chunk_ref[...] = mine_ref[...].astype(F32)
    side_plane(na, chunk_ref, {0: left_ref, 1: right_ref})
    tri_ref[...] = token_sums(left_ref, right_ref, order_ref, slice(0, left_ref.shape[0]))


def left_kernel(na, theirs_ref, left_ref, chunk_ref):
    chunk_ref[...] = theirs_ref[...].astype(F32)
    side_plane(na, chunk_ref, {0: left_ref})


def tri_kernel(
    na, theirs_ref, left_ref, right_mine_ref, tri_mine_ref, order_ref, tri_ref, right_ref,
    chunk_ref, tri_chunk_ref,
):
    tiles = na // 2
    half = left_ref.shape[0]
    chunk_ref[...] = theirs_ref[...].astype(F32)
    right_ref[0:half, :] = right_mine_ref[...]
    theirs = right_ref.at[half : 2 * half]
    side_plane(na, chunk_ref, {1: theirs})
    tri = tri_mine_ref[...] + token_sums(left_ref, theirs, order_ref, slice(half, 2 * half))
    for pair in range(4):
        for lo in range(2):
            for t in range(tiles):
                both = chunk_tiles(tri[plane_rows(na, lo, t), pair * LANES : (pair + 1) * LANES])
                for side in range(2):
                    tri_chunk_ref[group_rows(TRI_ROWS, lo, 2 * pair + side, t), :] = both[side]
    tri_ref[...] = tri_chunk_ref[...].astype(BF16)


def middle_kernel(
    tri_ref, normed_ref, back_norm_ref, gate_coef_ref,
    back_ref, gate_ref, out_proj_ref,
    tri_chunk_ref, scaled_ref, normed_out_ref,
):
    tiles = normed_ref.shape[1] // LANES
    tri_chunk_ref[...] = tri_ref[...].astype(F32)
    out_gain = back_norm_ref[:, tiles * LANES : (tiles + 1) * LANES]
    out_weight = back_norm_ref[:, (tiles + 1) * LANES :].astype(BF16)
    inv_out = []
    for t in range(tiles):
        at = slice(t * LANES, (t + 1) * LANES)
        scaled, inv = tile_norm(device_rows(tri_chunk_ref, TRI_ROWS, t))
        inv_out.append(inv)
        scaled_ref[:, at] = scaled
        normed_out_ref[:, at] = (scaled * out_gain).astype(BF16)
    out_proj = matmul(out_weight, normed_out_ref[...], TN)
    out_proj_ref[...] = out_proj
    gate_ref[...] = (out_proj * gate_coef_ref[...]).astype(BF16)
    term = matmul(normed_ref[...], gate_ref[...], NT)
    free = gap(term.shape)
    for t in range(tiles):
        at = slice(t * LANES, (t + 1) * LANES)
        row = tile_norm_grad(back_norm_ref[:, at], scaled_ref[:, at], inv_out[t])
        if t < 4:
            moved = pltpu.roll(term, SLOT - PIECE - PIECE * t, 1) if t < 3 else term
            row = jnp.where(free, moved, row)
        put_device_rows(tri_chunk_ref, TRI_ROWS, t, row)
    back_ref[...] = tri_chunk_ref[...].astype(BF16)


def update_kernel(gate_mask_ref, out_proj_ref, update_ref):
    for t in range(update_ref.shape[0] // 2):
        at = slice(t * LANES, (t + 1) * LANES)
        store_pairs(update_ref, t, gate_mask_ref[:, at] * out_proj_ref[:, at])


def back_plane(na, chunk_ref, plane_ref):
    free = gap((8, LANES))
    for pair in range(4):
        for lo in range(2):
            for t in range(na // 2):
                even, odd = [
                    jnp.where(free, 0.0, chunk_ref[group_rows(TRI_ROWS, lo, col, t), :])
                    for col in (2 * pair, 2 * pair + 1)
                ]
                plane_ref[plane_rows(na, lo, t), pair * LANES : (pair + 1) * LANES] = plane_tile(
                    even, odd
                ).astype(BF16)


def gap_total(chunk_ref):
    place = lax.broadcasted_iota(jnp.int32, (8, LANES), 1) % SLOT // PIECE
    total = jnp.zeros((8, LANES), F32)
    for t in range(4):
        rows = jnp.zeros((8, LANES), F32)
        for m in range(chunk_ref.shape[0] // (8 * TRI_ROWS)):
            rows += chunk_ref[pl.ds(8 * TRI_ROWS * m + t, 8, stride=TRI_ROWS), :]
        rows = jnp.broadcast_to(jnp.sum(rows, axis=0, keepdims=True), (8, LANES))
        if t < 3:
            rows = pltpu.roll(rows, LANES - (SLOT - PIECE) + PIECE * t, 1)
        total = jnp.where(place == t, rows, total)
    return total


def own_back_kernel(
    na, mine_ref, left_ref, right_ref, order_ref, back_left_ref, back_right_ref, total_ref,
    chunk_ref, plane_ref, turned_ref,
):
    half = left_ref.shape[0]
    chunk_ref[...] = mine_ref[...].astype(F32)
    back_plane(na, chunk_ref, plane_ref)
    turned_ref[...] = matmul(plane_ref[...], order_ref[...], NT).astype(BF16)
    back_left_ref[...] = matmul(turned_ref[...], right_ref[...])
    back_right_ref[...] = matmul(turned_ref[:, 0:half], left_ref[...], TN)
    total_ref[...] = gap_total(chunk_ref)


def back_kernel(
    na, theirs_ref, back_left_ref, back_right_ref, total_ref, left_ref, order_ref, out_ref,
    back_chunk_ref, chunk_ref, plane_ref, turned_ref,
):
    tiles = na // 2
    half = left_ref.shape[0]
    back_chunk_ref[...] = theirs_ref[...].astype(F32)
    back_plane(na, back_chunk_ref, plane_ref)
    turned_ref[...] = matmul(plane_ref[...], order_ref[0:half, :], NT).astype(BF16)
    back_right = back_right_ref[...] + matmul(turned_ref[...], left_ref[...], TN)
    total = (total_ref[...] + gap_total(back_chunk_ref)) / (4 * 8 * na)
    for m in range(chunk_ref.shape[0] // (8 * SIDE_ROWS)):
        chunk_ref[pl.ds(8 * SIDE_ROWS * m + 9, 8, stride=SIDE_ROWS), :] = total
    for pair in range(4):
        at = slice(pair * LANES, (pair + 1) * LANES)
        for lo in range(2):
            found = [chunk_tiles(back_left_ref[plane_rows(na, lo, t), at]) for t in range(tiles)]
            found += [chunk_tiles(back_right[plane_rows(na, lo, t), at]) for t in range(tiles)]
            for side in range(2):
                for t, row in enumerate(pack_tiles([both[side] for both in found])):
                    chunk_ref[group_rows(SIDE_ROWS, lo, 2 * pair + side, t), :] = row
    out_ref[...] = chunk_ref[...].astype(BF16)


def weight_kernel(
    back_ref, normed_ref, coef_ref, gate_ref, term_ref, back_proj_ref, gate_total_ref,
    chunk_ref, term_chunk_ref,
):
    tiles = normed_ref.shape[1] // LANES
    hidden = normed_ref.shape[0]
    chunk_ref[...] = back_ref[...].astype(F32)
    gate_total_ref[...] = device_rows(chunk_ref, SIDE_ROWS, 9)
    back_proj_ref[4 * hidden :, :] = gate_ref[...]
    upstreams = unpack_tiles([device_rows(chunk_ref, SIDE_ROWS, t) for t in range(9)])
    for side in range(2):
        for t in range(tiles):
            at = slice(t * LANES, (t + 1) * LANES)
            for base in (2 * side * hidden, (2 * side + 1) * hidden):
                rows = slice(base, base + hidden)
                back_proj_ref[rows, at] = (upstreams[tiles * side + t] * coef_ref[rows, at]).astype(BF16)
    term = matmul(normed_ref[...], back_proj_ref[0 : 4 * hidden, :], NT)
    for t in range(4):
        for m in range(hidden // 8):
            term_chunk_ref[weight_rows(m, t), :] = term[8 * m : 8 * m + 8, t * LANES : (t + 1) * LANES]
    term_ref[...] = term_chunk_ref[...].astype(BF16)


def weight_rows(chip, t):
    return pl.ds(2 * (16 * chip + 8 * (t // 2)) + t % 2, 8, stride=2)


def sum_kernel(full_len, parts_ref, out_ref):
    total = jnp.zeros((16, LANES), F32)
    for m in range(parts_ref.shape[0] // 16):
        total += parts_ref[16 * m : 16 * m + 16, :].astype(F32)
    total = total[0:8] + total[8:16]
    total = total + pltpu.roll(total, 4, 0)
    total = total + pltpu.roll(total, 2, 0)
    total = total / full_len
    total = jnp.concatenate([total, total], axis=0).astype(BF16)
    for m in range(out_ref.shape[0] // 16):
        out_ref[16 * m : 16 * m + 16, :] = total


def grad_weight_kernel(sums_ref, gate_total_ref, out_ref, chunk_ref):
    chunk_ref[...] = sums_ref[...].astype(F32)
    for t in range(4):
        for m in range(out_ref.shape[0] // 8):
            out_ref[8 * m : 8 * m + 8, t * LANES : (t + 1) * LANES] = chunk_ref[weight_rows(m, t), :]
    out_ref[:, 4 * LANES :] = gate_total_ref[...]


def pair_kernel(acts_ref, gain_ref, weight_ref, back_proj_ref, grad_pair_ref, spread_ref):
    na, nb, _ = acts_ref.shape
    spread(acts_ref, spread_ref)
    gain = column(gain_ref)
    back_normed = matmul(weight_ref[...], back_proj_ref[...])
    for t in range(na // 2):
        at = slice(t * LANES, (t + 1) * LANES)
        scaled, inv = tile_norm(spread_ref[at, :].T.astype(F32))
        store_pairs(grad_pair_ref, t, tile_norm_grad(back_normed[:, at] * gain, scaled, inv))


def local_call(body, outs, scratch, flops, inputs, space=pltpu.VMEM, limit=VMEM_LIMIT):
    return pl.pallas_call(
        body,
        out_shape=outs,
        in_specs=[pl.BlockSpec(memory_space=space)] * inputs,
        out_specs=jax.tree.map(lambda _: pl.BlockSpec(memory_space=pltpu.VMEM), outs),
        scratch_shapes=scratch,
        compiler_params=pltpu.CompilerParams(vmem_limit_bytes=limit),
        cost_estimate=pl.CostEstimate(flops=flops, bytes_accessed=2_000_000, transcendentals=0),
    )


def exchange(chunks, depth, axes):
    devices = chunks.shape[0] // depth
    split = chunks.reshape(devices, depth // 2, 2, chunks.shape[1])
    return lax.all_to_all(split, axes, 0, 0, tiled=True).reshape(chunks.shape)


def other_core(values):
    return lax.ppermute(values, "core", [(0, 1), (1, 0)])


def array(shape, dtype=BF16):
    return jax.ShapeDtypeStruct(shape, dtype)


def per_device(pair_acts, token_valid, norm_gain, proj_weight, out_gain, out_weight, out_cotangent):
    na, _, channels = pair_acts.shape
    hidden = out_weight.shape[0]
    width_all = proj_weight.shape[1]
    full_len = token_valid.shape[0]
    lanes = na // 2 * LANES
    plane = (full_len, 8 * SLOT)
    sides_chunk = (hidden * SIDE_ROWS, LANES)
    tri_chunk = (hidden * TRI_ROWS, LANES)
    term_chunk = (4 * hidden, LANES)
    gain = norm_gain.reshape(1, channels)
    out_gain = out_gain.reshape(1, hidden)
    spread_scratch = pltpu.VMEM((lanes, channels), BF16)

    sides, mask = local_call(
        sides_kernel,
        (array(sides_chunk), array((1, lanes), F32)),
        [
            pltpu.SMEM(token_valid.shape, jnp.int32),
            pltpu.VMEM(pair_acts.shape, BF16),
            pltpu.VMEM(gain.shape, F32),
            pltpu.VMEM(proj_weight.shape, BF16),
            spread_scratch,
            pltpu.VMEM((channels, lanes), BF16),
            pltpu.VMEM(sides_chunk, F32),
            pltpu.SemaphoreType.DMA((4,)),
        ],
        100_000_000,
        4,
        pltpu.HBM,
        WHOLE_VMEM,
    )(token_valid, pair_acts, gain, proj_weight)
    mine = exchange(sides, SIDE_ROWS, CHANNEL_AXES)
    order = local_call(functools.partial(order_kernel, na), array(plane), [], 1_000_000_000, 0)()
    normed, back_norm, gate_mask, gate_coef, coef = local_call(
        ready_kernel,
        (
            array((channels, lanes)),
            array((hidden, lanes + 2 * LANES), F32),
            array((channels, lanes), F32),
            array((channels, lanes), F32),
            array((4 * hidden, lanes), F32),
        ),
        [
            pltpu.VMEM(pair_acts.shape, BF16),
            pltpu.VMEM(gain.shape, F32),
            pltpu.VMEM(proj_weight.shape, BF16),
            pltpu.VMEM(out_cotangent.shape, BF16),
            pltpu.VMEM(mask.shape, F32),
            pltpu.VMEM(out_weight.shape, BF16),
            pltpu.VMEM(out_gain.shape, F32),
            spread_scratch,
            pltpu.VMEM((channels, lanes), BF16),
            pltpu.SemaphoreType.DMA((7,)),
        ],
        1_000_000_000,
        7,
        pltpu.HBM,
        READY_VMEM,
    )(pair_acts, gain, proj_weight, out_cotangent, mask, out_weight, out_gain)
    mine, normed, order = lax.optimization_barrier((mine, normed, order))
    half_plane = (full_len // 2, plane[1])
    theirs = other_core(mine)
    left_mine, right_mine, tri_mine = local_call(
        functools.partial(own_sides_kernel, na),
        (array(half_plane), array(half_plane), array(half_plane, F32)),
        [pltpu.VMEM(sides_chunk, F32)],
        1_000_000_000,
        2,
    )(mine, order)
    tri, right = local_call(
        functools.partial(tri_kernel, na),
        (array(tri_chunk), array(plane)),
        [pltpu.VMEM(sides_chunk, F32), pltpu.VMEM(tri_chunk, F32)],
        300_000_000,
        5,
    )(theirs, left_mine, right_mine, tri_mine, order)
    tri = exchange(tri, TRI_ROWS, CHANNEL_AXES)
    back, gate, out_proj = local_call(
        middle_kernel,
        (array(tri_chunk), array((channels, lanes)), array((channels, lanes), F32)),
        [
            pltpu.VMEM(tri_chunk, F32),
            pltpu.VMEM((hidden, lanes), F32),
            pltpu.VMEM((hidden, lanes), BF16),
        ],
        100_000_000,
        4,
    )(tri, normed, back_norm, gate_coef)
    back = exchange(back, TRI_ROWS, CHANNEL_AXES)
    side_theirs, back = lax.optimization_barrier((theirs, back))
    update = local_call(update_kernel, array(pair_acts.shape), [], 1_000_000_000, 2)(
        gate_mask, out_proj
    )
    theirs = other_core(back)
    left_theirs = local_call(
        functools.partial(left_kernel, na),
        array(half_plane),
        [pltpu.VMEM(sides_chunk, F32)],
        1_000_000_000,
        1,
    )(side_theirs)
    back_left, back_right, total = local_call(
        functools.partial(own_back_kernel, na),
        (array(half_plane, F32), array(half_plane, F32), array((8, LANES), F32)),
        [
            pltpu.VMEM(tri_chunk, F32),
            pltpu.VMEM(half_plane, BF16),
            pltpu.VMEM((full_len // 2, full_len), BF16),
        ],
        1_000_000_000,
        4,
    )(back, left_mine, right, order)
    back_sides = local_call(
        functools.partial(back_kernel, na),
        array(sides_chunk),
        [
            pltpu.VMEM(tri_chunk, F32),
            pltpu.VMEM(sides_chunk, F32),
            pltpu.VMEM(half_plane, BF16),
            pltpu.VMEM((full_len // 2, full_len // 2), BF16),
        ],
        300_000_000,
        6,
    )(theirs, back_left, back_right, total, left_theirs, order)
    back_sides = exchange(back_sides, SIDE_ROWS, CHANNEL_AXES)
    term, back_proj, gate_total = local_call(
        weight_kernel,
        (array(term_chunk), array((width_all, lanes)), array((channels, channels), F32)),
        [pltpu.VMEM(sides_chunk, F32), pltpu.VMEM(term_chunk, F32)],
        200_000_000,
        4,
    )(back_sides, normed, coef, gate)
    grad_pair = local_call(
        pair_kernel, array(pair_acts.shape), [spread_scratch], 1_000_000_000, 4
    )(pair_acts, gain, proj_weight, back_proj)
    parts = exchange(term, 2, ALL_AXES)
    parts, grad_pair, update = lax.optimization_barrier((parts, grad_pair, update))
    sums = local_call(functools.partial(sum_kernel, full_len), array(term_chunk), [], 100_000, 1)(parts)
    sums = exchange(sums, 2, ALL_AXES)
    grad_weight = local_call(
        grad_weight_kernel,
        array((channels, width_all), F32),
        [pltpu.VMEM(term_chunk, F32)],
        100_000,
        2,
    )(sums, gate_total)
    return update, grad_pair, grad_weight


def solution(mesh):
    rows, cols = mesh.devices.shape
    split = Mesh(mesh.devices.reshape(rows // 2, 2, cols), ("chip", "core", "col"))
    pairs = P(("chip", "core"), "col", None)
    return jax.shard_map(
        per_device,
        mesh=split,
        in_specs=(pairs, P(), P(), P(), P(), P(), pairs),
        out_specs=(pairs, pairs, P()),
        check_vma=False,
    )
```

```python
import functools

import jax
import jax.numpy as jnp
from jax import lax
from jax.experimental import pallas as pl
from jax.experimental.pallas import tpu as pltpu
from jax.sharding import Mesh
from jax.sharding import PartitionSpec as P

EPSILON = 1e-05
BF16 = jnp.bfloat16
F32 = jnp.float32
ALL_AXES = ("chip", "core", "col")
CHANNEL_AXES = ("col", "chip")
LANES = 128
SLOT = 64
PIECE = 16
SIDE_ROWS = 10
TRI_ROWS = 6
VMEM_LIMIT = 48 * 1024 * 1024
WHOLE_VMEM = 64 * 1024 * 1024 - 65536
READY_VMEM = 62 * 1024 * 1024

NT = (((1,), (1,)), ((), ()))
NN = (((1,), (0,)), ((), ()))
TN = (((0,), (0,)), ((), ()))


def matmul(lhs, rhs, dims=NN):
    return lax.dot_general(lhs, rhs, dims, preferred_element_type=F32)


def column(row_ref):
    return jnp.broadcast_to(row_ref[...], (LANES, LANES)).T


def swap_halves(values):
    return pltpu.roll(values, SLOT, 1)


def low_half(shape):
    return lax.broadcasted_iota(jnp.int32, shape, 1) < SLOT


def spread(pairs_ref, spread_ref):
    na, nb, channels = pairs_ref.shape
    for a in range(na):
        spread_ref[a * SLOT : a * SLOT + nb, :] = pairs_ref[a]
        spread_ref[a * SLOT + nb : (a + 1) * SLOT, :] = jnp.zeros((SLOT - nb, channels), BF16)


def store_pairs(out_ref, t, values):
    nb = out_ref.shape[1]
    turned = values.T
    out_ref[2 * t] = turned[0:nb].astype(out_ref.dtype)
    out_ref[2 * t + 1] = turned[SLOT : SLOT + nb].astype(out_ref.dtype)


def masks(valid_ref, na, nb):
    lane = lax.broadcasted_iota(jnp.int32, (1, LANES), 1)
    place = lane % SLOT
    first_row = (2 * lax.axis_index("chip") + lax.axis_index("core")) * na
    first_col = lax.axis_index("col") * nb
    cols = jnp.zeros((1, LANES), jnp.int32)
    for b in range(nb):
        cols = jnp.where(place == b, valid_ref[first_col + b], cols)
    found = []
    for t in range(na // 2):
        rows = jnp.where(lane < SLOT, valid_ref[first_row + 2 * t], valid_ref[first_row + 2 * t + 1])
        found.append((rows * cols).astype(F32))
    return found


def tile_norm(values):
    center = jnp.mean(values, axis=0, keepdims=True)
    shifted = values - center
    inv_std = lax.rsqrt(jnp.mean(shifted * shifted, axis=0, keepdims=True) + EPSILON)
    return shifted * inv_std, inv_std


def tile_norm_grad(upstream, scaled, inv_std):
    first = jnp.mean(upstream, axis=0, keepdims=True)
    second = jnp.mean(upstream * scaled, axis=0, keepdims=True)
    return inv_std * (upstream - first - scaled * second)


def norm_tiles(spread_ref, gain_ref, normed_ref):
    gain = column(gain_ref)
    tiles = spread_ref.shape[0] // LANES
    for t in range(tiles):
        at = slice(t * LANES, (t + 1) * LANES)
        scaled, _ = tile_norm(spread_ref[at, :].T.astype(F32))
        normed_ref[:, at] = (scaled * gain).astype(BF16)


def gap(shape):
    return lax.broadcasted_iota(jnp.int32, shape, 1) % SLOT >= SLOT - PIECE


def pack_tiles(tiles):
    free = gap(tiles[0].shape)
    rows = []
    for t in range(9):
        moved = pltpu.roll(tiles[9 + t // 3], SLOT - PIECE - PIECE * (t % 3), 1)
        rows.append(jnp.where(free, moved, tiles[t]))
    return rows


def unpack_tiles(rows):
    free = gap(rows[0].shape)
    place = lax.broadcasted_iota(jnp.int32, rows[0].shape, 1) % SLOT // PIECE
    tiles = [jnp.where(free, 0.0, row) for row in rows]
    for m in range(3):
        tile = jnp.zeros_like(rows[0])
        for p in range(3):
            moved = pltpu.roll(rows[3 * m + p], LANES - (SLOT - PIECE) + PIECE * p, 1)
            tile = jnp.where(place == p, moved, tile)
        tiles.append(tile)
    return tiles


def device_rows(chunk_ref, depth, row):
    return chunk_ref[pl.ds(row, chunk_ref.shape[0] // depth, stride=depth), :]


def put_device_rows(chunk_ref, depth, row, values):
    chunk_ref[pl.ds(row, chunk_ref.shape[0] // depth, stride=depth), :] = values


def group_rows(depth, lo, col, row):
    return pl.ds(depth * (16 * col + lo) + row, 8, stride=2 * depth)


def plane_rows(na, lo, t):
    return slice(8 * (na * lo + 2 * t), 8 * (na * lo + 2 * t) + 16)


def plane_tile(even, odd):
    low = low_half(even.shape)
    upper = jnp.where(low, even, swap_halves(odd))
    lower = jnp.where(low, swap_halves(even), odd)
    return jnp.concatenate([upper, lower], axis=0)


def chunk_tiles(rows):
    upper, lower = rows[0:8], rows[8:16]
    low = low_half(upper.shape)
    return jnp.where(low, upper, swap_halves(lower)), jnp.where(low, swap_halves(upper), lower)


def token_order(na, plane):
    row = lax.broadcasted_iota(jnp.int32, (16 * 2 * na, plane), 0)
    token = lax.broadcasted_iota(jnp.int32, (16 * 2 * na, plane), 1)
    place = row // 8
    theirs = (place >= 2 * na).astype(jnp.int32)
    place = place - 2 * na * theirs
    core = lax.axis_index("core")
    core = core + theirs * (1 - 2 * core)
    lo = (place >= na).astype(jnp.int32)
    a = place - na * lo
    return (token == SLOT * (row % 8) + na * (2 * lo + core) + a).astype(F32).astype(BF16)


def sides_kernel(
    valid_hbm, acts_hbm, gain_hbm, weight_hbm, out_ref, mask_ref,
    valid_ref, acts_ref, gain_ref, weight_ref, spread_ref, normed_ref, chunk_ref, sems,
):
    na, nb, _ = acts_hbm.shape
    tiles = na // 2
    hidden = weight_hbm.shape[0]
    copies = [
        pltpu.make_async_copy(valid_hbm, valid_ref, sems.at[0]),
        pltpu.make_async_copy(acts_hbm, acts_ref, sems.at[1]),
        pltpu.make_async_copy(gain_hbm, gain_ref, sems.at[2]),
        pltpu.make_async_copy(weight_hbm, weight_ref, sems.at[3]),
    ]
    for copy in copies:
        copy.start()
    copies[0].wait()
    mask = masks(valid_ref, na, nb)
    for t in range(tiles):
        mask_ref[:, t * LANES : (t + 1) * LANES] = mask[t]
    copies[1].wait()
    spread(acts_ref, spread_ref)
    copies[2].wait()
    norm_tiles(spread_ref, gain_ref, normed_ref)
    copies[3].wait()
    projected = matmul(weight_ref[:, 0 : 4 * hidden], normed_ref[...], TN)
    found = []
    for side in range(2):
        base = 2 * side * hidden
        for t in range(tiles):
            at = slice(t * LANES, (t + 1) * LANES)
            gate = jax.nn.sigmoid(projected[base : base + hidden, at])
            value = projected[base + hidden : base + 2 * hidden, at]
            found.append(gate * value * mask[t])
    for t, row in enumerate(pack_tiles(found)):
        put_device_rows(chunk_ref, SIDE_ROWS, t, row)
    put_device_rows(chunk_ref, SIDE_ROWS, 9, jnp.zeros((hidden, LANES), F32))
    out_ref[...] = chunk_ref[...].astype(BF16)


def ready_kernel(
    acts_hbm, gain_hbm, weight_hbm, cotangent_hbm, mask_hbm, out_weight_hbm, out_gain_hbm,
    normed_ref, back_norm_ref, gate_mask_ref, gate_coef_ref, coef_ref,
    acts_ref, gain_ref, weight_ref, cotangent_ref, mask_ref, out_weight_ref, out_gain_ref,
    spread_ref, back_out_ref, sems,
):
    na = acts_ref.shape[0]
    tiles = na // 2
    hidden = out_weight_ref.shape[0]
    copies = [
        pltpu.make_async_copy(acts_hbm, acts_ref, sems.at[0]),
        pltpu.make_async_copy(gain_hbm, gain_ref, sems.at[1]),
        pltpu.make_async_copy(weight_hbm, weight_ref, sems.at[2]),
        pltpu.make_async_copy(cotangent_hbm, cotangent_ref, sems.at[3]),
        pltpu.make_async_copy(mask_hbm, mask_ref, sems.at[4]),
        pltpu.make_async_copy(out_weight_hbm, out_weight_ref, sems.at[5]),
        pltpu.make_async_copy(out_gain_hbm, out_gain_ref, sems.at[6]),
    ]
    for copy in copies:
        copy.start()
    for copy in copies:
        copy.wait()
    spread(acts_ref, spread_ref)
    norm_tiles(spread_ref, gain_ref, normed_ref)
    spread(cotangent_ref, spread_ref)
    projected = matmul(weight_ref[...], normed_ref[...], TN)
    for t in range(tiles):
        at = slice(t * LANES, (t + 1) * LANES)
        mask = mask_ref[:, at]
        gate = jax.nn.sigmoid(projected[4 * hidden :, at])
        gate_mask = gate * mask
        cotangent = spread_ref[at, :].T.astype(F32)
        gate_mask_ref[:, at] = gate_mask
        gate_coef_ref[:, at] = cotangent * gate_mask * (1.0 - gate)
        back_out_ref[:, at] = (cotangent * gate_mask).astype(BF16)
        for base in (0, 2 * hidden):
            gate = jax.nn.sigmoid(projected[base : base + hidden, at])
            value = projected[base + hidden : base + 2 * hidden, at]
            coef_ref[base : base + hidden, at] = value * gate * (1.0 - gate) * mask
            coef_ref[base + hidden : base + 2 * hidden, at] = gate * mask
    out_gain = column(out_gain_ref)
    back_norm = matmul(out_weight_ref[...], back_out_ref[...])
    for t in range(tiles):
        at = slice(t * LANES, (t + 1) * LANES)
        back_norm_ref[:, at] = back_norm[:, at] * out_gain
    back_norm_ref[:, tiles * LANES : (tiles + 1) * LANES] = out_gain
    back_norm_ref[:, (tiles + 1) * LANES :] = out_weight_ref[...].astype(F32)


def order_kernel(na, order_ref):
    order_ref[...] = token_order(na, order_ref.shape[1])


def side_rows(chunk_ref, lo, pair):
    return [
        unpack_tiles([chunk_ref[group_rows(SIDE_ROWS, lo, col, t), :] for t in range(9)])
        for col in (2 * pair, 2 * pair + 1)
    ]


def side_plane(na, chunk_ref, sides):
    tiles = na // 2
    for pair in range(4):
        at = slice(pair * LANES, (pair + 1) * LANES)
        for lo in range(2):
            even, odd = side_rows(chunk_ref, lo, pair)
            for side, plane_ref in sides.items():
                for t in range(tiles):
                    tile = plane_tile(even[side * tiles + t], odd[side * tiles + t])
                    plane_ref[plane_rows(na, lo, t), at] = tile.astype(BF16)


def token_sums(left_ref, right_ref, order_ref, rows):
    tri = matmul(left_ref[...], right_ref[...], NT).astype(BF16)
    return matmul(tri, order_ref[rows, :])


def own_sides_kernel(na, mine_ref, order_ref, left_ref, right_ref, tri_ref, chunk_ref):
    chunk_ref[...] = mine_ref[...].astype(F32)
    side_plane(na, chunk_ref, {0: left_ref, 1: right_ref})
    tri_ref[...] = token_sums(left_ref, right_ref, order_ref, slice(0, left_ref.shape[0]))


def left_kernel(na, theirs_ref, left_ref, chunk_ref):
    chunk_ref[...] = theirs_ref[...].astype(F32)
    side_plane(na, chunk_ref, {0: left_ref})


def tri_kernel(
    na, theirs_ref, left_ref, right_mine_ref, tri_mine_ref, order_ref, tri_ref, right_ref,
    chunk_ref, tri_chunk_ref,
):
    tiles = na // 2
    half = left_ref.shape[0]
    chunk_ref[...] = theirs_ref[...].astype(F32)
    right_ref[0:half, :] = right_mine_ref[...]
    theirs = right_ref.at[half : 2 * half]
    side_plane(na, chunk_ref, {1: theirs})
    tri = tri_mine_ref[...] + token_sums(left_ref, theirs, order_ref, slice(half, 2 * half))
    for pair in range(4):
        for lo in range(2):
            for t in range(tiles):
                both = chunk_tiles(tri[plane_rows(na, lo, t), pair * LANES : (pair + 1) * LANES])
                for side in range(2):
                    tri_chunk_ref[group_rows(TRI_ROWS, lo, 2 * pair + side, t), :] = both[side]
    tri_ref[...] = tri_chunk_ref[...].astype(BF16)


def middle_kernel(
    tri_ref, normed_ref, back_norm_ref, gate_coef_ref,
    back_ref, gate_ref, out_proj_ref,
    tri_chunk_ref, scaled_ref, normed_out_ref,
):
    tiles = normed_ref.shape[1] // LANES
    tri_chunk_ref[...] = tri_ref[...].astype(F32)
    out_gain = back_norm_ref[:, tiles * LANES : (tiles + 1) * LANES]
    out_weight = back_norm_ref[:, (tiles + 1) * LANES :].astype(BF16)
    inv_out = []
    for t in range(tiles):
        at = slice(t * LANES, (t + 1) * LANES)
        scaled, inv = tile_norm(device_rows(tri_chunk_ref, TRI_ROWS, t))
        inv_out.append(inv)
        scaled_ref[:, at] = scaled
        normed_out_ref[:, at] = (scaled * out_gain).astype(BF16)
    out_proj = matmul(out_weight, normed_out_ref[...], TN)
    out_proj_ref[...] = out_proj
    gate_ref[...] = (out_proj * gate_coef_ref[...]).astype(BF16)
    term = matmul(normed_ref[...], gate_ref[...], NT)
    free = gap(term.shape)
    for t in range(tiles):
        at = slice(t * LANES, (t + 1) * LANES)
        row = tile_norm_grad(back_norm_ref[:, at], scaled_ref[:, at], inv_out[t])
        if t < 4:
            moved = pltpu.roll(term, SLOT - PIECE - PIECE * t, 1) if t < 3 else term
            row = jnp.where(free, moved, row)
        put_device_rows(tri_chunk_ref, TRI_ROWS, t, row)
    back_ref[...] = tri_chunk_ref[...].astype(BF16)


def update_kernel(gate_mask_ref, out_proj_ref, update_ref):
    for t in range(update_ref.shape[0] // 2):
        at = slice(t * LANES, (t + 1) * LANES)
        store_pairs(update_ref, t, gate_mask_ref[:, at] * out_proj_ref[:, at])


def back_plane(na, chunk_ref, plane_ref):
    free = gap((8, LANES))
    for pair in range(4):
        for lo in range(2):
            for t in range(na // 2):
                even, odd = [
                    jnp.where(free, 0.0, chunk_ref[group_rows(TRI_ROWS, lo, col, t), :])
                    for col in (2 * pair, 2 * pair + 1)
                ]
                plane_ref[plane_rows(na, lo, t), pair * LANES : (pair + 1) * LANES] = plane_tile(
                    even, odd
                ).astype(BF16)


def gap_total(chunk_ref):
    place = lax.broadcasted_iota(jnp.int32, (8, LANES), 1) % SLOT // PIECE
    total = jnp.zeros((8, LANES), F32)
    for t in range(4):
        rows = jnp.zeros((8, LANES), F32)
        for m in range(chunk_ref.shape[0] // (8 * TRI_ROWS)):
            rows += chunk_ref[pl.ds(8 * TRI_ROWS * m + t, 8, stride=TRI_ROWS), :]
        rows = jnp.broadcast_to(jnp.sum(rows, axis=0, keepdims=True), (8, LANES))
        if t < 3:
            rows = pltpu.roll(rows, LANES - (SLOT - PIECE) + PIECE * t, 1)
        total = jnp.where(place == t, rows, total)
    return total


def tile_rows(na, pair, lo, t, side):
    start = 8 * (((2 * pair + lo) * (na // 2) + t) * 2 + side)
    return slice(start, start + 8)


def own_back_kernel(
    na, mine_ref, left_ref, right_ref, order_ref, back_left_ref, back_right_ref, total_ref,
    chunk_ref, plane_ref, turned_ref,
):
    half = left_ref.shape[0]
    chunk_ref[...] = mine_ref[...].astype(F32)
    back_plane(na, chunk_ref, plane_ref)
    turned_ref[...] = matmul(plane_ref[...], order_ref[...], NT).astype(BF16)
    back_left = matmul(turned_ref[...], right_ref[...])
    for pair in range(4):
        for lo in range(2):
            for t in range(na // 2):
                rows = back_left[plane_rows(na, lo, t), pair * LANES : (pair + 1) * LANES]
                for side, tile in enumerate(chunk_tiles(rows)):
                    back_left_ref[tile_rows(na, pair, lo, t, side), :] = tile
    back_right_ref[...] = matmul(turned_ref[:, 0:half], left_ref[...], TN)
    total_ref[...] = gap_total(chunk_ref)


def back_kernel(
    na, theirs_ref, back_left_ref, back_right_ref, total_ref, left_ref, order_ref, out_ref,
    back_chunk_ref, chunk_ref, plane_ref, turned_ref,
):
    tiles = na // 2
    half = left_ref.shape[0]
    back_chunk_ref[...] = theirs_ref[...].astype(F32)
    back_plane(na, back_chunk_ref, plane_ref)
    turned_ref[...] = matmul(plane_ref[...], order_ref[0:half, :], NT).astype(BF16)
    back_right = back_right_ref[...] + matmul(turned_ref[...], left_ref[...], TN)
    total = (total_ref[...] + gap_total(back_chunk_ref)) / (4 * 8 * na)
    for m in range(chunk_ref.shape[0] // (8 * SIDE_ROWS)):
        chunk_ref[pl.ds(8 * SIDE_ROWS * m + 9, 8, stride=SIDE_ROWS), :] = total
    for pair in range(4):
        at = slice(pair * LANES, (pair + 1) * LANES)
        for lo in range(2):
            found = [
                [back_left_ref[tile_rows(na, pair, lo, t, side), :] for side in range(2)]
                for t in range(tiles)
            ]
            found += [chunk_tiles(back_right[plane_rows(na, lo, t), at]) for t in range(tiles)]
            for side in range(2):
                for t, row in enumerate(pack_tiles([both[side] for both in found])):
                    chunk_ref[group_rows(SIDE_ROWS, lo, 2 * pair + side, t), :] = row
    out_ref[...] = chunk_ref[...].astype(BF16)


def weight_kernel(
    back_ref, normed_ref, coef_ref, gate_ref, term_ref, back_proj_ref, gate_total_ref,
    chunk_ref, term_chunk_ref,
):
    tiles = normed_ref.shape[1] // LANES
    hidden = normed_ref.shape[0]
    chunk_ref[...] = back_ref[...].astype(F32)
    gate_total_ref[...] = device_rows(chunk_ref, SIDE_ROWS, 9)
    back_proj_ref[4 * hidden :, :] = gate_ref[...]
    upstreams = unpack_tiles([device_rows(chunk_ref, SIDE_ROWS, t) for t in range(9)])
    for side in range(2):
        for t in range(tiles):
            at = slice(t * LANES, (t + 1) * LANES)
            for base in (2 * side * hidden, (2 * side + 1) * hidden):
                rows = slice(base, base + hidden)
                back_proj_ref[rows, at] = (upstreams[tiles * side + t] * coef_ref[rows, at]).astype(BF16)
    term = matmul(normed_ref[...], back_proj_ref[0 : 4 * hidden, :], NT)
    for t in range(4):
        for m in range(hidden // 8):
            term_chunk_ref[weight_rows(m, t), :] = term[8 * m : 8 * m + 8, t * LANES : (t + 1) * LANES]
    term_ref[...] = term_chunk_ref[...].astype(BF16)


def weight_rows(chip, t):
    return pl.ds(2 * (16 * chip + 8 * (t // 2)) + t % 2, 8, stride=2)


def sum_kernel(full_len, parts_ref, out_ref):
    total = jnp.zeros((16, LANES), F32)
    for m in range(parts_ref.shape[0] // 16):
        total += parts_ref[16 * m : 16 * m + 16, :].astype(F32)
    total = total[0:8] + total[8:16]
    total = total + pltpu.roll(total, 4, 0)
    total = total + pltpu.roll(total, 2, 0)
    total = total / full_len
    total = jnp.concatenate([total, total], axis=0).astype(BF16)
    for m in range(out_ref.shape[0] // 16):
        out_ref[16 * m : 16 * m + 16, :] = total


def grad_weight_kernel(sums_ref, gate_total_ref, out_ref, chunk_ref):
    chunk_ref[...] = sums_ref[...].astype(F32)
    for t in range(4):
        for m in range(out_ref.shape[0] // 8):
            out_ref[8 * m : 8 * m + 8, t * LANES : (t + 1) * LANES] = chunk_ref[weight_rows(m, t), :]
    out_ref[:, 4 * LANES :] = gate_total_ref[...]


def pair_kernel(acts_ref, gain_ref, weight_ref, back_proj_ref, grad_pair_ref, spread_ref):
    na, nb, _ = acts_ref.shape
    spread(acts_ref, spread_ref)
    gain = column(gain_ref)
    back_normed = matmul(weight_ref[...], back_proj_ref[...])
    for t in range(na // 2):
        at = slice(t * LANES, (t + 1) * LANES)
        scaled, inv = tile_norm(spread_ref[at, :].T.astype(F32))
        store_pairs(grad_pair_ref, t, tile_norm_grad(back_normed[:, at] * gain, scaled, inv))


def local_call(body, outs, scratch, flops, inputs, space=pltpu.VMEM, limit=VMEM_LIMIT):
    return pl.pallas_call(
        body,
        out_shape=outs,
        in_specs=[pl.BlockSpec(memory_space=space)] * inputs,
        out_specs=jax.tree.map(lambda _: pl.BlockSpec(memory_space=pltpu.VMEM), outs),
        scratch_shapes=scratch,
        compiler_params=pltpu.CompilerParams(vmem_limit_bytes=limit),
        cost_estimate=pl.CostEstimate(flops=flops, bytes_accessed=2_000_000, transcendentals=0),
    )


def exchange(chunks, depth, axes):
    devices = chunks.shape[0] // depth
    split = chunks.reshape(devices, depth // 2, 2, chunks.shape[1])
    return lax.all_to_all(split, axes, 0, 0, tiled=True).reshape(chunks.shape)


def other_core(values):
    return lax.ppermute(values, "core", [(0, 1), (1, 0)])


def array(shape, dtype=BF16):
    return jax.ShapeDtypeStruct(shape, dtype)


def per_device(pair_acts, token_valid, norm_gain, proj_weight, out_gain, out_weight, out_cotangent):
    na, _, channels = pair_acts.shape
    hidden = out_weight.shape[0]
    width_all = proj_weight.shape[1]
    full_len = token_valid.shape[0]
    lanes = na // 2 * LANES
    plane = (full_len, 8 * SLOT)
    sides_chunk = (hidden * SIDE_ROWS, LANES)
    tri_chunk = (hidden * TRI_ROWS, LANES)
    term_chunk = (4 * hidden, LANES)
    gain = norm_gain.reshape(1, channels)
    out_gain = out_gain.reshape(1, hidden)
    spread_scratch = pltpu.VMEM((lanes, channels), BF16)

    sides, mask = local_call(
        sides_kernel,
        (array(sides_chunk), array((1, lanes), F32)),
        [
            pltpu.SMEM(token_valid.shape, jnp.int32),
            pltpu.VMEM(pair_acts.shape, BF16),
            pltpu.VMEM(gain.shape, F32),
            pltpu.VMEM(proj_weight.shape, BF16),
            spread_scratch,
            pltpu.VMEM((channels, lanes), BF16),
            pltpu.VMEM(sides_chunk, F32),
            pltpu.SemaphoreType.DMA((4,)),
        ],
        100_000_000,
        4,
        pltpu.HBM,
        WHOLE_VMEM,
    )(token_valid, pair_acts, gain, proj_weight)
    mine = exchange(sides, SIDE_ROWS, CHANNEL_AXES)
    order = local_call(functools.partial(order_kernel, na), array(plane), [], 1_000_000_000, 0)()
    normed, back_norm, gate_mask, gate_coef, coef = local_call(
        ready_kernel,
        (
            array((channels, lanes)),
            array((hidden, lanes + 2 * LANES), F32),
            array((channels, lanes), F32),
            array((channels, lanes), F32),
            array((4 * hidden, lanes), F32),
        ),
        [
            pltpu.VMEM(pair_acts.shape, BF16),
            pltpu.VMEM(gain.shape, F32),
            pltpu.VMEM(proj_weight.shape, BF16),
            pltpu.VMEM(out_cotangent.shape, BF16),
            pltpu.VMEM(mask.shape, F32),
            pltpu.VMEM(out_weight.shape, BF16),
            pltpu.VMEM(out_gain.shape, F32),
            spread_scratch,
            pltpu.VMEM((channels, lanes), BF16),
            pltpu.SemaphoreType.DMA((7,)),
        ],
        1_000_000_000,
        7,
        pltpu.HBM,
        READY_VMEM,
    )(pair_acts, gain, proj_weight, out_cotangent, mask, out_weight, out_gain)
    mine, normed, order = lax.optimization_barrier((mine, normed, order))
    half_plane = (full_len // 2, plane[1])
    theirs = other_core(mine)
    left_mine, right_mine, tri_mine = local_call(
        functools.partial(own_sides_kernel, na),
        (array(half_plane), array(half_plane), array(half_plane, F32)),
        [pltpu.VMEM(sides_chunk, F32)],
        1_000_000_000,
        2,
    )(mine, order)
    tri, right = local_call(
        functools.partial(tri_kernel, na),
        (array(tri_chunk), array(plane)),
        [pltpu.VMEM(sides_chunk, F32), pltpu.VMEM(tri_chunk, F32)],
        300_000_000,
        5,
    )(theirs, left_mine, right_mine, tri_mine, order)
    tri = exchange(tri, TRI_ROWS, CHANNEL_AXES)
    back, gate, out_proj = local_call(
        middle_kernel,
        (array(tri_chunk), array((channels, lanes)), array((channels, lanes), F32)),
        [
            pltpu.VMEM(tri_chunk, F32),
            pltpu.VMEM((hidden, lanes), F32),
            pltpu.VMEM((hidden, lanes), BF16),
        ],
        100_000_000,
        4,
    )(tri, normed, back_norm, gate_coef)
    back = exchange(back, TRI_ROWS, CHANNEL_AXES)
    side_theirs, back = lax.optimization_barrier((theirs, back))
    update = local_call(update_kernel, array(pair_acts.shape), [], 1_000_000_000, 2)(
        gate_mask, out_proj
    )
    theirs = other_core(back)
    left_theirs = local_call(
        functools.partial(left_kernel, na),
        array(half_plane),
        [pltpu.VMEM(sides_chunk, F32)],
        1_000_000_000,
        1,
    )(side_theirs)
    back_left, back_right, total = local_call(
        functools.partial(own_back_kernel, na),
        (array(tri_chunk, F32), array(half_plane, F32), array((8, LANES), F32)),
        [
            pltpu.VMEM(tri_chunk, F32),
            pltpu.VMEM(half_plane, BF16),
            pltpu.VMEM((full_len // 2, full_len), BF16),
        ],
        1_000_000_000,
        4,
    )(back, left_mine, right, order)
    back_sides = local_call(
        functools.partial(back_kernel, na),
        array(sides_chunk),
        [
            pltpu.VMEM(tri_chunk, F32),
            pltpu.VMEM(sides_chunk, F32),
            pltpu.VMEM(half_plane, BF16),
            pltpu.VMEM((full_len // 2, full_len // 2), BF16),
        ],
        300_000_000,
        6,
    )(theirs, back_left, back_right, total, left_theirs, order)
    back_sides = exchange(back_sides, SIDE_ROWS, CHANNEL_AXES)
    term, back_proj, gate_total = local_call(
        weight_kernel,
        (array(term_chunk), array((width_all, lanes)), array((channels, channels), F32)),
        [pltpu.VMEM(sides_chunk, F32), pltpu.VMEM(term_chunk, F32)],
        200_000_000,
        4,
    )(back_sides, normed, coef, gate)
    grad_pair = local_call(
        pair_kernel, array(pair_acts.shape), [spread_scratch], 1_000_000_000, 4
    )(pair_acts, gain, proj_weight, back_proj)
    parts = exchange(term, 2, ALL_AXES)
    sums = local_call(functools.partial(sum_kernel, full_len), array(term_chunk), [], 100_000, 1)(parts)
    sums = exchange(sums, 2, ALL_AXES)
    grad_weight = local_call(
        grad_weight_kernel,
        array((channels, width_all), F32),
        [pltpu.VMEM(term_chunk, F32)],
        100_000,
        2,
    )(sums, gate_total)
    return update, grad_pair, grad_weight


def solution(mesh):
    rows, cols = mesh.devices.shape
    split = Mesh(mesh.devices.reshape(rows // 2, 2, cols), ("chip", "core", "col"))
    pairs = P(("chip", "core"), "col", None)
    return jax.shard_map(
        per_device,
        mesh=split,
        in_specs=(pairs, P(), P(), P(), P(), P(), pairs),
        out_specs=(pairs, pairs, P()),
        check_vma=False,
    )
```
